32 devices in a mesh: group: 4 (over z), local: 8 (over y, x, core).
Axes of the slice: x: 2, y: 2, z: 4, core: 2. Of those that a mesh axis runs over, the one named last changes fastest.
Arguments:
- features: bfloat16 [65536, 512], P(('group', 'local')), may hold values from -6 to 6
- weight: bfloat16 [512, 512], replicated, may hold values from -0.25 to 0.25
- cotangent: bfloat16 [65536, 512], P(('group', 'local')), may hold values from -6 to 6
- tile_vals: bfloat16 [8192, 128, 128], P(('group', 'local')), may hold values from -0.125 to 0.125
- tile_rows: int32 [8192], P(('group', 'local')), may hold values from 0 to 15
- tile_cols: int32 [8192], P(('group', 'local')), may hold values from 0 to 23
- send_rows: int32 [32, 32, 32], P(('group', 'local')), may hold values from 0 to 2047, as said below
- counts: int32 [32, 32], P(('group', 'local')), may hold values from 1 to 32, as said below
Outputs:
- activated: bfloat16 [65536, 512], P(('group', 'local'))
- feature_grad: bfloat16 [65536, 512], P(('group', 'local'))
- weight_grad: float32 [512, 512], replicated
The draws below stay inside these ranges and needn't reach their ends.
Inputs may be any that keep to these rules, and one draw needn't show every extreme that they name: Each list send_rows[s, d] holds 32 distinct local row numbers of device s. `counts`: some destinations are busy: every source sends them 32 rows; at least one such destination exists.
All inputs are finite; a program needn't handle non-finite values.
Results may differ from the reference program's by a relative error of at most 0.006.
Values may be sent and summed in bfloat16 or wider, within the bound.
No kernel may reach another device: no remote copies, remote signals or barrier semaphores. Data moves between devices by JAX's collectives and lax.ppermute only.
A program may use at most 192 MiB of HBM per device.

```python
import jax
import jax.numpy as jnp
from jax import lax

WIDTH = 512
TILE = 128
ROWS_DEV = 2048
TILES_DEV = 256
SLOTS = 32
ROW_BLOCKS = 16
COL_BLOCKS = 24
NODES = 65536
ALL_TILES = 8192
DEVICES = 32


def draw_send_rows(key, part):
    key = jax.random.fold_in(key, 11)
    scores = jax.random.randint(key, (DEVICES, DEVICES, ROWS_DEV), 0, 2 ** 19)
    distinct = scores * ROWS_DEV + jnp.arange(ROWS_DEV, dtype=jnp.int32)
    chosen_values, chosen = lax.top_k(distinct, SLOTS)
    return (chosen_values % ROWS_DEV).astype(jnp.int32)


def draw_counts(key, part):
    key = jax.random.fold_in(key, 23)
    key_busy, key_pick, key_count = jax.random.split(key, 3)
    busy = jax.random.randint(key_busy, (DEVICES,), 0, 8) == 0
    forced = jax.random.randint(key_pick, (), 0, DEVICES)
    busy = busy | (jnp.arange(DEVICES) == forced)
    quiet = jax.random.randint(key_count, (DEVICES, DEVICES), 1, SLOTS // 2 + 1)
    return jnp.where(busy[None, :], SLOTS, quiet).astype(jnp.int32)


def set_ends(values, stream_key, low, largest):
    longest = values.shape.index(max(values.shape))
    spots = []
    for shift in (0, 1):
        where = [jax.random.randint(jax.random.fold_in(stream_key, axis), (), 0, length) for axis, length in enumerate(values.shape)]
        where[longest] = (where[longest] + shift) % values.shape[longest]
        spots.append(tuple(where))
    return values.at[spots[0]].set(low).at[spots[1]].set(largest)


def block_levels(rng, dims, pieces, low, high):
    loudness, own = 1.0, jax.random.fold_in(rng, 6)
    for dim, blocks in pieces:
        steps = jnp.exp(jax.random.uniform(jax.random.fold_in(own, dim), (blocks,), jnp.float32, low / len(pieces), high / len(pieces)))
        loudness = loudness * jnp.repeat(steps, dims[dim] // blocks).reshape([-1 if axis == dim else 1 for axis in range(len(dims))])
    return loudness


def centred(stream_key, dims, scale, most, cuts=(), kind=jnp.bfloat16):
    loudness = block_levels(stream_key, dims, cuts, -0.22, 0.18) if cuts else 1.0
    array = jax.random.normal(stream_key, dims, jnp.float32) * scale * loudness
    return jnp.minimum(jnp.maximum(array, -most), most).astype(kind)


def setup_inputs(seed: int = 0) -> dict:
    arg_keys = jax.random.split(jax.random.key(seed), 9)
    features = centred(arg_keys[0], (NODES, WIDTH), 1.0, 6.0, ((0, 32),))
    weight = centred(arg_keys[1], (WIDTH, WIDTH), WIDTH ** -0.5, 0.25)
    cotangent = centred(arg_keys[2], (NODES, WIDTH), 1.0, 6.0, ((0, 32),))
    tile_vals = centred(arg_keys[3], (ALL_TILES, TILE, TILE), (TILES_DEV * TILE // ROW_BLOCKS) ** -0.5, 0.125, ((0, 32),))
    tile_rows = set_ends(jax.random.randint(arg_keys[4], (ALL_TILES,), 0, ROW_BLOCKS), jax.random.fold_in(arg_keys[4], 1), 0, ROW_BLOCKS - 1).astype(jnp.int32)
    tile_cols = set_ends(jax.random.randint(arg_keys[5], (ALL_TILES,), 0, COL_BLOCKS), jax.random.fold_in(arg_keys[5], 1), 0, COL_BLOCKS - 1).astype(jnp.int32)
    send_rows = draw_send_rows(jax.random.fold_in(arg_keys[8], 71), 0)
    counts = draw_counts(jax.random.fold_in(arg_keys[8], 71), 0)
    return dict(features=features, weight=weight, cotangent=cotangent, tile_vals=tile_vals, tile_rows=tile_rows, tile_cols=tile_cols, send_rows=send_rows, counts=counts)


def tiles_of(tile_vals, tile_rows, tile_cols, device):
    start = device * TILES_DEV
    values = lax.dynamic_slice_in_dim(tile_vals, start, TILES_DEV, 0)
    rows_of = lax.dynamic_slice_in_dim(tile_rows, start, TILES_DEV, 0)
    cols_of = lax.dynamic_slice_in_dim(tile_cols, start, TILES_DEV, 0)
    return values, rows_of, cols_of


def reference(features, weight, cotangent, tile_vals, tile_rows, tile_cols, send_rows, counts):
    slot_ids = jnp.arange(SLOTS).astype(jnp.int32)
    sources = jnp.arange(DEVICES).astype(jnp.int32)

    def remote_index(device):
        indices = sources[:, None] * ROWS_DEV + send_rows[:, device, :]
        live_slots = slot_ids[None, :] < counts[:, device][:, None]
        return indices, live_slots

    def forward(device):
        owned = lax.dynamic_slice_in_dim(features, device * ROWS_DEV, ROWS_DEV, 0)
        indices, live_slots = remote_index(device)
        remote = jnp.where(live_slots[..., None], features[indices], jnp.zeros((), features.dtype))
        extended = jnp.concatenate([owned, remote.reshape(-1, WIDTH)], axis=0).reshape(COL_BLOCKS, TILE, WIDTH)
        values, rows_of, cols_of = tiles_of(tile_vals, tile_rows, tile_cols, device)
        product = jnp.einsum('tij,tjf->tif', values.astype(jnp.float32), extended[cols_of].astype(jnp.float32),
                             precision=lax.Precision.HIGHEST)
        summed = jax.ops.segment_sum(product, rows_of, num_segments=ROW_BLOCKS)
        return summed.reshape(ROWS_DEV, WIDTH).astype(jnp.bfloat16)

    hidden = lax.map(forward, sources).reshape(NODES, WIDTH)
    preact = jnp.dot(hidden, weight, preferred_element_type=jnp.float32)
    gate = jax.nn.sigmoid(preact)
    activated = (preact * gate).astype(jnp.bfloat16)
    slope = (cotangent.astype(jnp.float32) * gate * (1.0 + preact * (1.0 - gate))).astype(jnp.bfloat16)
    weight_grad = jnp.dot(hidden.T, slope, preferred_element_type=jnp.float32)
    hidden_grad = jnp.dot(slope, weight.T, preferred_element_type=jnp.float32).astype(jnp.bfloat16)

    def backward(total, device):
        values, rows_of, cols_of = tiles_of(tile_vals, tile_rows, tile_cols, device)
        block_grad = lax.dynamic_slice_in_dim(hidden_grad, device * ROWS_DEV, ROWS_DEV, 0).reshape(ROW_BLOCKS, TILE, WIDTH)
        product = jnp.einsum('tji,tjf->tif', values.astype(jnp.float32), block_grad[rows_of].astype(jnp.float32),
                             precision=lax.Precision.HIGHEST)
        spread = jax.ops.segment_sum(product, cols_of, num_segments=COL_BLOCKS).reshape(-1, WIDTH)
        owned = spread[:ROWS_DEV]
        indices, live_slots = remote_index(device)
        returned = jnp.where(live_slots[..., None], spread[ROWS_DEV:].reshape(DEVICES, SLOTS, WIDTH), jnp.float32(0.0))
        current = lax.dynamic_slice_in_dim(total, device * ROWS_DEV, ROWS_DEV, 0)
        total = lax.dynamic_update_slice_in_dim(total, current + owned, device * ROWS_DEV, 0)
        total = total.at[indices.reshape(-1)].add(returned.reshape(-1, WIDTH))
        return total, None

    total, unused = lax.scan(backward, jnp.zeros((NODES, WIDTH), jnp.float32), sources)
    return activated, total.astype(jnp.bfloat16), weight_grad
```

```python
import functools

import jax
import jax.numpy as jnp
from jax import lax
from jax.experimental import pallas as pl
from jax.experimental.pallas import tpu as pltpu
from jax.sharding import PartitionSpec as P

AXES = ("group", "local")
BF16 = jnp.bfloat16
F32 = jnp.float32
ROWS = 256
LIMIT = 56 * 1024 * 1024


def params():
    return pltpu.CompilerParams(vmem_limit_bytes=LIMIT)


def dot(a, b, contract=((1,), (0,))):
    return lax.dot_general(a, b, (contract, ((), ())), preferred_element_type=F32)


def whole(shape):
    return pl.BlockSpec(shape, lambda i, *unused: (0,) * len(shape))


def collect_kernel(index_ref, x_ref, out_ref):
    slots, width = index_ref.shape[0], x_ref.shape[0]
    dests = out_ref.shape[0] // slots
    step = ROWS // slots
    lane = lax.broadcasted_iota(jnp.int32, (slots, width), 1)
    for first in range(0, dests, step):
        parts = []
        for d in range(first, first + step):
            hit = index_ref[:, d : d + 1] == lane
            parts.append(jnp.where(hit, 1.0, 0.0).astype(BF16))
        pick = jnp.concatenate(parts, axis=0)
        out_ref[first * slots : (first + step) * slots, :] = dot(pick, x_ref[...]).astype(BF16)


def collect(index, x):
    slots, dests = index.shape
    return pl.pallas_call(
        collect_kernel,
        out_shape=jax.ShapeDtypeStruct((dests * slots, x.shape[1]), BF16),
        compiler_params=params(),
        name="collect",
    )(index, x)


def build_kernel(rows_ref, cols_ref, tiles_ref, x_ref, adj_ref, own_ref, total, order, starts, cursor):
    num_tiles, edge = tiles_ref.shape[0], tiles_ref.shape[1]
    per = ROWS // edge
    blocks = pl.num_programs(0)
    i = pl.program_id(0)

    @pl.when(i == 0)
    def _():
        def clear(b, unused):
            starts[b] = 0
            return unused

        lax.fori_loop(0, blocks + 1, clear, 0)

        def count(t, unused):
            k = rows_ref[t] // per + 1
            starts[k] = starts[k] + 1
            return unused

        lax.fori_loop(0, num_tiles, count, 0, unroll=4)

        def add(b, running):
            running = running + starts[b]
            starts[b] = running
            cursor[b] = running
            return running

        lax.fori_loop(0, blocks + 1, add, 0)

        def place(t, unused):
            k = rows_ref[t] // per
            at = cursor[k]
            cursor[k] = at + 1
            order[at] = t
            return unused

        lax.fori_loop(0, num_tiles, place, 0, unroll=4)

    total[...] = jnp.zeros_like(total)

    def one(j, unused):
        t = order[j]
        r = pl.multiple_of((rows_ref[t] % per) * edge, edge)
        c = pl.multiple_of(cols_ref[t] * edge, edge)
        at = (pl.ds(r, edge), pl.ds(c, edge))
        total[at] = total[at] + tiles_ref[t].astype(F32)
        return unused

    lax.fori_loop(starts[i], starts[i + 1], one, 0)
    adj_ref[...] = total[...].astype(BF16)
    owned = x_ref.shape[0]
    own_ref[...] = dot(adj_ref[:, :owned], x_ref[...])


def build(tile_rows, tile_cols, tile_vals, x, extended):
    owned, width = x.shape
    num_tiles = tile_vals.shape[0]
    blocks = owned // ROWS
    return pl.pallas_call(
        build_kernel,
        grid_spec=pltpu.PrefetchScalarGridSpec(
            num_scalar_prefetch=2,
            grid=(blocks,),
            in_specs=[whole(tile_vals.shape), whole(x.shape)],
            out_specs=[
                pl.BlockSpec((ROWS, extended), lambda i, *unused: (i, 0)),
                pl.BlockSpec((ROWS, width), lambda i, *unused: (i, 0)),
            ],
            scratch_shapes=[
                pltpu.VMEM((ROWS, extended), F32),
                pltpu.SMEM((num_tiles,), jnp.int32),
                pltpu.SMEM((blocks + 1,), jnp.int32),
                pltpu.SMEM((blocks + 1,), jnp.int32),
            ],
        ),
        out_shape=[
            jax.ShapeDtypeStruct((owned, extended), BF16),
            jax.ShapeDtypeStruct((owned, width), F32),
        ],
        compiler_params=params(),
        cost_estimate=pl.CostEstimate(
            flops=2 * owned * owned * width, bytes_accessed=40 * 1024 * 1024, transcendentals=0
        ),
        name="build",
    )(tile_rows, tile_cols, tile_vals, x)


def layer_kernel(adj_ref, own_ref, far_ref, cot_ref, w_ref, act_ref, hid_ref, slope_ref, grad_ref, back_ref, total):
    i = pl.program_id(0)
    hidden = (own_ref[...] + dot(adj_ref[...], far_ref[...])).astype(BF16)
    hid_ref[...] = hidden
    w = w_ref[...]
    preact = dot(hidden, w)
    gate = 0.5 + 0.5 * jnp.tanh(0.5 * preact)
    act_ref[...] = (preact * gate).astype(BF16)
    slope = (cot_ref[...].astype(F32) * gate * (1.0 + preact * (1.0 - gate))).astype(BF16)
    slope_ref[...] = slope
    grad = dot(w, slope, ((1,), (1,))).astype(BF16)
    grad_ref[...] = grad
    part = dot(grad, adj_ref[...])

    @pl.when(i == 0)
    def _():
        total[...] = part

    @pl.when(i > 0)
    def _():
        total[...] += part

    @pl.when(i == pl.num_programs(0) - 1)
    def _():
        back_ref[...] = total[...].astype(BF16).T


def layer(adjacency, own, far, cotangent, weight):
    owned, width = own.shape
    remote = far.shape[0]
    assert owned % remote == 0 or remote % owned == 0
    rows = pl.BlockSpec((ROWS, width), lambda i: (i, 0))
    rows_type = jax.ShapeDtypeStruct((owned, width), BF16)
    return pl.pallas_call(
        layer_kernel,
        grid=(owned // ROWS,),
        in_specs=[
            pl.BlockSpec((pl.Element(ROWS), pl.Element(remote)), lambda i: (i * ROWS, owned)),
            rows,
            whole(far.shape),
            rows,
            whole(weight.shape),
        ],
        out_specs=[
            rows,
            rows,
            rows,
            pl.BlockSpec((width, ROWS), lambda i: (0, i)),
            whole(far.shape),
        ],
        out_shape=[
            rows_type,
            rows_type,
            rows_type,
            jax.ShapeDtypeStruct((width, owned), BF16),
            jax.ShapeDtypeStruct(far.shape, BF16),
        ],
        scratch_shapes=[pltpu.VMEM((width, remote), F32)],
        compiler_params=params(),
        name="layer",
    )(adjacency, own, far, cotangent, weight)


def spread_kernel(adj_ref, grad_ref, out_ref):
    out_ref[...] = dot(grad_ref[...], adj_ref[...]).T


def spread(adjacency, grad):
    width, owned = grad.shape
    return pl.pallas_call(
        spread_kernel,
        grid=(owned // ROWS,),
        in_specs=[pl.BlockSpec((owned, ROWS), lambda i: (0, i)), whole(grad.shape)],
        out_specs=pl.BlockSpec((ROWS, width), lambda i: (i, 0)),
        out_shape=jax.ShapeDtypeStruct((owned, width), F32),
        compiler_params=params(),
        cost_estimate=pl.CostEstimate(
            flops=2 * owned * owned * width, bytes_accessed=16 * 1024 * 1024, transcendentals=0
        ),
        name="spread",
    )(adjacency, grad)


def return_kernel(index_ref, owned_ref, back_ref, out_ref):
    base = pl.program_id(0) * ROWS
    row = lax.broadcasted_iota(jnp.int32, (ROWS, index_ref.shape[1]), 0) + base
    pick = jnp.where(row == index_ref[...], 1.0, 0.0).astype(BF16)
    out_ref[...] = (owned_ref[...] + dot(pick, back_ref[...])).astype(BF16)


def give_back(index, owned, back):
    rows, width = owned.shape
    block = pl.BlockSpec((ROWS, width), lambda i: (i, 0))
    return pl.pallas_call(
        return_kernel,
        grid=(rows // ROWS,),
        in_specs=[whole(index.shape), block, whole(back.shape)],
        out_specs=block,
        out_shape=jax.ShapeDtypeStruct((rows, width), BF16),
        compiler_params=params(),
        name="give_back",
    )(index, owned, back)


def exchange(x, axes):
    return lax.all_to_all(x, axes, split_axis=0, concat_axis=0, tiled=True)


def reduce_everywhere(partial, groups, locals_):
    height, width = partial.shape
    pieces = exchange(partial.astype(BF16).reshape(locals_, height // locals_, width), "local")
    piece = jnp.sum(pieces.astype(F32), axis=0).astype(BF16)
    pieces = exchange(jnp.broadcast_to(piece[None], (groups,) + piece.shape), "group")
    piece = jnp.sum(pieces.astype(F32), axis=0).astype(BF16)
    pieces = exchange(jnp.broadcast_to(piece[None], (locals_,) + piece.shape), "local")
    return pieces.reshape(height, width).astype(F32)


def per_device(groups, locals_, features, weight, cotangent, tile_vals, tile_rows, tile_cols, send_rows, counts):
    rows_own, width = features.shape
    lists = send_rows[0]
    peers, slots = lists.shape
    live = jnp.arange(slots)[None, :] < counts[0][:, None]
    index = jnp.where(live, lists, -1)
    outgoing = collect(index.T, features)
    arrived = exchange(outgoing.reshape(peers, slots, width), AXES).reshape(peers * slots, width)
    adjacency, own = build(tile_rows, tile_cols, tile_vals, features, rows_own + peers * slots)
    activated, hidden, slope, grad, back = layer(adjacency, own, arrived, cotangent, weight)
    returned = exchange(back.reshape(peers, slots, width), AXES).reshape(peers * slots, width)
    partial = dot(hidden, slope, ((0,), (0,)))
    weight_grad = reduce_everywhere(partial, groups, locals_)
    owned = spread(adjacency, grad)
    feature_grad = give_back(index.reshape(1, peers * slots), owned, returned)
    return activated, feature_grad, weight_grad


def solution(mesh):
    return jax.shard_map(
        functools.partial(per_device, mesh.shape["group"], mesh.shape["local"]),
        mesh=mesh,
        in_specs=(
            P(AXES, None),
            P(),
            P(AXES, None),
            P(AXES, None, None),
            P(AXES),
            P(AXES),
            P(AXES, None, None),
            P(AXES, None),
        ),
        out_specs=(P(AXES, None), P(AXES, None), P()),
        check_vma=False,
    )
```

```python
import functools

import jax
import jax.numpy as jnp
from jax import lax
from jax.experimental import pallas as pl
from jax.experimental.pallas import tpu as pltpu
from jax.sharding import PartitionSpec as P

AXES = ("group", "local")
BF16 = jnp.bfloat16
F32 = jnp.float32
ROWS = 256
BIG = 512
MIB = 1024 * 1024


def params(mib):
    return pltpu.CompilerParams(vmem_limit_bytes=mib * MIB)


VMEM = pl.BlockSpec(memory_space=pltpu.VMEM)
SMEM = pl.BlockSpec(memory_space=pltpu.SMEM)
HBM = pl.BlockSpec(memory_space=pl.ANY)


def made(keep, shape, dtype):
    return pltpu.VMEM(shape, dtype) if keep else jax.ShapeDtypeStruct(shape, dtype)


def held(keep, *arrays):
    if not keep:
        return arrays
    return [pltpu.with_memory_space_constraint(x, pltpu.VMEM) for x in arrays]


def dot(a, b, contract=((1,), (0,))):
    return lax.dot_general(a, b, (contract, ((), ())), preferred_element_type=F32)


def whole(shape):
    return pl.BlockSpec(shape, lambda i, *unused: (0,) * len(shape))


def collect_kernel(counts_ref, lists_ref, x_ref, out_ref):
    dests, slots = lists_ref.shape
    step = BIG // slots
    lane = lax.broadcasted_iota(jnp.int32, (slots, x_ref.shape[0]), 1)
    slot = lax.broadcasted_iota(jnp.int32, (slots, 1), 0)
    turned = lists_ref[...].T
    for first in range(0, dests, step):
        parts = []
        for d in range(first, first + step):
            named = jnp.where(slot < counts_ref[0, d], turned[:, d : d + 1], -1)
            parts.append(jnp.where(named == lane, 1.0, 0.0).astype(BF16))
        pick = jnp.concatenate(parts, axis=0)
        out_ref[first * slots : (first + step) * slots, :] = dot(pick, x_ref[...]).astype(BF16)


def collect(counts, lists, x):
    dests, slots = lists.shape
    return pl.pallas_call(
        collect_kernel,
        in_specs=[SMEM, VMEM, VMEM],
        out_shape=jax.ShapeDtypeStruct((dests * slots, x.shape[1]), BF16),
        compiler_params=params(60),
        name="collect",
    )(counts, lists, x)


def build_kernel(rows_ref, cols_ref, tiles_ref, x_ref, adj_ref, far_ref, own_ref, total, order, starts, cursor):
    num_tiles, edge = tiles_ref.shape[0], tiles_ref.shape[1]
    per = ROWS // edge
    blocks = pl.num_programs(0)
    i = pl.program_id(0)

    @pl.when(i == 0)
    def _():
        def clear(b, unused):
            starts[b] = 0
            return unused

        lax.fori_loop(0, blocks + 1, clear, 0)

        def count(t, unused):
            k = rows_ref[t] // per + 1
            starts[k] = starts[k] + 1
            return unused

        lax.fori_loop(0, num_tiles, count, 0, unroll=4)

        def add(b, running):
            running = running + starts[b]
            starts[b] = running
            cursor[b] = running
            return running

        lax.fori_loop(0, blocks + 1, add, 0)

        def place(t, unused):
            k = rows_ref[t] // per
            at = cursor[k]
            cursor[k] = at + 1
            order[at] = t
            return unused

        lax.fori_loop(0, num_tiles, place, 0, unroll=4)

    total[...] = jnp.zeros_like(total)

    def one(j, unused):
        t = order[j]
        r = pl.multiple_of((rows_ref[t] % per) * edge, edge)
        c = pl.multiple_of(cols_ref[t] * edge, edge)
        at = (pl.ds(r, edge), pl.ds(c, edge))
        total[at] = total[at] + tiles_ref[t].astype(F32)
        return unused

    lax.fori_loop(starts[i], starts[i + 1], one, 0)
    owned = x_ref.shape[0]
    adj_ref[...] = total[:, :owned].astype(BF16)
    own_ref[...] = dot(adj_ref[...], x_ref[...])
    far_ref[...] = total[:, owned:].astype(BF16)


def build(tile_rows, tile_cols, tile_vals, x, remote):
    owned, width = x.shape
    num_tiles = tile_vals.shape[0]
    blocks = owned // ROWS
    return pl.pallas_call(
        build_kernel,
        grid_spec=pltpu.PrefetchScalarGridSpec(
            num_scalar_prefetch=2,
            grid=(blocks,),
            in_specs=[whole(tile_vals.shape), whole(x.shape)],
            out_specs=[
                pl.BlockSpec((ROWS, owned), lambda i, *unused: (i, 0)),
                pl.BlockSpec((ROWS, remote), lambda i, *unused: (i, 0)),
                pl.BlockSpec((ROWS, width), lambda i, *unused: (i, 0)),
            ],
            scratch_shapes=[
                pltpu.VMEM((ROWS, owned + remote), F32),
                pltpu.SMEM((num_tiles,), jnp.int32),
                pltpu.SMEM((blocks + 1,), jnp.int32),
                pltpu.SMEM((blocks + 1,), jnp.int32),
            ],
        ),
        out_shape=[
            jax.ShapeDtypeStruct((owned, owned), BF16),
            jax.ShapeDtypeStruct((owned, remote), BF16),
            jax.ShapeDtypeStruct((owned, width), F32),
        ],
        compiler_params=params(48),
        cost_estimate=pl.CostEstimate(
            flops=2 * owned * owned * width, bytes_accessed=40 * 1024 * 1024, transcendentals=0
        ),
        name="build",
    )(tile_rows, tile_cols, tile_vals, x)


def layer_kernel(
    me_ref, far_hbm, own_hbm, cot_hbm, w_ref, got_ref,
    act_hbm, far_ref, slope_ref, mine_ref, other_ref,
    own, cot, hid, act, sems, sent,
):
    blocks = sems.shape[1]
    views = [pl.ds(n * BIG, BIG) for n in range(blocks)]

    def fetch(n):
        pairs = ((far_hbm, far_ref), (own_hbm, own), (cot_hbm, cot))
        copies = [pltpu.make_async_copy(a.at[views[n]], b.at[views[n]], sems.at[k, n]) for k, (a, b) in enumerate(pairs)]
        for copy in copies:
            copy.start()
        return copies

    coming = fetch(0)
    sending = []
    for n, at in enumerate(views):
        copies = coming
        for copy in copies[:2]:
            copy.wait()
        if n + 1 < blocks:
            coming = fetch(n + 1)
        hidden = (own[at, :] + dot(far_ref[at, :], got_ref[...])).astype(BF16)
        hid[at, :] = hidden
        preact = dot(hidden, w_ref[...])
        copies[2].wait()
        gate = 0.5 + 0.5 * jnp.tanh(0.5 * preact)
        act[at, :] = (preact * gate).astype(BF16)
        sending.append(pltpu.make_async_copy(act.at[at], act_hbm.at[at], sent.at[n]))
        sending[n].start()
        slope = cot[at, :].astype(F32) * gate * (1.0 + preact * (1.0 - gate))
        slope_ref[at, :] = slope.astype(BF16)
    half = mine_ref.shape[0]
    core = me_ref[0] % 2
    for out_ref, first in ((other_ref, (1 - core) * half), (mine_ref, core * half)):
        columns = hid[:, pl.ds(pl.multiple_of(first, half), half)]
        out_ref[...] = dot(columns, slope_ref[...], ((0,), (0,))).astype(out_ref.dtype)
    for copy in sending:
        copy.wait()


def layer(keep, me, far, own, got, cotangent, weight):
    owned, width = own.shape
    half = (width // 2, width)
    blocks = owned // BIG
    weight, got = held(keep, weight, got)
    return pl.pallas_call(
        layer_kernel,
        in_specs=[SMEM, HBM, HBM, HBM, VMEM, VMEM],
        out_specs=[HBM, VMEM, VMEM, VMEM, VMEM],
        out_shape=[
            jax.ShapeDtypeStruct((owned, width), BF16),
            made(keep, far.shape, BF16),
            made(keep, (owned, width), BF16),
            made(keep, half, F32),
            made(keep, half, BF16),
        ],
        scratch_shapes=[
            pltpu.VMEM((owned, width), F32),
            pltpu.VMEM((owned, width), BF16),
            pltpu.VMEM((owned, width), BF16),
            pltpu.VMEM((owned, width), BF16),
            pltpu.SemaphoreType.DMA((3, blocks)),
            pltpu.SemaphoreType.DMA((blocks,)),
        ],
        compiler_params=params(28 if keep else 60),
        name="layer",
    )(me, far, own, cotangent, weight, got)


def grad_kernel(slope_ref, w_ref, grad_ref, grad_hbm, sems):
    copies = []
    for n in range(sems.shape[0]):
        at = pl.ds(n * BIG, BIG)
        grad_ref[at, :] = dot(slope_ref[at, :], w_ref[...], ((1,), (1,))).astype(BF16)
        copies.append(pltpu.make_async_copy(grad_ref.at[at], grad_hbm.at[at], sems.at[n]))
        copies[n].start()
    for copy in copies:
        copy.wait()


def hidden_grad(keep, slope, weight):
    return pl.pallas_call(
        grad_kernel,
        in_specs=[VMEM] * 2,
        out_specs=[VMEM, HBM],
        out_shape=[made(keep, slope.shape, BF16), jax.ShapeDtypeStruct(slope.shape, BF16)],
        scratch_shapes=[pltpu.SemaphoreType.DMA((slope.shape[0] // BIG,))],
        compiler_params=params(12 if keep else 40),
        name="hidden_grad",
    )(*held(keep, slope, weight))


def back_kernel(far_ref, grad_ref, after_ref, out_hbm, out, sems):
    copies = []
    for n in range(sems.shape[0]):
        at = pl.ds(n * BIG, BIG)
        out[at, :] = dot(far_ref[:, at], grad_ref[...], ((0,), (0,))).astype(BF16)
        copies.append(pltpu.make_async_copy(out.at[at], out_hbm.at[at], sems.at[n]))
        copies[n].start()
    for copy in copies:
        copy.wait()


def back_rows(keep, far, grad, after):
    shape = (far.shape[1], grad.shape[1])
    return pl.pallas_call(
        back_kernel,
        in_specs=[VMEM, VMEM, HBM],
        out_specs=HBM,
        out_shape=jax.ShapeDtypeStruct(shape, BF16),
        scratch_shapes=[pltpu.VMEM(shape, BF16), pltpu.SemaphoreType.DMA((shape[0] // BIG,))],
        compiler_params=params(16 if keep else 60),
        name="back_rows",
    )(*held(keep, far, grad), after)


def spread_kernel(adj_ref, grad_ref, out_ref):
    out_ref[...] = dot(adj_ref[...], grad_ref[...], ((0,), (0,)))


def spread(adjacency, grad):
    owned, width = grad.shape
    return pl.pallas_call(
        spread_kernel,
        grid=(owned // BIG,),
        in_specs=[pl.BlockSpec((owned, BIG), lambda i: (0, i)), whole(grad.shape)],
        out_specs=pl.BlockSpec((BIG, width), lambda i: (i, 0)),
        out_shape=jax.ShapeDtypeStruct((owned, width), F32),
        compiler_params=params(60),
        cost_estimate=pl.CostEstimate(
            flops=2 * owned * owned * width, bytes_accessed=16 * 1024 * 1024, transcendentals=0
        ),
        name="spread",
    )(adjacency, grad)


def return_kernel(index_ref, owned_hbm, got_ref, out_hbm, owned, out, sems, sent):
    blocks = sems.shape[0]
    views = [pl.ds(n * BIG, BIG) for n in range(blocks)]
    coming = [pltpu.make_async_copy(owned_hbm.at[at], owned.at[at], sems.at[n]) for n, at in enumerate(views)]
    for copy in coming:
        copy.start()

    def pick(n):
        row = lax.broadcasted_iota(jnp.int32, (BIG, index_ref.shape[1]), 0) + n * BIG
        return jnp.where(row == index_ref[...], 1.0, 0.0).astype(BF16)

    sending = []
    for n, at in enumerate(views):
        added = dot(pick(n), got_ref[...])
        coming[n].wait()
        out[at, :] = (owned[at, :] + added).astype(BF16)
        sending.append(pltpu.make_async_copy(out.at[at], out_hbm.at[at], sent.at[n]))
        sending[n].start()
    for copy in sending:
        copy.wait()


def give_back(keep, index, owned, got):
    rows, width = owned.shape
    (got,) = held(keep, got)
    return pl.pallas_call(
        return_kernel,
        in_specs=[VMEM, HBM, VMEM],
        out_specs=HBM,
        out_shape=jax.ShapeDtypeStruct((rows, width), BF16),
        scratch_shapes=[
            pltpu.VMEM((rows, width), F32),
            pltpu.VMEM((rows, width), BF16),
            pltpu.SemaphoreType.DMA((rows // BIG,)),
            pltpu.SemaphoreType.DMA((rows // BIG,)),
        ],
        compiler_params=params(28 if keep else 60),
        name="give_back",
    )(index, owned, got)


def exchange(x, axes):
    return lax.all_to_all(x, axes, split_axis=0, concat_axis=0, tiled=True)


def cut_kernel(me_ref, mine_ref, got_ref, *out_refs):
    height = mine_ref.shape[0] // len(out_refs)
    for k, out_ref in enumerate(out_refs):
        at = pl.ds(pl.multiple_of(((me_ref[0] // 2) ^ k) * height, height), height)
        out_ref[...] = (mine_ref[at, :] + got_ref[at, :].astype(F32)).astype(out_ref.dtype)


def cut(me, mine, got, chips):
    height, width = got.shape[0] // chips, got.shape[1]
    return pl.pallas_call(
        cut_kernel,
        in_specs=[SMEM, VMEM, VMEM],
        out_shape=[jax.ShapeDtypeStruct((height, width), F32 if k == 0 else BF16) for k in range(chips)],
        compiler_params=params(8),
        name="cut",
    )(me, mine, got)


def join_kernel(me_ref, *refs):
    in_refs, out_ref = refs[:-1], refs[-1]
    height, half = in_refs[0].shape[0], out_ref.shape[0] // 2
    for k, in_ref in enumerate(in_refs):
        owner = me_ref[0] ^ k
        at = pl.multiple_of((owner % 2) * half + (owner // 2) * height, height)
        out_ref[pl.ds(at, height), :] = in_ref[...].astype(F32)


def join(me, parts):
    height, width = parts[0].shape
    return pl.pallas_call(
        join_kernel,
        in_specs=[SMEM] + [VMEM] * len(parts),
        out_shape=jax.ShapeDtypeStruct((height * len(parts), width), F32),
        compiler_params=params(8),
        name="join",
    )(me, *parts)


def add_kernel(after_ref, *refs):
    parts = [ref[...].astype(F32) for ref in refs[:-1]]
    while len(parts) > 1:
        parts = [parts[k] + parts[k + 1] for k in range(0, len(parts), 2)]
    refs[-1][...] = parts[0].astype(BF16)


def add(after, parts):
    return pl.pallas_call(
        add_kernel,
        in_specs=[HBM] + [VMEM] * len(parts),
        out_shape=jax.ShapeDtypeStruct(parts[0].shape, BF16),
        compiler_params=params(8),
        name="add",
    )(after, *parts)


def swap(x, axis, size, k):
    return lax.ppermute(x, axis, [(i, i ^ k) for i in range(size)])


def per_device(groups, locals_, features, weight, cotangent, tile_vals, tile_rows, tile_cols, send_rows, counts):
    rows_own, width = features.shape
    lists = send_rows[0]
    peers, slots = lists.shape
    remote = peers * slots
    keep = remote <= rows_own
    me = lax.axis_index("local").astype(jnp.int32).reshape(1)
    outgoing = collect(counts, lists, features)
    arrived = exchange(outgoing.reshape(peers, slots, width), AXES).reshape(remote, width)
    adjacency, far, own = build(tile_rows, tile_cols, tile_vals, features, remote)
    activated, far, slope, mine, other = layer(keep, me, far, own, arrived, cotangent, weight)
    chips = locals_ // 2
    pieces = cut(me, mine, swap(other, "local", locals_, 1), chips)
    grad, grad_out = hidden_grad(keep, slope, weight)
    back = back_rows(keep, far, grad, pieces[-1])
    returned = exchange(back.reshape(peers, slots, width), AXES).reshape(remote, width)
    owned = spread(adjacency, grad_out)
    piece = add(owned, [pieces[0]] + [swap(pieces[k], "local", locals_, 2 * k) for k in range(1, chips)])
    piece = add(me, [piece] + [swap(piece, "group", groups, k) for k in range(1, groups)])
    weight_grad = join(me, [piece] + [swap(piece, "local", locals_, k) for k in range(1, locals_)])
    live = jnp.arange(slots)[None, :] < counts[0][:, None]
    feature_grad = give_back(keep, jnp.where(live, lists, -1).reshape(1, remote), owned, returned)
    return activated, feature_grad, weight_grad


def solution(mesh):
    return jax.shard_map(
        functools.partial(per_device, mesh.shape["group"], mesh.shape["local"]),
        mesh=mesh,
        in_specs=(
            P(AXES, None),
            P(),
            P(AXES, None),
            P(AXES, None, None),
            P(AXES),
            P(AXES),
            P(AXES, None, None),
            P(AXES, None),
        ),
        out_specs=(P(AXES, None), P(AXES, None), P()),
        check_vma=False,
    )
```

```python
import functools

import jax
import jax.numpy as jnp
from jax import lax
from jax.experimental import pallas as pl
from jax.experimental.pallas import tpu as pltpu
from jax.sharding import PartitionSpec as P

AXES = ("group", "local")
BF16 = jnp.bfloat16
F32 = jnp.float32
ROWS = 256
BIG = 512
MIB = 1024 * 1024


def params(mib):
    return pltpu.CompilerParams(vmem_limit_bytes=mib * MIB)


VMEM = pl.BlockSpec(memory_space=pltpu.VMEM)
SMEM = pl.BlockSpec(memory_space=pltpu.SMEM)
ANY = pl.BlockSpec(memory_space=pl.ANY)
HBM = pl.BlockSpec(memory_space=pltpu.MemorySpace.HBM)


def made(keep, shape, dtype):
    return pltpu.VMEM(shape, dtype) if keep else jax.ShapeDtypeStruct(shape, dtype)


def held(keep, *arrays):
    if not keep:
        return arrays
    return [pltpu.with_memory_space_constraint(x, pltpu.VMEM) for x in arrays]


def stored(*arrays):
    return [pltpu.with_memory_space_constraint(x, pltpu.MemorySpace.HBM) for x in arrays]


def far_made(shape, dtype):
    return pltpu.MemorySpace.HBM(shape, dtype)


def dot(a, b, contract=((1,), (0,))):
    return lax.dot_general(a, b, (contract, ((), ())), preferred_element_type=F32)


def whole(shape):
    return pl.BlockSpec(shape, lambda i, *unused: (0,) * len(shape))


def collect_kernel(counts_ref, lists_ref, x_ref, out_ref):
    dests, slots = lists_ref.shape
    step = BIG // slots
    lane = lax.broadcasted_iota(jnp.int32, (slots, x_ref.shape[0]), 1)
    slot = lax.broadcasted_iota(jnp.int32, (slots, 1), 0)
    turned = lists_ref[...].T
    for first in range(0, dests, step):
        parts = []
        for d in range(first, first + step):
            named = jnp.where(slot < counts_ref[0, d], turned[:, d : d + 1], -1)
            parts.append(jnp.where(named == lane, 1.0, 0.0).astype(BF16))
        pick = jnp.concatenate(parts, axis=0)
        out_ref[first * slots : (first + step) * slots, :] = dot(pick, x_ref[...]).astype(BF16)


def collect(counts, lists, x):
    dests, slots = lists.shape
    return pl.pallas_call(
        collect_kernel,
        in_specs=[SMEM, VMEM, VMEM],
        out_shape=jax.ShapeDtypeStruct((dests * slots, x.shape[1]), BF16),
        compiler_params=params(60),
        name="collect",
    )(counts, lists, x)


def build_kernel(rows_ref, cols_ref, tiles_ref, x_ref, adj_ref, far_ref, own_ref, total, order, starts, cursor):
    num_tiles, edge = tiles_ref.shape[0], tiles_ref.shape[1]
    per = ROWS // edge
    blocks = pl.num_programs(0)
    i = pl.program_id(0)

    @pl.when(i == 0)
    def _():
        def clear(b, unused):
            starts[b] = 0
            return unused

        lax.fori_loop(0, blocks + 1, clear, 0)

        def count(t, unused):
            k = rows_ref[t] // per + 1
            starts[k] = starts[k] + 1
            return unused

        lax.fori_loop(0, num_tiles, count, 0, unroll=4)

        def add(b, running):
            running = running + starts[b]
            starts[b] = running
            cursor[b] = running
            return running

        lax.fori_loop(0, blocks + 1, add, 0)

        def place(t, unused):
            k = rows_ref[t] // per
            at = cursor[k]
            cursor[k] = at + 1
            order[at] = t
            return unused

        lax.fori_loop(0, num_tiles, place, 0, unroll=4)

    total[...] = jnp.zeros_like(total)

    def one(j, unused):
        t = order[j]
        r = pl.multiple_of((rows_ref[t] % per) * edge, edge)
        c = pl.multiple_of(cols_ref[t] * edge, edge)
        at = (pl.ds(r, edge), pl.ds(c, edge))
        total[at] = total[at] + tiles_ref[t].astype(F32)
        return unused

    lax.fori_loop(starts[i], starts[i + 1], one, 0)
    owned = x_ref.shape[0]
    adj_ref[...] = total[:, :owned].astype(BF16)
    own_ref[...] = dot(adj_ref[...], x_ref[...])
    far_ref[...] = total[:, owned:].astype(BF16)


def build(tile_rows, tile_cols, tile_vals, x, remote):
    owned, width = x.shape
    num_tiles = tile_vals.shape[0]
    blocks = owned // ROWS
    return pl.pallas_call(
        build_kernel,
        grid_spec=pltpu.PrefetchScalarGridSpec(
            num_scalar_prefetch=2,
            grid=(blocks,),
            in_specs=[whole(tile_vals.shape), whole(x.shape)],
            out_specs=[
                pl.BlockSpec((ROWS, owned), lambda i, *unused: (i, 0)),
                pl.BlockSpec((ROWS, remote), lambda i, *unused: (i, 0)),
                pl.BlockSpec((ROWS, width), lambda i, *unused: (i, 0)),
            ],
            scratch_shapes=[
                pltpu.VMEM((ROWS, owned + remote), F32),
                pltpu.SMEM((num_tiles,), jnp.int32),
                pltpu.SMEM((blocks + 1,), jnp.int32),
                pltpu.SMEM((blocks + 1,), jnp.int32),
            ],
        ),
        out_shape=[
            far_made((owned, owned), BF16),
            far_made((owned, remote), BF16),
            far_made((owned, width), F32),
        ],
        compiler_params=params(48),
        cost_estimate=pl.CostEstimate(
            flops=2 * owned * owned * width, bytes_accessed=40 * 1024 * 1024, transcendentals=0
        ),
        name="build",
    )(tile_rows, tile_cols, tile_vals, x)


def layer_kernel(
    me_ref, far_hbm, own_hbm, cot_hbm, w_ref, got_ref,
    act_hbm, far_ref, slope_ref, mine_ref, other_ref,
    own, cot, hid, act, sems, sent,
):
    blocks = sems.shape[1]
    views = [pl.ds(n * BIG, BIG) for n in range(blocks)]

    def fetch(n):
        pairs = ((far_hbm, far_ref), (own_hbm, own), (cot_hbm, cot))
        copies = [pltpu.make_async_copy(a.at[views[n]], b.at[views[n]], sems.at[k, n]) for k, (a, b) in enumerate(pairs)]
        for copy in copies:
            copy.start()
        return copies

    coming = fetch(0)
    sending = []
    for n, at in enumerate(views):
        copies = coming
        for copy in copies[:2]:
            copy.wait()
        if n + 1 < blocks:
            coming = fetch(n + 1)
        hidden = (own[at, :] + dot(far_ref[at, :], got_ref[...])).astype(BF16)
        hid[at, :] = hidden
        preact = dot(hidden, w_ref[...])
        copies[2].wait()
        gate = 0.5 + 0.5 * jnp.tanh(0.5 * preact)
        act[at, :] = (preact * gate).astype(BF16)
        sending.append(pltpu.make_async_copy(act.at[at], act_hbm.at[at], sent.at[n]))
        sending[n].start()
        slope = cot[at, :].astype(F32) * gate * (1.0 + preact * (1.0 - gate))
        slope_ref[at, :] = slope.astype(BF16)
    half = mine_ref.shape[0]
    core = me_ref[0] % 2
    for out_ref, first in ((other_ref, (1 - core) * half), (mine_ref, core * half)):
        columns = hid[:, pl.ds(pl.multiple_of(first, half), half)]
        out_ref[...] = dot(columns, slope_ref[...], ((0,), (0,))).astype(out_ref.dtype)
    for copy in sending:
        copy.wait()


def layer(keep, me, far, own, got, cotangent, weight):
    owned, width = own.shape
    half = (width // 2, width)
    blocks = owned // BIG
    weight, got = held(keep, weight, got)
    return pl.pallas_call(
        layer_kernel,
        in_specs=[SMEM, HBM, HBM, HBM, VMEM, VMEM],
        out_specs=[HBM, VMEM, VMEM, VMEM, VMEM],
        out_shape=[
            far_made((owned, width), BF16),
            made(keep, far.shape, BF16),
            made(keep, (owned, width), BF16),
            made(keep, half, F32),
            made(keep, half, BF16),
        ],
        scratch_shapes=[
            pltpu.VMEM((owned, width), F32),
            pltpu.VMEM((owned, width), BF16),
            pltpu.VMEM((owned, width), BF16),
            pltpu.VMEM((owned, width), BF16),
            pltpu.SemaphoreType.DMA((3, blocks)),
            pltpu.SemaphoreType.DMA((blocks,)),
        ],
        compiler_params=params(28 if keep else 60),
        name="layer",
    )(me, *stored(far, own, cotangent), weight, got)


def grad_kernel(slope_ref, w_ref, grad_ref, grad_hbm, sems):
    copies = []
    for n in range(sems.shape[0]):
        at = pl.ds(n * BIG, BIG)
        grad_ref[at, :] = dot(slope_ref[at, :], w_ref[...], ((1,), (1,))).astype(BF16)
        copies.append(pltpu.make_async_copy(grad_ref.at[at], grad_hbm.at[at], sems.at[n]))
        copies[n].start()
    for copy in copies:
        copy.wait()


def hidden_grad(keep, slope, weight):
    return pl.pallas_call(
        grad_kernel,
        in_specs=[VMEM] * 2,
        out_specs=[VMEM, HBM],
        out_shape=[made(keep, slope.shape, BF16), far_made(slope.shape, BF16)],
        scratch_shapes=[pltpu.SemaphoreType.DMA((slope.shape[0] // BIG,))],
        compiler_params=params(12 if keep else 40),
        name="hidden_grad",
    )(*held(keep, slope, weight))


def back_kernel(far_ref, grad_ref, after_ref, out_hbm, out, sems):
    copies = []
    for n in range(sems.shape[0]):
        at = pl.ds(n * BIG, BIG)
        out[at, :] = dot(far_ref[:, at], grad_ref[...], ((0,), (0,))).astype(BF16)
        copies.append(pltpu.make_async_copy(out.at[at], out_hbm.at[at], sems.at[n]))
        copies[n].start()
    for copy in copies:
        copy.wait()


def back_rows(keep, far, grad, after):
    shape = (far.shape[1], grad.shape[1])
    return pl.pallas_call(
        back_kernel,
        in_specs=[VMEM, VMEM, ANY],
        out_specs=HBM,
        out_shape=far_made(shape, BF16),
        scratch_shapes=[pltpu.VMEM(shape, BF16), pltpu.SemaphoreType.DMA((shape[0] // BIG,))],
        compiler_params=params(16 if keep else 60),
        name="back_rows",
    )(*held(keep, far, grad), after)


def spread_kernel(adj_ref, grad_ref, out_ref):
    out_ref[...] = dot(adj_ref[...], grad_ref[...], ((0,), (0,)))


def spread(adjacency, grad):
    owned, width = grad.shape
    return pl.pallas_call(
        spread_kernel,
        grid=(owned // BIG,),
        in_specs=[pl.BlockSpec((owned, BIG), lambda i: (0, i)), whole(grad.shape)],
        out_specs=pl.BlockSpec((BIG, width), lambda i: (i, 0)),
        out_shape=far_made((owned, width), F32),
        compiler_params=params(60),
        cost_estimate=pl.CostEstimate(
            flops=2 * owned * owned * width, bytes_accessed=16 * 1024 * 1024, transcendentals=0
        ),
        name="spread",
    )(*stored(adjacency, grad))


def return_kernel(index_ref, owned_hbm, got_ref, out_hbm, owned, out, sems, sent):
    blocks = sems.shape[0]
    views = [pl.ds(n * BIG, BIG) for n in range(blocks)]
    coming = [pltpu.make_async_copy(owned_hbm.at[at], owned.at[at], sems.at[n]) for n, at in enumerate(views)]
    for copy in coming:
        copy.start()

    def pick(n):
        row = lax.broadcasted_iota(jnp.int32, (BIG, index_ref.shape[1]), 0) + n * BIG
        return jnp.where(row == index_ref[...], 1.0, 0.0).astype(BF16)

    sending = []
    for n, at in enumerate(views):
        added = dot(pick(n), got_ref[...])
        coming[n].wait()
        out[at, :] = (owned[at, :] + added).astype(BF16)
        sending.append(pltpu.make_async_copy(out.at[at], out_hbm.at[at], sent.at[n]))
        sending[n].start()
    for copy in sending:
        copy.wait()


def give_back(keep, index, owned, got):
    rows, width = owned.shape
    (got,) = held(keep, got)
    return pl.pallas_call(
        return_kernel,
        in_specs=[VMEM, HBM, VMEM],
        out_specs=HBM,
        out_shape=far_made((rows, width), BF16),
        scratch_shapes=[
            pltpu.VMEM((rows, width), F32),
            pltpu.VMEM((rows, width), BF16),
            pltpu.SemaphoreType.DMA((rows // BIG,)),
            pltpu.SemaphoreType.DMA((rows // BIG,)),
        ],
        compiler_params=params(28 if keep else 60),
        name="give_back",
    )(index, *stored(owned), got)


def exchange(x, axes):
    return lax.all_to_all(x, axes, split_axis=0, concat_axis=0, tiled=True)


def cut_kernel(me_ref, mine_ref, got_ref, *out_refs):
    height = mine_ref.shape[0] // len(out_refs)
    for k, out_ref in enumerate(out_refs):
        at = pl.ds(pl.multiple_of(((me_ref[0] // 2) ^ k) * height, height), height)
        out_ref[...] = (mine_ref[at, :] + got_ref[at, :].astype(F32)).astype(out_ref.dtype)


def cut(me, mine, got, chips):
    height, width = got.shape[0] // chips, got.shape[1]
    return pl.pallas_call(
        cut_kernel,
        in_specs=[SMEM, VMEM, VMEM],
        out_shape=[jax.ShapeDtypeStruct((height, width), F32 if k == 0 else BF16) for k in range(chips)],
        compiler_params=params(8),
        name="cut",
    )(me, mine, got)


def join_kernel(me_ref, after_ref, *refs):
    in_refs, out_ref = refs[:-1], refs[-1]
    height, half = in_refs[0].shape[0], out_ref.shape[0] // 2
    for k, in_ref in enumerate(in_refs):
        owner = me_ref[0] ^ k
        at = pl.multiple_of((owner % 2) * half + (owner // 2) * height, height)
        out_ref[pl.ds(at, height), :] = in_ref[...].astype(F32)


def join(me, after, parts):
    height, width = parts[0].shape
    return pl.pallas_call(
        join_kernel,
        in_specs=[SMEM, ANY] + [VMEM] * len(parts),
        out_shape=jax.ShapeDtypeStruct((height * len(parts), width), F32),
        compiler_params=params(8),
        name="join",
    )(me, after, *parts)


def add_kernel(after_ref, *refs):
    parts = [ref[...].astype(F32) for ref in refs[:-1]]
    while len(parts) > 1:
        parts = [parts[k] + parts[k + 1] for k in range(0, len(parts), 2)]
    refs[-1][...] = parts[0].astype(BF16)


def add(after, parts):
    return pl.pallas_call(
        add_kernel,
        in_specs=[ANY] + [VMEM] * len(parts),
        out_shape=jax.ShapeDtypeStruct(parts[0].shape, BF16),
        compiler_params=params(8),
        name="add",
    )(after, *parts)


def swap(x, axis, size, k):
    return lax.ppermute(x, axis, [(i, i ^ k) for i in range(size)])


def per_device(groups, locals_, features, weight, cotangent, tile_vals, tile_rows, tile_cols, send_rows, counts):
    rows_own, width = features.shape
    lists = send_rows[0]
    peers, slots = lists.shape
    remote = peers * slots
    keep = remote <= rows_own
    me = lax.axis_index("local").astype(jnp.int32).reshape(1)
    outgoing = collect(counts, lists, features)
    arrived = exchange(outgoing.reshape(peers, slots, width), AXES).reshape(remote, width)
    adjacency, far, own = build(tile_rows, tile_cols, tile_vals, features, remote)
    activated, far, slope, mine, other = layer(keep, me, far, own, arrived, cotangent, weight)
    chips = locals_ // 2
    pieces = cut(me, mine, swap(other, "local", locals_, 1), chips)
    grad, grad_out = hidden_grad(keep, slope, weight)
    back = back_rows(keep, far, grad, pieces[-1])
    returned = exchange(back.reshape(peers, slots, width), AXES).reshape(remote, width)
    owned = spread(adjacency, grad_out)
    piece = add(owned, [pieces[0]] + [swap(pieces[k], "local", locals_, 2 * k) for k in range(1, chips)])
    step = 1
    while step < groups:
        piece = add(me, [piece, swap(piece, "group", groups, step)])
        step *= 2
    gathered = []
    for k in range(chips):
        mine = swap(piece, "local", locals_, 2 * k) if k else piece
        gathered += [mine, swap(mine, "local", locals_, 1)]
    live = jnp.arange(slots)[None, :] < counts[0][:, None]
    feature_grad = give_back(keep, jnp.where(live, lists, -1).reshape(1, remote), owned, returned)
    return activated, feature_grad, join(me, feature_grad, gathered)


def solution(mesh):
    return jax.shard_map(
        functools.partial(per_device, mesh.shape["group"], mesh.shape["local"]),
        mesh=mesh,
        in_specs=(
            P(AXES, None),
            P(),
            P(AXES, None),
            P(AXES, None, None),
            P(AXES),
            P(AXES),
            P(AXES, None, None),
            P(AXES, None),
        ),
        out_specs=(P(AXES, None), P(AXES, None), P()),
        check_vma=False,
    )
```

```python
import functools

import jax
import jax.numpy as jnp
from jax import lax
from jax.experimental import pallas as pl
from jax.experimental.pallas import tpu as pltpu
from jax.sharding import PartitionSpec as P

AXES = ("group", "local")
BF16 = jnp.bfloat16
F32 = jnp.float32
ROWS = 256
BIG = 512
MIB = 1024 * 1024


def params(mib):
    return pltpu.CompilerParams(vmem_limit_bytes=mib * MIB)


VMEM = pl.BlockSpec(memory_space=pltpu.VMEM)
SMEM = pl.BlockSpec(memory_space=pltpu.SMEM)
HBM = pl.BlockSpec(memory_space=pltpu.MemorySpace.HBM)


def made(keep, shape, dtype):
    return pltpu.VMEM(shape, dtype) if keep else jax.ShapeDtypeStruct(shape, dtype)


def held(keep, *arrays):
    if not keep:
        return arrays
    return [pltpu.with_memory_space_constraint(x, pltpu.VMEM) for x in arrays]


def stored(*arrays):
    return [pltpu.with_memory_space_constraint(x, pltpu.MemorySpace.HBM) for x in arrays]


def far_made(shape, dtype):
    return pltpu.MemorySpace.HBM(shape, dtype)


def dot(a, b, contract=((1,), (0,))):
    return lax.dot_general(a, b, (contract, ((), ())), preferred_element_type=F32)


def whole(shape):
    return pl.BlockSpec(shape, lambda i, *unused: (0,) * len(shape))


def collect_kernel(counts_ref, lists_ref, x_ref, out_ref):
    dests, slots = lists_ref.shape
    step = BIG // slots
    lane = lax.broadcasted_iota(jnp.int32, (slots, x_ref.shape[0]), 1)
    slot = lax.broadcasted_iota(jnp.int32, (slots, 1), 0)
    turned = lists_ref[...].T
    for first in range(0, dests, step):
        parts = []
        for d in range(first, first + step):
            named = jnp.where(slot < counts_ref[0, d], turned[:, d : d + 1], -1)
            parts.append(jnp.where(named == lane, 1.0, 0.0).astype(BF16))
        pick = jnp.concatenate(parts, axis=0)
        out_ref[first * slots : (first + step) * slots, :] = dot(pick, x_ref[...]).astype(BF16)


def collect(counts, lists, x):
    dests, slots = lists.shape
    return pl.pallas_call(
        collect_kernel,
        in_specs=[SMEM, VMEM, VMEM],
        out_shape=jax.ShapeDtypeStruct((dests * slots, x.shape[1]), BF16),
        compiler_params=params(60),
        name="collect",
    )(counts, lists, x)


def build_kernel(rows_ref, cols_ref, tiles_ref, x_ref, adj_ref, far_ref, own_ref, total, order, starts, cursor):
    num_tiles, edge = tiles_ref.shape[0], tiles_ref.shape[1]
    per = ROWS // edge
    blocks = pl.num_programs(0)
    i = pl.program_id(0)

    @pl.when(i == 0)
    def _():
        def clear(b, unused):
            starts[b] = 0
            return unused

        lax.fori_loop(0, blocks + 1, clear, 0)

        def count(t, unused):
            k = rows_ref[t] // per + 1
            starts[k] = starts[k] + 1
            return unused

        lax.fori_loop(0, num_tiles, count, 0, unroll=4)

        def add(b, running):
            running = running + starts[b]
            starts[b] = running
            cursor[b] = running
            return running

        lax.fori_loop(0, blocks + 1, add, 0)

        def place(t, unused):
            k = rows_ref[t] // per
            at = cursor[k]
            cursor[k] = at + 1
            order[at] = t
            return unused

        lax.fori_loop(0, num_tiles, place, 0, unroll=4)

    total[...] = jnp.zeros_like(total)

    def one(j, unused):
        t = order[j]
        r = pl.multiple_of((rows_ref[t] % per) * edge, edge)
        c = pl.multiple_of(cols_ref[t] * edge, edge)
        at = (pl.ds(r, edge), pl.ds(c, edge))
        total[at] = total[at] + tiles_ref[t].astype(F32)
        return unused

    lax.fori_loop(starts[i], starts[i + 1], one, 0)
    owned = x_ref.shape[0]
    adj_ref[...] = total[:, :owned].astype(BF16)
    own_ref[...] = dot(adj_ref[...], x_ref[...])
    far_ref[...] = total[:, owned:].astype(BF16)


def build(tile_rows, tile_cols, tile_vals, x, remote):
    owned, width = x.shape
    num_tiles = tile_vals.shape[0]
    blocks = owned // ROWS
    return pl.pallas_call(
        build_kernel,
        grid_spec=pltpu.PrefetchScalarGridSpec(
            num_scalar_prefetch=2,
            grid=(blocks,),
            in_specs=[whole(tile_vals.shape), whole(x.shape)],
            out_specs=[
                pl.BlockSpec((ROWS, owned), lambda i, *unused: (i, 0)),
                pl.BlockSpec((ROWS, remote), lambda i, *unused: (i, 0)),
                pl.BlockSpec((ROWS, width), lambda i, *unused: (i, 0)),
            ],
            scratch_shapes=[
                pltpu.VMEM((ROWS, owned + remote), F32),
                pltpu.SMEM((num_tiles,), jnp.int32),
                pltpu.SMEM((blocks + 1,), jnp.int32),
                pltpu.SMEM((blocks + 1,), jnp.int32),
            ],
        ),
        out_shape=[
            far_made((owned, owned), BF16),
            far_made((owned, remote), BF16),
            far_made((owned, width), F32),
        ],
        compiler_params=params(48),
        cost_estimate=pl.CostEstimate(
            flops=2 * owned * owned * width, bytes_accessed=40 * 1024 * 1024, transcendentals=0
        ),
        name="build",
    )(tile_rows, tile_cols, tile_vals, x)


def layer_kernel(
    far_hbm, own_hbm, cot_hbm, w_ref, got_ref,
    act_hbm, hid_hbm, slope_hbm, grad_hbm, back_hbm,
    far, own, cot, act, hid, slope, grad, back, sems, sent,
):
    blocks = sems.shape[1]
    views = [pl.ds(n * BIG, BIG) for n in range(blocks)]

    def fetch(n):
        pairs = ((far_hbm, far), (own_hbm, own), (cot_hbm, cot))
        copies = [pltpu.make_async_copy(a.at[views[n]], b.at[views[n]], sems.at[k, n]) for k, (a, b) in enumerate(pairs)]
        for copy in copies:
            copy.start()
        return copies

    sending = []

    def send(k, n, a, b, at):
        sending.append(pltpu.make_async_copy(a.at[at], b.at[at], sent.at[k, n]))
        sending[-1].start()

    coming = fetch(0)
    for n, at in enumerate(views):
        copies = coming
        for copy in copies[:2]:
            copy.wait()
        if n + 1 < blocks:
            coming = fetch(n + 1)
        hid[at, :] = (own[at, :] + dot(far[at, :], got_ref[...])).astype(BF16)
        send(0, n, hid, hid_hbm, at)
        preact = dot(hid[at, :], w_ref[...])
        copies[2].wait()
        gate = 0.5 + 0.5 * jnp.tanh(0.5 * preact)
        act[at, :] = (preact * gate).astype(BF16)
        send(1, n, act, act_hbm, at)
        slope[at, :] = (cot[at, :].astype(F32) * gate * (1.0 + preact * (1.0 - gate))).astype(BF16)
        send(2, n, slope, slope_hbm, at)
        grad[at, :] = dot(slope[at, :], w_ref[...], ((1,), (1,))).astype(BF16)
        send(3, n, grad, grad_hbm, at)
    for n in range(back.shape[0] // BIG):
        at = pl.ds(n * BIG, BIG)
        back[at, :] = dot(far[:, at], grad[...], ((0,), (0,))).astype(BF16)
        send(4, n, back, back_hbm, at)
    for copy in sending:
        copy.wait()


def layer(keep, far, own, got, cotangent, weight):
    owned, width = own.shape
    remote = got.shape[0]
    blocks = owned // BIG
    weight, got = held(keep, weight, got)
    rows = (owned, width)
    return pl.pallas_call(
        layer_kernel,
        in_specs=[HBM, HBM, HBM, VMEM, VMEM],
        out_specs=[HBM] * 5,
        out_shape=[far_made(rows, BF16)] * 4 + [far_made(got.shape, BF16)],
        scratch_shapes=[pltpu.VMEM(far.shape, BF16), pltpu.VMEM(rows, F32)]
        + [pltpu.VMEM(rows, BF16)] * 5
        + [
            pltpu.VMEM(got.shape, BF16),
            pltpu.SemaphoreType.DMA((3, blocks)),
            pltpu.SemaphoreType.DMA((5, max(blocks, remote // BIG))),
        ],
        compiler_params=params(40 if keep else 60),
        name="layer",
    )(*stored(far, own, cotangent), weight, got)


def partial_kernel(me_ref, hid_hbm, slope_hbm, mine_ref, other_ref, hid, slope, total, sems):
    blocks = sems.shape[1]
    views = [pl.ds(n * BIG, BIG) for n in range(blocks)]
    coming = [
        [pltpu.make_async_copy(a.at[at], b.at[at], sems.at[k, n]) for k, (a, b) in enumerate(((hid_hbm, hid), (slope_hbm, slope)))]
        for n, at in enumerate(views)
    ]
    for copies in coming:
        for copy in copies:
            copy.start()
    for n, at in enumerate(views):
        for copy in coming[n]:
            copy.wait()
        part = dot(hid[at, :], slope[at, :], ((0,), (0,)))
        total[...] = part if n == 0 else total[...] + part
    half = mine_ref.shape[0]
    core = me_ref[0] % 2
    for out_ref, first in ((other_ref, (1 - core) * half), (mine_ref, core * half)):
        out_ref[...] = total[pl.ds(pl.multiple_of(first, half), half), :].astype(out_ref.dtype)


def partial_grad(keep, me, hidden, slope):
    owned, width = hidden.shape
    half = (width // 2, width)
    return pl.pallas_call(
        partial_kernel,
        in_specs=[SMEM, HBM, HBM],
        out_specs=[VMEM, VMEM],
        out_shape=[made(keep, half, F32), made(keep, half, BF16)],
        scratch_shapes=[
            pltpu.VMEM((owned, width), BF16),
            pltpu.VMEM((owned, width), BF16),
            pltpu.VMEM((width, width), F32),
            pltpu.SemaphoreType.DMA((2, owned // BIG)),
        ],
        compiler_params=params(20),
        name="partial_grad",
    )(me, *stored(hidden, slope))


def spread_kernel(adj_ref, grad_ref, out_ref):
    out_ref[...] = dot(adj_ref[...], grad_ref[...], ((0,), (0,)))


def spread(adjacency, grad, part, parts):
    owned, width = grad.shape
    blocks = owned // BIG // parts
    return pl.pallas_call(
        spread_kernel,
        grid=(blocks,),
        in_specs=[pl.BlockSpec((owned, BIG), lambda i: (0, i + part * blocks)), whole(grad.shape)],
        out_specs=pl.BlockSpec((BIG, width), lambda i: (i, 0)),
        out_shape=far_made((owned // parts, width), F32),
        compiler_params=params(60),
        cost_estimate=pl.CostEstimate(
            flops=2 * owned * owned * width, bytes_accessed=16 * 1024 * 1024, transcendentals=0
        ),
        name="spread",
    )(*stored(adjacency, grad))


def return_kernel(index_ref, first_hbm, second_hbm, got_ref, out_hbm, owned, out, sems, sent):
    blocks = sems.shape[0]
    views = [pl.ds(n * BIG, BIG) for n in range(blocks)]
    coming = []
    for n, at in enumerate(views):
        half_hbm = (first_hbm, second_hbm)[2 * n // blocks]
        coming.append(pltpu.make_async_copy(half_hbm.at[views[n % (blocks // 2)]], owned.at[at], sems.at[n]))
    for copy in coming:
        copy.start()

    def pick(n):
        row = lax.broadcasted_iota(jnp.int32, (BIG, index_ref.shape[1]), 0) + n * BIG
        return jnp.where(row == index_ref[...], 1.0, 0.0).astype(BF16)

    sending = []
    for n, at in enumerate(views):
        added = dot(pick(n), got_ref[...])
        coming[n].wait()
        out[at, :] = (owned[at, :] + added).astype(BF16)
        sending.append(pltpu.make_async_copy(out.at[at], out_hbm.at[at], sent.at[n]))
        sending[n].start()
    for copy in sending:
        copy.wait()


def give_back(keep, index, first, second, got):
    rows, width = 2 * first.shape[0], first.shape[1]
    (got,) = held(keep, got)
    return pl.pallas_call(
        return_kernel,
        in_specs=[VMEM, HBM, HBM, VMEM],
        out_specs=HBM,
        out_shape=far_made((rows, width), BF16),
        scratch_shapes=[
            pltpu.VMEM((rows, width), F32),
            pltpu.VMEM((rows, width), BF16),
            pltpu.SemaphoreType.DMA((rows // BIG,)),
            pltpu.SemaphoreType.DMA((rows // BIG,)),
        ],
        compiler_params=params(28 if keep else 60),
        name="give_back",
    )(index, *stored(first, second), got)


def exchange(x, axes):
    return lax.all_to_all(x, axes, split_axis=0, concat_axis=0, tiled=True)


def cut_kernel(me_ref, mine_ref, got_ref, *out_refs):
    height = mine_ref.shape[0] // len(out_refs)
    for k, out_ref in enumerate(out_refs):
        at = pl.ds(pl.multiple_of(((me_ref[0] // 2) ^ k) * height, height), height)
        out_ref[...] = (mine_ref[at, :] + got_ref[at, :].astype(F32)).astype(out_ref.dtype)


def cut(me, mine, got, chips):
    height, width = got.shape[0] // chips, got.shape[1]
    return pl.pallas_call(
        cut_kernel,
        in_specs=[SMEM, VMEM, VMEM],
        out_shape=[jax.ShapeDtypeStruct((height, width), F32 if k == 0 else BF16) for k in range(chips)],
        compiler_params=params(8),
        name="cut",
    )(me, mine, got)


def join_kernel(me_ref, *refs):
    in_refs, out_ref = refs[:-1], refs[-1]
    height, half = in_refs[0].shape[0], out_ref.shape[0] // 2
    for k, in_ref in enumerate(in_refs):
        owner = me_ref[0] ^ k
        at = pl.multiple_of((owner % 2) * half + (owner // 2) * height, height)
        out_ref[pl.ds(at, height), :] = in_ref[...].astype(F32)


def join(me, parts):
    height, width = parts[0].shape
    return pl.pallas_call(
        join_kernel,
        in_specs=[SMEM] + [VMEM] * len(parts),
        out_shape=jax.ShapeDtypeStruct((height * len(parts), width), F32),
        compiler_params=params(8),
        name="join",
    )(me, *parts)


def add_kernel(after_ref, *refs):
    parts = [ref[...].astype(F32) for ref in refs[:-1]]
    while len(parts) > 1:
        parts = [parts[k] + parts[k + 1] for k in range(0, len(parts), 2)]
    refs[-1][...] = parts[0].astype(BF16)


def add(after, parts):
    return pl.pallas_call(
        add_kernel,
        in_specs=[HBM] + [VMEM] * len(parts),
        out_shape=jax.ShapeDtypeStruct(parts[0].shape, BF16),
        compiler_params=params(8),
        name="add",
    )(*stored(after), *parts)


def swap(x, axis, size, k):
    return lax.ppermute(x, axis, [(i, i ^ k) for i in range(size)])


def per_device(groups, locals_, features, weight, cotangent, tile_vals, tile_rows, tile_cols, send_rows, counts):
    rows_own, width = features.shape
    lists = send_rows[0]
    peers, slots = lists.shape
    remote = peers * slots
    keep = remote <= rows_own
    me = lax.axis_index("local").astype(jnp.int32).reshape(1)
    outgoing = collect(counts, lists, features)
    arrived = exchange(outgoing.reshape(peers, slots, width), AXES).reshape(remote, width)
    adjacency, far, own = build(tile_rows, tile_cols, tile_vals, features, remote)
    activated, hidden, slope, grad, back = layer(keep, far, own, arrived, cotangent, weight)
    returned = exchange(back.reshape(peers, slots, width), AXES).reshape(remote, width)
    first = spread(adjacency, grad, 0, 2)
    second = spread(adjacency, grad, 1, 2)
    live = jnp.arange(slots)[None, :] < counts[0][:, None]
    feature_grad = give_back(keep, jnp.where(live, lists, -1).reshape(1, remote), first, second, returned)
    chips = locals_ // 2
    mine, other = partial_grad(keep, me, hidden, slope)
    pieces = cut(me, mine, swap(other, "local", locals_, 1), chips)
    piece = add(first, [pieces[0]] + [swap(pieces[k], "local", locals_, 2 * k) for k in range(1, chips)])
    step, after = groups // 2, second
    while step:
        piece = add(after, [piece, swap(piece, "group", groups, step)])
        step, after = step // 2, feature_grad
    gathered = []
    for k in range(chips):
        mine = swap(piece, "local", locals_, 2 * k) if k else piece
        gathered += [mine, swap(mine, "local", locals_, 1)]
    return activated, feature_grad, join(me, gathered)


def solution(mesh):
    return jax.shard_map(
        functools.partial(per_device, mesh.shape["group"], mesh.shape["local"]),
        mesh=mesh,
        in_specs=(
            P(AXES, None),
            P(),
            P(AXES, None),
            P(AXES, None, None),
            P(AXES),
            P(AXES),
            P(AXES, None, None),
            P(AXES, None),
        ),
        out_specs=(P(AXES, None), P(AXES, None), P()),
        check_vma=False,
    )
```

```python
import functools

import jax
import jax.numpy as jnp
from jax import lax
from jax.experimental import pallas as pl
from jax.experimental.pallas import tpu as pltpu
from jax.sharding import PartitionSpec as P

AXES = ("group", "local")
BF16 = jnp.bfloat16
F32 = jnp.float32
ROWS = 256
BIG = 512
MIB = 1024 * 1024


def params(mib):
    return pltpu.CompilerParams(vmem_limit_bytes=mib * MIB)


VMEM = pl.BlockSpec(memory_space=pltpu.VMEM)
SMEM = pl.BlockSpec(memory_space=pltpu.SMEM)
HBM = pl.BlockSpec(memory_space=pltpu.MemorySpace.HBM)


def made(keep, shape, dtype):
    return pltpu.VMEM(shape, dtype) if keep else jax.ShapeDtypeStruct(shape, dtype)


def held(keep, *arrays):
    if not keep:
        return arrays
    return [pltpu.with_memory_space_constraint(x, pltpu.VMEM) for x in arrays]


def stored(*arrays):
    return [pltpu.with_memory_space_constraint(x, pltpu.MemorySpace.HBM) for x in arrays]


def far_made(shape, dtype):
    return pltpu.MemorySpace.HBM(shape, dtype)


def dot(a, b, contract=((1,), (0,))):
    return lax.dot_general(a, b, (contract, ((), ())), preferred_element_type=F32)


def whole(shape):
    return pl.BlockSpec(shape, lambda i, *unused: (0,) * len(shape))


def collect_kernel(counts_ref, lists_ref, x_ref, out_ref):
    dests, slots = lists_ref.shape
    step = BIG // slots
    lane = lax.broadcasted_iota(jnp.int32, (slots, x_ref.shape[0]), 1)
    slot = lax.broadcasted_iota(jnp.int32, (slots, 1), 0)
    turned = lists_ref[...].T
    for first in range(0, dests, step):
        parts = []
        for d in range(first, first + step):
            named = jnp.where(slot < counts_ref[0, d], turned[:, d : d + 1], -1)
            parts.append(jnp.where(named == lane, 1.0, 0.0).astype(BF16))
        pick = jnp.concatenate(parts, axis=0)
        out_ref[first * slots : (first + step) * slots, :] = dot(pick, x_ref[...]).astype(BF16)


def collect(counts, lists, x):
    dests, slots = lists.shape
    return pl.pallas_call(
        collect_kernel,
        in_specs=[SMEM, VMEM, VMEM],
        out_shape=jax.ShapeDtypeStruct((dests * slots, x.shape[1]), BF16),
        compiler_params=params(60),
        name="collect",
    )(counts, lists, x)


def build_kernel(rows_ref, cols_ref, tiles_ref, x_ref, adj_ref, far_ref, own_ref, total, order, starts, cursor):
    num_tiles, edge = tiles_ref.shape[0], tiles_ref.shape[1]
    per = ROWS // edge
    blocks = pl.num_programs(0)
    i = pl.program_id(0)

    @pl.when(i == 0)
    def _():
        def clear(b, unused):
            starts[b] = 0
            return unused

        lax.fori_loop(0, blocks + 1, clear, 0)

        def count(t, unused):
            k = rows_ref[t] // per + 1
            starts[k] = starts[k] + 1
            return unused

        lax.fori_loop(0, num_tiles, count, 0, unroll=4)

        def add(b, running):
            running = running + starts[b]
            starts[b] = running
            cursor[b] = running
            return running

        lax.fori_loop(0, blocks + 1, add, 0)

        def place(t, unused):
            k = rows_ref[t] // per
            at = cursor[k]
            cursor[k] = at + 1
            order[at] = t
            return unused

        lax.fori_loop(0, num_tiles, place, 0, unroll=4)

    total[...] = jnp.zeros_like(total)

    def one(j, unused):
        t = order[j]
        r = pl.multiple_of((rows_ref[t] % per) * edge, edge)
        c = pl.multiple_of(cols_ref[t] * edge, edge)
        at = (pl.ds(r, edge), pl.ds(c, edge))
        total[at] = total[at] + tiles_ref[t].astype(F32)
        return unused

    lax.fori_loop(starts[i], starts[i + 1], one, 0)
    owned = x_ref.shape[0]
    adj_ref[...] = total[:, :owned].astype(BF16)
    own_ref[...] = dot(adj_ref[...], x_ref[...])
    far_ref[...] = total[:, owned:].astype(BF16)


def build(tile_rows, tile_cols, tile_vals, x, remote):
    owned, width = x.shape
    num_tiles = tile_vals.shape[0]
    blocks = owned // ROWS
    return pl.pallas_call(
        build_kernel,
        grid_spec=pltpu.PrefetchScalarGridSpec(
            num_scalar_prefetch=2,
            grid=(blocks,),
            in_specs=[whole(tile_vals.shape), whole(x.shape)],
            out_specs=[
                pl.BlockSpec((ROWS, owned), lambda i, *unused: (i, 0)),
                pl.BlockSpec((ROWS, remote), lambda i, *unused: (i, 0)),
                pl.BlockSpec((ROWS, width), lambda i, *unused: (i, 0)),
            ],
            scratch_shapes=[
                pltpu.VMEM((ROWS, owned + remote), F32),
                pltpu.SMEM((num_tiles,), jnp.int32),
                pltpu.SMEM((blocks + 1,), jnp.int32),
                pltpu.SMEM((blocks + 1,), jnp.int32),
            ],
        ),
        out_shape=[
            far_made((owned, owned), BF16),
            far_made((owned, remote), BF16),
            far_made((owned, width), F32),
        ],
        compiler_params=params(48),
        cost_estimate=pl.CostEstimate(
            flops=2 * owned * owned * width, bytes_accessed=40 * 1024 * 1024, transcendentals=0
        ),
        name="build",
    )(tile_rows, tile_cols, tile_vals, x)


def layer_kernel(
    far_hbm, own_hbm, cot_hbm, w_hbm, got_ref,
    act_hbm, hid_hbm, slope_hbm, grad_hbm, back_hbm,
    far, own, cot, act, hid, slope, grad, w, back, sems, sent, w_sem,
):
    blocks = sems.shape[1]
    views = [pl.ds(n * BIG, BIG) for n in range(blocks)]

    def fetch(n):
        pairs = ((far_hbm, far), (own_hbm, own), (cot_hbm, cot))
        copies = [pltpu.make_async_copy(a.at[views[n]], b.at[views[n]], sems.at[k, n]) for k, (a, b) in enumerate(pairs)]
        for copy in copies:
            copy.start()
        return copies

    sending = []

    def send(k, n, a, b, at):
        sending.append(pltpu.make_async_copy(a.at[at], b.at[at], sent.at[k, n]))
        sending[-1].start()

    coming = fetch(0)
    weight = pltpu.make_async_copy(w_hbm, w, w_sem)
    weight.start()
    for n, at in enumerate(views):
        copies = coming
        for copy in copies[:2]:
            copy.wait()
        if n + 1 < blocks:
            coming = fetch(n + 1)
        hid[at, :] = (own[at, :] + dot(far[at, :], got_ref[...])).astype(BF16)
        send(0, n, hid, hid_hbm, at)
        copies[2].wait()
        if n == 0:
            weight.wait()
        preact = dot(hid[at, :], w[...])
        gate = 0.5 + 0.5 * jnp.tanh(0.5 * preact)
        act[at, :] = (preact * gate).astype(BF16)
        send(1, n, act, act_hbm, at)
        slope[at, :] = (cot[at, :].astype(F32) * gate * (1.0 + preact * (1.0 - gate))).astype(BF16)
        send(2, n, slope, slope_hbm, at)
        grad[at, :] = dot(slope[at, :], w[...], ((1,), (1,))).astype(BF16)
        send(3, n, grad, grad_hbm, at)
    for n in range(back.shape[0] // BIG):
        at = pl.ds(n * BIG, BIG)
        back[at, :] = dot(far[:, at], grad[...], ((0,), (0,))).astype(BF16)
        send(4, n, back, back_hbm, at)
    for copy in sending:
        copy.wait()


def layer(keep, far, own, got, cotangent, weight):
    owned, width = own.shape
    remote = got.shape[0]
    blocks = owned // BIG
    (got,) = held(keep, got)
    rows = (owned, width)
    return pl.pallas_call(
        layer_kernel,
        in_specs=[HBM] * 4 + [VMEM],
        out_specs=[HBM] * 5,
        out_shape=[far_made(rows, BF16)] * 4 + [far_made(got.shape, BF16)],
        scratch_shapes=[pltpu.VMEM(far.shape, BF16), pltpu.VMEM(rows, F32)]
        + [pltpu.VMEM(rows, BF16)] * 5
        + [
            pltpu.VMEM(weight.shape, BF16),
            pltpu.VMEM(got.shape, BF16),
            pltpu.SemaphoreType.DMA((3, blocks)),
            pltpu.SemaphoreType.DMA((5, max(blocks, remote // BIG))),
            pltpu.SemaphoreType.DMA,
        ],
        compiler_params=params(40 if keep else 60),
        name="layer",
    )(*stored(far, own, cotangent, weight), got)


def partial_kernel(me_ref, hid_hbm, slope_hbm, mine_ref, other_ref, hid, slope, total, sems):
    blocks = sems.shape[1]
    views = [pl.ds(n * BIG, BIG) for n in range(blocks)]
    coming = [
        [pltpu.make_async_copy(a.at[at], b.at[at], sems.at[k, n]) for k, (a, b) in enumerate(((hid_hbm, hid), (slope_hbm, slope)))]
        for n, at in enumerate(views)
    ]
    for copies in coming:
        for copy in copies:
            copy.start()
    for n, at in enumerate(views):
        for copy in coming[n]:
            copy.wait()
        part = dot(hid[at, :], slope[at, :], ((0,), (0,)))
        total[...] = part if n == 0 else total[...] + part
    half = mine_ref.shape[0]
    core = me_ref[0] % 2
    for out_ref, first in ((other_ref, (1 - core) * half), (mine_ref, core * half)):
        out_ref[...] = total[pl.ds(pl.multiple_of(first, half), half), :].astype(out_ref.dtype)


def partial_grad(keep, me, hidden, slope):
    owned, width = hidden.shape
    half = (width // 2, width)
    return pl.pallas_call(
        partial_kernel,
        in_specs=[SMEM, HBM, HBM],
        out_specs=[VMEM, VMEM],
        out_shape=[made(keep, half, F32), made(keep, half, BF16)],
        scratch_shapes=[
            pltpu.VMEM((owned, width), BF16),
            pltpu.VMEM((owned, width), BF16),
            pltpu.VMEM((width, width), F32),
            pltpu.SemaphoreType.DMA((2, owned // BIG)),
        ],
        compiler_params=params(20),
        name="partial_grad",
    )(me, *stored(hidden, slope))


def spread_kernel(adj_ref, grad_ref, out_ref):
    out_ref[...] = dot(adj_ref[...], grad_ref[...], ((0,), (0,)))


def spread(adjacency, grad, part, parts):
    owned, width = grad.shape
    blocks = owned // BIG // parts
    return pl.pallas_call(
        spread_kernel,
        grid=(blocks,),
        in_specs=[pl.BlockSpec((owned, BIG), lambda i: (0, i + part * blocks)), whole(grad.shape)],
        out_specs=pl.BlockSpec((BIG, width), lambda i: (i, 0)),
        out_shape=far_made((owned // parts, width), F32),
        compiler_params=params(60),
        cost_estimate=pl.CostEstimate(
            flops=2 * owned * owned * width, bytes_accessed=16 * 1024 * 1024, transcendentals=0
        ),
        name="spread",
    )(*stored(adjacency, grad))


def return_kernel(index_ref, first_hbm, second_hbm, got_ref, out_hbm, owned, out, sems, sent):
    blocks = sems.shape[0]
    views = [pl.ds(n * BIG, BIG) for n in range(blocks)]
    coming = []
    for n, at in enumerate(views):
        half_hbm = (first_hbm, second_hbm)[2 * n // blocks]
        coming.append(pltpu.make_async_copy(half_hbm.at[views[n % (blocks // 2)]], owned.at[at], sems.at[n]))
    for copy in coming:
        copy.start()

    def pick(n):
        row = lax.broadcasted_iota(jnp.int32, (BIG, index_ref.shape[1]), 0) + n * BIG
        return jnp.where(row == index_ref[...], 1.0, 0.0).astype(BF16)

    sending = []
    for n, at in enumerate(views):
        added = dot(pick(n), got_ref[...])
        coming[n].wait()
        out[at, :] = (owned[at, :] + added).astype(BF16)
        sending.append(pltpu.make_async_copy(out.at[at], out_hbm.at[at], sent.at[n]))
        sending[n].start()
    for copy in sending:
        copy.wait()


def give_back(keep, index, first, second, got):
    rows, width = 2 * first.shape[0], first.shape[1]
    (got,) = held(keep, got)
    return pl.pallas_call(
        return_kernel,
        in_specs=[VMEM, HBM, HBM, VMEM],
        out_specs=HBM,
        out_shape=far_made((rows, width), BF16),
        scratch_shapes=[
            pltpu.VMEM((rows, width), F32),
            pltpu.VMEM((rows, width), BF16),
            pltpu.SemaphoreType.DMA((rows // BIG,)),
            pltpu.SemaphoreType.DMA((rows // BIG,)),
        ],
        compiler_params=params(28 if keep else 60),
        name="give_back",
    )(index, *stored(first, second), got)


def exchange(x, axes):
    return lax.all_to_all(x, axes, split_axis=0, concat_axis=0, tiled=True)


def cut_kernel(me_ref, mine_ref, got_ref, *out_refs):
    height = mine_ref.shape[0] // len(out_refs)
    for k, out_ref in enumerate(out_refs):
        at = pl.ds(pl.multiple_of(((me_ref[0] // 2) ^ k) * height, height), height)
        out_ref[...] = (mine_ref[at, :] + got_ref[at, :].astype(F32)).astype(out_ref.dtype)


def cut(me, mine, got, chips):
    height, width = got.shape[0] // chips, got.shape[1]
    return pl.pallas_call(
        cut_kernel,
        in_specs=[SMEM, VMEM, VMEM],
        out_shape=[jax.ShapeDtypeStruct((height, width), F32 if k == 0 else BF16) for k in range(chips)],
        compiler_params=params(8),
        name="cut",
    )(me, mine, got)


def relay_kernel(after_ref, *refs):
    height = refs[0].shape[0]
    for k, ref in enumerate(refs[:-1]):
        refs[-1][k * height : (k + 1) * height, :] = ref[...]


def relay(after, pieces):
    height, width = pieces[0].shape
    return pl.pallas_call(
        relay_kernel,
        in_specs=[HBM] + [VMEM] * len(pieces),
        out_shape=jax.ShapeDtypeStruct((height * len(pieces), width), BF16),
        compiler_params=params(8),
        name="relay",
    )(*stored(after), *pieces)


def join_kernel(chips, me_ref, mine_ref, other_ref, out_ref):
    half = mine_ref.shape[0]
    height = half // chips
    core, chip = me_ref[0] % 2, me_ref[0] // 2
    for owner, ref in ((core, mine_ref), (1 - core, other_ref)):
        for k in range(chips):
            at = pl.multiple_of(owner * half + (chip ^ k) * height, height)
            out_ref[pl.ds(at, height), :] = ref[k * height : (k + 1) * height, :].astype(F32)


def join(me, mine, other, chips):
    half, width = mine.shape
    return pl.pallas_call(
        functools.partial(join_kernel, chips),
        in_specs=[SMEM, VMEM, VMEM],
        out_shape=jax.ShapeDtypeStruct((2 * half, width), F32),
        compiler_params=params(8),
        name="join",
    )(me, mine, other)


def add_kernel(after_ref, *refs):
    parts = [ref[...].astype(F32) for ref in refs[:-1]]
    while len(parts) > 1:
        parts = [parts[k] + parts[k + 1] for k in range(0, len(parts), 2)]
    refs[-1][...] = parts[0].astype(BF16)


def add(after, parts):
    return pl.pallas_call(
        add_kernel,
        in_specs=[HBM] + [VMEM] * len(parts),
        out_shape=jax.ShapeDtypeStruct(parts[0].shape, BF16),
        compiler_params=params(8),
        name="add",
    )(*stored(after), *parts)


def swap(x, axis, size, k):
    return lax.ppermute(x, axis, [(i, i ^ k) for i in range(size)])


def per_device(groups, locals_, features, weight, cotangent, tile_vals, tile_rows, tile_cols, send_rows, counts):
    rows_own, width = features.shape
    lists = send_rows[0]
    peers, slots = lists.shape
    remote = peers * slots
    keep = remote <= rows_own
    me = lax.axis_index("local").astype(jnp.int32).reshape(1)
    outgoing = collect(counts, lists, features)
    arrived = exchange(outgoing.reshape(peers, slots, width), AXES).reshape(remote, width)
    adjacency, far, own = build(tile_rows, tile_cols, tile_vals, features, remote)
    activated, hidden, slope, grad, back = layer(keep, far, own, arrived, cotangent, weight)
    returned = exchange(back.reshape(peers, slots, width), AXES).reshape(remote, width)
    first = spread(adjacency, grad, 0, 2)
    second = spread(adjacency, grad, 1, 2)
    live = jnp.arange(slots)[None, :] < counts[0][:, None]
    feature_grad = give_back(keep, jnp.where(live, lists, -1).reshape(1, remote), first, second, returned)
    chips = locals_ // 2
    mine, other = partial_grad(keep, me, hidden, slope)
    pieces = cut(me, mine, swap(other, "local", locals_, 1), chips)
    piece = add(first, [pieces[0]] + [swap(pieces[k], "local", locals_, 2 * k) for k in range(1, chips)])
    step, after = 1, second
    while step < groups:
        piece = add(after, [piece, swap(piece, "group", groups, step)])
        step, after = 2 * step, second
    pieces = [piece] + [swap(piece, "local", locals_, 2 * k) for k in range(1, chips)]
    half = relay(feature_grad, pieces)
    weight_grad = join(me, half, swap(half, "local", locals_, 1), chips)
    return activated, feature_grad, weight_grad


def solution(mesh):
    return jax.shard_map(
        functools.partial(per_device, mesh.shape["group"], mesh.shape["local"]),
        mesh=mesh,
        in_specs=(
            P(AXES, None),
            P(),
            P(AXES, None),
            P(AXES, None, None),
            P(AXES),
            P(AXES),
            P(AXES, None, None),
            P(AXES, None),
        ),
        out_specs=(P(AXES, None), P(AXES, None), P()),
        check_vma=False,
    )
```

```python
import functools

import jax
import jax.numpy as jnp
from jax import lax
from jax.experimental import pallas as pl
from jax.experimental.pallas import tpu as pltpu
from jax.sharding import PartitionSpec as P

AXES = ("group", "local")
BF16 = jnp.bfloat16
F32 = jnp.float32
ROWS = 256
BIG = 512
MIB = 1024 * 1024


def params(mib):
    return pltpu.CompilerParams(vmem_limit_bytes=mib * MIB)


VMEM = pl.BlockSpec(memory_space=pltpu.VMEM)
SMEM = pl.BlockSpec(memory_space=pltpu.SMEM)
HBM = pl.BlockSpec(memory_space=pltpu.MemorySpace.HBM)


def made(keep, shape, dtype):
    return pltpu.VMEM(shape, dtype) if keep else jax.ShapeDtypeStruct(shape, dtype)


def held(keep, *arrays):
    if not keep:
        return arrays
    return [pltpu.with_memory_space_constraint(x, pltpu.VMEM) for x in arrays]


def stored(*arrays):
    return [pltpu.with_memory_space_constraint(x, pltpu.MemorySpace.HBM) for x in arrays]


def far_made(shape, dtype):
    return pltpu.MemorySpace.HBM(shape, dtype)


def dot(a, b, contract=((1,), (0,))):
    return lax.dot_general(a, b, (contract, ((), ())), preferred_element_type=F32)


def whole(shape):
    return pl.BlockSpec(shape, lambda i, *unused: (0,) * len(shape))


def collect_kernel(counts_ref, lists_ref, x_hbm, out_hbm, x, total, out, came, sent):
    dests, slots = lists_ref.shape
    step = BIG // slots
    chunks, rounds = came.shape[0], sent.shape[0]
    deep = x.shape[0] // chunks
    fetch = []
    for k in range(chunks):
        at = pl.ds(k * deep, deep)
        fetch.append(pltpu.make_async_copy(x_hbm.at[at], x.at[at], came.at[k]))
        fetch[k].start()
    lane = lax.broadcasted_iota(jnp.int32, (slots, deep), 1)
    slot = lax.broadcasted_iota(jnp.int32, (slots, 1), 0)
    turned = lists_ref[...].T
    named = [jnp.where(slot < counts_ref[0, d], turned[:, d : d + 1], -1) for d in range(dests)]
    sending = []
    for k in range(chunks):
        fetch[k].wait()
        for n in range(rounds):
            at = pl.ds(n * BIG, BIG)
            picks = [jnp.where(named[d] - k * deep == lane, 1.0, 0.0).astype(BF16) for d in range(n * step, (n + 1) * step)]
            found = dot(jnp.concatenate(picks, axis=0), x[k * deep : (k + 1) * deep, :])
            if k > 0:
                found = total[at, :] + found
            if k + 1 < chunks:
                total[at, :] = found
            else:
                out[at, :] = found.astype(BF16)
                sending.append(pltpu.make_async_copy(out.at[at], out_hbm.at[at], sent.at[n]))
                sending[n].start()
    for copy in sending:
        copy.wait()


def collect(counts, lists, x):
    dests, slots = lists.shape
    shape = (dests * slots, x.shape[1])
    return pl.pallas_call(
        collect_kernel,
        in_specs=[SMEM, VMEM, HBM],
        out_specs=HBM,
        out_shape=far_made(shape, BF16),
        scratch_shapes=[
            pltpu.VMEM(x.shape, BF16),
            pltpu.VMEM(shape, F32),
            pltpu.VMEM(shape, BF16),
            pltpu.SemaphoreType.DMA((4,)),
            pltpu.SemaphoreType.DMA((shape[0] // BIG,)),
        ],
        compiler_params=params(60),
        name="collect",
    )(counts, lists, *stored(x))


def build_kernel(rows_ref, cols_ref, tiles_ref, x_ref, adj_ref, far_ref, own_ref, total, order, starts, cursor):
    num_tiles, edge = tiles_ref.shape[0], tiles_ref.shape[1]
    per = ROWS // edge
    blocks = pl.num_programs(0)
    i = pl.program_id(0)

    @pl.when(i == 0)
    def _():
        def clear(b, unused):
            starts[b] = 0
            return unused

        lax.fori_loop(0, blocks + 1, clear, 0)

        def count(t, unused):
            k = rows_ref[t] // per + 1
            starts[k] = starts[k] + 1
            return unused

        lax.fori_loop(0, num_tiles, count, 0, unroll=4)

        def add(b, running):
            running = running + starts[b]
            starts[b] = running
            cursor[b] = running
            return running

        lax.fori_loop(0, blocks + 1, add, 0)

        def place(t, unused):
            k = rows_ref[t] // per
            at = cursor[k]
            cursor[k] = at + 1
            order[at] = t
            return unused

        lax.fori_loop(0, num_tiles, place, 0, unroll=4)

    total[...] = jnp.zeros_like(total)

    def one(j, unused):
        t = order[j]
        r = pl.multiple_of((rows_ref[t] % per) * edge, edge)
        c = pl.multiple_of(cols_ref[t] * edge, edge)
        at = (pl.ds(r, edge), pl.ds(c, edge))
        total[at] = total[at] + tiles_ref[t].astype(F32)
        return unused

    lax.fori_loop(starts[i], starts[i + 1], one, 0)
    owned = x_ref.shape[0]
    adj_ref[...] = total[:, :owned].astype(BF16)
    own_ref[...] = dot(adj_ref[...], x_ref[...])
    far_ref[...] = total[:, owned:].astype(BF16)


def build(tile_rows, tile_cols, tile_vals, x, remote):
    owned, width = x.shape
    num_tiles = tile_vals.shape[0]
    blocks = owned // ROWS
    return pl.pallas_call(
        build_kernel,
        grid_spec=pltpu.PrefetchScalarGridSpec(
            num_scalar_prefetch=2,
            grid=(blocks,),
            in_specs=[whole(tile_vals.shape), whole(x.shape)],
            out_specs=[
                pl.BlockSpec((ROWS, owned), lambda i, *unused: (i, 0)),
                pl.BlockSpec((ROWS, remote), lambda i, *unused: (i, 0)),
                pl.BlockSpec((ROWS, width), lambda i, *unused: (i, 0)),
            ],
            scratch_shapes=[
                pltpu.VMEM((ROWS, owned + remote), F32),
                pltpu.SMEM((num_tiles,), jnp.int32),
                pltpu.SMEM((blocks + 1,), jnp.int32),
                pltpu.SMEM((blocks + 1,), jnp.int32),
            ],
        ),
        out_shape=[
            far_made((owned, owned), BF16),
            far_made((owned, remote), BF16),
            far_made((owned, width), F32),
        ],
        compiler_params=params(48),
        cost_estimate=pl.CostEstimate(
            flops=2 * owned * owned * width, bytes_accessed=40 * 1024 * 1024, transcendentals=0
        ),
        name="build",
    )(tile_rows, tile_cols, tile_vals, x)


def layer_kernel(
    far_hbm, own_hbm, cot_hbm, w_hbm, got_ref,
    act_hbm, hid_hbm, slope_hbm, grad_hbm, back_hbm,
    far, own, cot, act, hid, slope, grad, w, pre, back, sems, sent, w_sem,
):
    blocks = sems.shape[1]
    views = [pl.ds(n * BIG, BIG) for n in range(blocks)]

    def fetch(n):
        pairs = ((far_hbm, far), (own_hbm, own), (cot_hbm, cot))
        copies = [pltpu.make_async_copy(a.at[views[n]], b.at[views[n]], sems.at[k, n]) for k, (a, b) in enumerate(pairs)]
        for copy in copies:
            copy.start()
        return copies

    sending = []

    def send(k, n, a, b, at):
        sending.append(pltpu.make_async_copy(a.at[at], b.at[at], sent.at[k, n]))
        sending[-1].start()

    coming = fetch(0)
    weight = pltpu.make_async_copy(w_hbm, w, w_sem)
    weight.start()
    for n in range(blocks + 1):
        if n < blocks:
            at = views[n]
            for copy in coming:
                copy.wait()
            if n == 0:
                weight.wait()
            if n + 1 < blocks:
                coming = fetch(n + 1)
        if n > 0:
            old = views[n - 1]
            preact = pre[(n - 1) % 2]
            gate = 0.5 + 0.5 * jnp.tanh(0.5 * preact)
            activated = (preact * gate).astype(BF16)
            slopes = (cot[old, :].astype(F32) * gate * (1.0 + preact * (1.0 - gate))).astype(BF16)
        if n < blocks:
            hidden = (own[at, :] + dot(far[at, :], got_ref[...])).astype(BF16)
            hid[at, :] = hidden
            pre[n % 2] = dot(hidden, w[...])
        if n > 0:
            act[old, :] = activated
            slope[old, :] = slopes
            grad[old, :] = dot(slopes, w[...], ((1,), (1,))).astype(BF16)
            for k, (ref, ref_hbm) in enumerate(((act, act_hbm), (slope, slope_hbm), (grad, grad_hbm))):
                send(k + 1, n - 1, ref, ref_hbm, old)
        if n < blocks:
            send(0, n, hid, hid_hbm, at)
    for n in range(back.shape[0] // BIG):
        at = pl.ds(n * BIG, BIG)
        back[at, :] = dot(far[:, at], grad[...], ((0,), (0,))).astype(BF16)
        send(4, n, back, back_hbm, at)
    for copy in sending:
        copy.wait()


def layer(keep, far, own, got, cotangent, weight):
    owned, width = own.shape
    remote = got.shape[0]
    blocks = owned // BIG
    (got,) = held(keep, got)
    rows = (owned, width)
    return pl.pallas_call(
        layer_kernel,
        in_specs=[HBM] * 4 + [VMEM],
        out_specs=[HBM] * 5,
        out_shape=[far_made(rows, BF16)] * 4 + [far_made(got.shape, BF16)],
        scratch_shapes=[pltpu.VMEM(far.shape, BF16), pltpu.VMEM(rows, F32)]
        + [pltpu.VMEM(rows, BF16)] * 5
        + [
            pltpu.VMEM(weight.shape, BF16),
            pltpu.VMEM((2, BIG, width), F32),
            pltpu.VMEM(got.shape, BF16),
            pltpu.SemaphoreType.DMA((3, blocks)),
            pltpu.SemaphoreType.DMA((5, max(blocks, remote // BIG))),
            pltpu.SemaphoreType.DMA,
        ],
        compiler_params=params(40 if keep else 60),
        name="layer",
    )(*stored(far, own, cotangent, weight), got)


def partial_kernel(me_ref, hid_hbm, slope_hbm, mine_ref, other_ref, hid, slope, total, sems):
    blocks = sems.shape[1]
    views = [pl.ds(n * BIG, BIG) for n in range(blocks)]
    coming = [
        [pltpu.make_async_copy(a.at[at], b.at[at], sems.at[k, n]) for k, (a, b) in enumerate(((hid_hbm, hid), (slope_hbm, slope)))]
        for n, at in enumerate(views)
    ]
    for copies in coming:
        for copy in copies:
            copy.start()
    for n, at in enumerate(views):
        for copy in coming[n]:
            copy.wait()
        part = dot(hid[at, :], slope[at, :], ((0,), (0,)))
        total[...] = part if n == 0 else total[...] + part
    half = mine_ref.shape[0]
    core = me_ref[0] % 2
    for out_ref, first in ((other_ref, (1 - core) * half), (mine_ref, core * half)):
        out_ref[...] = total[pl.ds(pl.multiple_of(first, half), half), :].astype(out_ref.dtype)


def partial_grad(keep, me, hidden, slope):
    owned, width = hidden.shape
    half = (width // 2, width)
    return pl.pallas_call(
        partial_kernel,
        in_specs=[SMEM, HBM, HBM],
        out_specs=[VMEM, VMEM],
        out_shape=[made(keep, half, F32), made(keep, half, BF16)],
        scratch_shapes=[
            pltpu.VMEM((owned, width), BF16),
            pltpu.VMEM((owned, width), BF16),
            pltpu.VMEM((width, width), F32),
            pltpu.SemaphoreType.DMA((2, owned // BIG)),
        ],
        compiler_params=params(20),
        name="partial_grad",
    )(me, *stored(hidden, slope))


def spread_kernel(adj_ref, grad_ref, out_ref):
    out_ref[...] = dot(adj_ref[...], grad_ref[...], ((0,), (0,)))


def spread(adjacency, grad, part, parts):
    owned, width = grad.shape
    blocks = owned // BIG // parts
    return pl.pallas_call(
        spread_kernel,
        grid=(blocks,),
        in_specs=[pl.BlockSpec((owned, BIG), lambda i: (0, i + part * blocks)), whole(grad.shape)],
        out_specs=pl.BlockSpec((BIG, width), lambda i: (i, 0)),
        out_shape=far_made((owned // parts, width), F32),
        compiler_params=params(60),
        cost_estimate=pl.CostEstimate(
            flops=2 * owned * owned * width, bytes_accessed=16 * 1024 * 1024, transcendentals=0
        ),
        name="spread",
    )(*stored(adjacency, grad))


def return_kernel(index_ref, first_hbm, second_hbm, got_ref, out_hbm, owned, out, sems, sent):
    blocks = sems.shape[0]
    views = [pl.ds(n * BIG, BIG) for n in range(blocks)]
    coming = []
    for n, at in enumerate(views):
        half_hbm = (first_hbm, second_hbm)[2 * n // blocks]
        coming.append(pltpu.make_async_copy(half_hbm.at[views[n % (blocks // 2)]], owned.at[at], sems.at[n]))
    for copy in coming:
        copy.start()

    def pick(n):
        row = lax.broadcasted_iota(jnp.int32, (BIG, index_ref.shape[1]), 0) + n * BIG
        return jnp.where(row == index_ref[...], 1.0, 0.0).astype(BF16)

    sending = []
    for n, at in enumerate(views):
        added = dot(pick(n), got_ref[...])
        coming[n].wait()
        out[at, :] = (owned[at, :] + added).astype(BF16)
        sending.append(pltpu.make_async_copy(out.at[at], out_hbm.at[at], sent.at[n]))
        sending[n].start()
    for copy in sending:
        copy.wait()


def give_back(keep, index, first, second, got):
    rows, width = 2 * first.shape[0], first.shape[1]
    (got,) = held(keep, got)
    return pl.pallas_call(
        return_kernel,
        in_specs=[VMEM, HBM, HBM, VMEM],
        out_specs=HBM,
        out_shape=far_made((rows, width), BF16),
        scratch_shapes=[
            pltpu.VMEM((rows, width), F32),
            pltpu.VMEM((rows, width), BF16),
            pltpu.SemaphoreType.DMA((rows // BIG,)),
            pltpu.SemaphoreType.DMA((rows // BIG,)),
        ],
        compiler_params=params(28 if keep else 60),
        name="give_back",
    )(index, *stored(first, second), got)


def exchange(x, axes):
    return lax.all_to_all(x, axes, split_axis=0, concat_axis=0, tiled=True)


def cut_kernel(me_ref, mine_ref, got_ref, *out_refs):
    height = mine_ref.shape[0] // len(out_refs)
    for k, out_ref in enumerate(out_refs):
        at = pl.ds(pl.multiple_of(((me_ref[0] // 2) ^ k) * height, height), height)
        out_ref[...] = (mine_ref[at, :] + got_ref[at, :].astype(F32)).astype(out_ref.dtype)


def cut(me, mine, got, chips):
    height, width = got.shape[0] // chips, got.shape[1]
    return pl.pallas_call(
        cut_kernel,
        in_specs=[SMEM, VMEM, VMEM],
        out_shape=[jax.ShapeDtypeStruct((height, width), F32 if k == 0 else BF16) for k in range(chips)],
        compiler_params=params(8),
        name="cut",
    )(me, mine, got)


def relay_kernel(after_ref, *refs):
    height = refs[0].shape[0]
    for k, ref in enumerate(refs[:-1]):
        refs[-1][k * height : (k + 1) * height, :] = ref[...]


def relay(after, pieces):
    height, width = pieces[0].shape
    return pl.pallas_call(
        relay_kernel,
        in_specs=[HBM] + [VMEM] * len(pieces),
        out_shape=jax.ShapeDtypeStruct((height * len(pieces), width), BF16),
        compiler_params=params(8),
        name="relay",
    )(*stored(after), *pieces)


def place_kernel(chips, other, me_ref, half_ref, *refs):
    out_hbm, placed, sem = refs[-3:]
    half = half_ref.shape[0]
    height = half // chips
    for k in range(chips):
        at = pl.multiple_of(((me_ref[0] // 2) ^ k) * height, height)
        placed[pl.ds(at, height), :] = half_ref[k * height : (k + 1) * height, :].astype(F32)
    at = pl.multiple_of((me_ref[0] + other) % 2 * half, half)
    copy = pltpu.make_async_copy(placed, out_hbm.at[pl.ds(at, half)], sem)
    copy.start()
    copy.wait()


def place(me, half, chips, into=()):
    return pl.pallas_call(
        functools.partial(place_kernel, chips, len(into)),
        in_specs=[SMEM, VMEM] + [HBM] * len(into),
        out_specs=HBM,
        out_shape=far_made((2 * half.shape[0], half.shape[1]), F32),
        scratch_shapes=[pltpu.VMEM(half.shape, F32), pltpu.SemaphoreType.DMA],
        input_output_aliases={2: 0} if into else {},
        compiler_params=params(8),
        name="place",
    )(me, half, *stored(*into))


def add_kernel(after_ref, *refs):
    parts = [ref[...].astype(F32) for ref in refs[:-1]]
    while len(parts) > 1:
        parts = [parts[k] + parts[k + 1] for k in range(0, len(parts), 2)]
    refs[-1][...] = parts[0].astype(BF16)


def add(after, parts):
    return pl.pallas_call(
        add_kernel,
        in_specs=[HBM] + [VMEM] * len(parts),
        out_shape=jax.ShapeDtypeStruct(parts[0].shape, BF16),
        compiler_params=params(8),
        name="add",
    )(*stored(after), *parts)


def swap(x, axis, size, k):
    return lax.ppermute(x, axis, [(i, i ^ k) for i in range(size)])


def per_device(groups, locals_, features, weight, cotangent, tile_vals, tile_rows, tile_cols, send_rows, counts):
    rows_own, width = features.shape
    lists = send_rows[0]
    peers, slots = lists.shape
    remote = peers * slots
    keep = remote <= rows_own
    me = lax.axis_index("local").astype(jnp.int32).reshape(1)
    outgoing = collect(counts, lists, features)
    arrived = exchange(outgoing.reshape(peers, slots, width), AXES).reshape(remote, width)
    adjacency, far, own = build(tile_rows, tile_cols, tile_vals, features, remote)
    activated, hidden, slope, grad, back = layer(keep, far, own, arrived, cotangent, weight)
    returned = exchange(back.reshape(peers, slots, width), AXES).reshape(remote, width)
    first = spread(adjacency, grad, 0, 2)
    second = spread(adjacency, grad, 1, 2)
    live = jnp.arange(slots)[None, :] < counts[0][:, None]
    feature_grad = give_back(keep, jnp.where(live, lists, -1).reshape(1, remote), first, second, returned)
    chips = locals_ // 2
    mine, other = partial_grad(keep, me, hidden, slope)
    pieces = cut(me, mine, swap(other, "local", locals_, 1), chips)
    piece = add(first, [pieces[0]] + [swap(pieces[k], "local", locals_, 2 * k) for k in range(1, chips)])
    step, after = 1, second
    while step < groups:
        piece = add(after, [piece, swap(piece, "group", groups, step)])
        step, after = 2 * step, second
    pieces = [piece] + [swap(piece, "local", locals_, 2 * k) for k in range(1, chips)]
    half = relay(feature_grad, pieces)
    weight_grad = place(me, swap(half, "local", locals_, 1), chips, [place(me, half, chips)])
    return activated, feature_grad, weight_grad


def solution(mesh):
    return jax.shard_map(
        functools.partial(per_device, mesh.shape["group"], mesh.shape["local"]),
        mesh=mesh,
        in_specs=(
            P(AXES, None),
            P(),
            P(AXES, None),
            P(AXES, None, None),
            P(AXES),
            P(AXES),
            P(AXES, None, None),
            P(AXES, None),
        ),
        out_specs=(P(AXES, None), P(AXES, None), P()),
        check_vma=False,
    )
```

```python
import functools

import jax
import jax.numpy as jnp
from jax import lax
from jax.experimental import pallas as pl
from jax.experimental.pallas import tpu as pltpu
from jax.sharding import PartitionSpec as P

AXES = ("group", "local")
BF16 = jnp.bfloat16
F32 = jnp.float32
ROWS = 256
BIG = 512
MIB = 1024 * 1024


def params(mib):
    return pltpu.CompilerParams(vmem_limit_bytes=mib * MIB)


VMEM = pl.BlockSpec(memory_space=pltpu.VMEM)
SMEM = pl.BlockSpec(memory_space=pltpu.SMEM)
HBM = pl.BlockSpec(memory_space=pltpu.MemorySpace.HBM)


def made(keep, shape, dtype):
    return pltpu.VMEM(shape, dtype) if keep else jax.ShapeDtypeStruct(shape, dtype)


def held(keep, *arrays):
    if not keep:
        return arrays
    return [pltpu.with_memory_space_constraint(x, pltpu.VMEM) for x in arrays]


def stored(*arrays):
    return [pltpu.with_memory_space_constraint(x, pltpu.MemorySpace.HBM) for x in arrays]


def far_made(shape, dtype):
    return pltpu.MemorySpace.HBM(shape, dtype)


def dot(a, b, contract=((1,), (0,))):
    return lax.dot_general(a, b, (contract, ((), ())), preferred_element_type=F32)


def whole(shape):
    return pl.BlockSpec(shape, lambda i, *unused: (0,) * len(shape))


def digits(index):
    return (index >> 7).astype(F32).astype(BF16), (index & 127).astype(F32).astype(BF16)


def collect_kernel(counts_ref, lists_ref, x_ref, out_ref):
    dests, slots = lists_ref.shape
    step = BIG // slots
    lane = lax.broadcasted_iota(jnp.int32, (slots, 128), 1).astype(F32).astype(BF16)
    slot = lax.broadcasted_iota(jnp.int32, (slots, 1), 0)
    one, zero = jnp.ones((slots, 128), BF16), jnp.zeros((slots, 128), BF16)
    turned = lists_ref[...].T
    for first in range(0, dests, step):
        parts = []
        for d in range(first, first + step):
            named = jnp.where(slot < counts_ref[0, d], turned[:, d : d + 1], -1)
            high, low = digits(jnp.broadcast_to(named, (slots, 128)))
            hit = jnp.where(low == lane, one, zero)
            tiles = [jnp.where(high == t, hit, zero) for t in range(x_ref.shape[0] // 128)]
            parts.append(jnp.concatenate(tiles, axis=1))
        pick = jnp.concatenate(parts, axis=0)
        out_ref[first * slots : (first + step) * slots, :] = dot(pick, x_ref[...]).astype(BF16)


def collect(counts, lists, x):
    dests, slots = lists.shape
    return pl.pallas_call(
        collect_kernel,
        in_specs=[SMEM, VMEM, VMEM],
        out_shape=jax.ShapeDtypeStruct((dests * slots, x.shape[1]), BF16),
        compiler_params=params(60),
        name="collect",
    )(counts, lists, x)


def build_kernel(rows_ref, cols_ref, tiles_ref, x_ref, adj_ref, far_ref, own_ref, total, order, starts, cursor):
    num_tiles, edge = tiles_ref.shape[0], tiles_ref.shape[1]
    per = ROWS // edge
    blocks = pl.num_programs(0)
    i = pl.program_id(0)

    @pl.when(i == 0)
    def _():
        def clear(b, unused):
            starts[b] = 0
            return unused

        lax.fori_loop(0, blocks + 1, clear, 0)

        def count(t, unused):
            k = rows_ref[t] // per + 1
            starts[k] = starts[k] + 1
            return unused

        lax.fori_loop(0, num_tiles, count, 0, unroll=4)

        def add(b, running):
            running = running + starts[b]
            starts[b] = running
            cursor[b] = running
            return running

        lax.fori_loop(0, blocks + 1, add, 0)

        def place(t, unused):
            k = rows_ref[t] // per
            at = cursor[k]
            cursor[k] = at + 1
            order[at] = t
            return unused

        lax.fori_loop(0, num_tiles, place, 0, unroll=4)

    total[...] = jnp.zeros_like(total)

    def one(j, unused):
        t = order[j]
        r = pl.multiple_of((rows_ref[t] % per) * edge, edge)
        c = pl.multiple_of(cols_ref[t] * edge, edge)
        at = (pl.ds(r, edge), pl.ds(c, edge))
        total[at] = total[at] + tiles_ref[t].astype(F32)
        return unused

    lax.fori_loop(starts[i], starts[i + 1], one, 0)
    owned = x_ref.shape[0]
    adj_ref[...] = total[:, :owned].astype(BF16)
    own_ref[...] = dot(adj_ref[...], x_ref[...])
    far_ref[...] = total[:, owned:].astype(BF16)


def build(tile_rows, tile_cols, tile_vals, x, remote):
    owned, width = x.shape
    num_tiles = tile_vals.shape[0]
    blocks = owned // ROWS
    return pl.pallas_call(
        build_kernel,
        grid_spec=pltpu.PrefetchScalarGridSpec(
            num_scalar_prefetch=2,
            grid=(blocks,),
            in_specs=[whole(tile_vals.shape), whole(x.shape)],
            out_specs=[
                pl.BlockSpec((ROWS, owned), lambda i, *unused: (i, 0)),
                pl.BlockSpec((ROWS, remote), lambda i, *unused: (i, 0)),
                pl.BlockSpec((ROWS, width), lambda i, *unused: (i, 0)),
            ],
            scratch_shapes=[
                pltpu.VMEM((ROWS, owned + remote), F32),
                pltpu.SMEM((num_tiles,), jnp.int32),
                pltpu.SMEM((blocks + 1,), jnp.int32),
                pltpu.SMEM((blocks + 1,), jnp.int32),
            ],
        ),
        out_shape=[
            far_made((owned, owned), BF16),
            far_made((owned, remote), BF16),
            far_made((owned, width), F32),
        ],
        compiler_params=params(48),
        cost_estimate=pl.CostEstimate(
            flops=2 * owned * owned * width, bytes_accessed=40 * 1024 * 1024, transcendentals=0
        ),
        name="build",
    )(tile_rows, tile_cols, tile_vals, x)


def layer_kernel(
    far_hbm, own_hbm, cot_hbm, w_hbm, got_ref,
    act_hbm, hid_hbm, slope_hbm, grad_hbm, back_hbm,
    far, own, cot, act, hid, slope, grad, w, back, sems, sent, w_sem,
):
    blocks = sems.shape[1]
    views = [pl.ds(n * BIG, BIG) for n in range(blocks)]

    def fetch(n):
        pairs = ((far_hbm, far), (own_hbm, own), (cot_hbm, cot))
        copies = [pltpu.make_async_copy(a.at[views[n]], b.at[views[n]], sems.at[k, n]) for k, (a, b) in enumerate(pairs)]
        for copy in copies:
            copy.start()
        return copies

    sending = []

    def send(k, n, a, b, at):
        sending.append(pltpu.make_async_copy(a.at[at], b.at[at], sent.at[k, n]))
        sending[-1].start()

    coming = fetch(0)
    weight = pltpu.make_async_copy(w_hbm, w, w_sem)
    weight.start()
    for n, at in enumerate(views):
        copies = coming
        for copy in copies[:2]:
            copy.wait()
        if n + 1 < blocks:
            coming = fetch(n + 1)
        hid[at, :] = (own[at, :] + dot(far[at, :], got_ref[...])).astype(BF16)
        send(0, n, hid, hid_hbm, at)
        copies[2].wait()
        if n == 0:
            weight.wait()
        preact = dot(hid[at, :], w[...])
        gate = 0.5 + 0.5 * jnp.tanh(0.5 * preact)
        act[at, :] = (preact * gate).astype(BF16)
        send(1, n, act, act_hbm, at)
        slope[at, :] = (cot[at, :].astype(F32) * gate * (1.0 + preact * (1.0 - gate))).astype(BF16)
        send(2, n, slope, slope_hbm, at)
        grad[at, :] = dot(slope[at, :], w[...], ((1,), (1,))).astype(BF16)
        send(3, n, grad, grad_hbm, at)
    for n in range(back.shape[0] // BIG):
        at = pl.ds(n * BIG, BIG)
        back[at, :] = dot(far[:, at], grad[...], ((0,), (0,))).astype(BF16)
        send(4, n, back, back_hbm, at)
    for copy in sending:
        copy.wait()


def layer(keep, far, own, got, cotangent, weight):
    owned, width = own.shape
    remote = got.shape[0]
    blocks = owned // BIG
    (got,) = held(keep, got)
    rows = (owned, width)
    return pl.pallas_call(
        layer_kernel,
        in_specs=[HBM] * 4 + [VMEM],
        out_specs=[HBM] * 5,
        out_shape=[far_made(rows, BF16)] * 4 + [far_made(got.shape, BF16)],
        scratch_shapes=[pltpu.VMEM(far.shape, BF16), pltpu.VMEM(rows, F32)]
        + [pltpu.VMEM(rows, BF16)] * 5
        + [
            pltpu.VMEM(weight.shape, BF16),
            pltpu.VMEM(got.shape, BF16),
            pltpu.SemaphoreType.DMA((3, blocks)),
            pltpu.SemaphoreType.DMA((5, max(blocks, remote // BIG))),
            pltpu.SemaphoreType.DMA,
        ],
        compiler_params=params(40 if keep else 60),
        name="layer",
    )(*stored(far, own, cotangent, weight), got)


def partial_kernel(me_ref, hid_hbm, slope_hbm, mine_ref, other_ref, hid, slope, total, sems):
    blocks = sems.shape[1]
    views = [pl.ds(n * BIG, BIG) for n in range(blocks)]
    coming = [
        [pltpu.make_async_copy(a.at[at], b.at[at], sems.at[k, n]) for k, (a, b) in enumerate(((hid_hbm, hid), (slope_hbm, slope)))]
        for n, at in enumerate(views)
    ]
    for copies in coming:
        for copy in copies:
            copy.start()
    for n, at in enumerate(views):
        for copy in coming[n]:
            copy.wait()
        part = dot(hid[at, :], slope[at, :], ((0,), (0,)))
        total[...] = part if n == 0 else total[...] + part
    half = mine_ref.shape[0]
    core = me_ref[0] % 2
    for out_ref, first in ((other_ref, (1 - core) * half), (mine_ref, core * half)):
        out_ref[...] = total[pl.ds(pl.multiple_of(first, half), half), :].astype(out_ref.dtype)


def partial_grad(keep, me, hidden, slope):
    owned, width = hidden.shape
    half = (width // 2, width)
    return pl.pallas_call(
        partial_kernel,
        in_specs=[SMEM, HBM, HBM],
        out_specs=[VMEM, VMEM],
        out_shape=[made(keep, half, F32), made(keep, half, BF16)],
        scratch_shapes=[
            pltpu.VMEM((owned, width), BF16),
            pltpu.VMEM((owned, width), BF16),
            pltpu.VMEM((width, width), F32),
            pltpu.SemaphoreType.DMA((2, owned // BIG)),
        ],
        compiler_params=params(20),
        name="partial_grad",
    )(me, *stored(hidden, slope))


def spread_kernel(adj_ref, grad_ref, out_ref):
    out_ref[...] = dot(adj_ref[...], grad_ref[...], ((0,), (0,)))


def spread(adjacency, grad, part, parts):
    owned, width = grad.shape
    blocks = owned // BIG // parts
    return pl.pallas_call(
        spread_kernel,
        grid=(blocks,),
        in_specs=[pl.BlockSpec((owned, BIG), lambda i: (0, i + part * blocks)), whole(grad.shape)],
        out_specs=pl.BlockSpec((BIG, width), lambda i: (i, 0)),
        out_shape=far_made((owned // parts, width), F32),
        compiler_params=params(60),
        cost_estimate=pl.CostEstimate(
            flops=2 * owned * owned * width, bytes_accessed=16 * 1024 * 1024, transcendentals=0
        ),
        name="spread",
    )(*stored(adjacency, grad))


def return_kernel(index_ref, first_hbm, second_hbm, got_ref, out_hbm, owned, out, sems, sent):
    blocks = sems.shape[0]
    views = [pl.ds(n * BIG, BIG) for n in range(blocks)]
    coming = []
    for n, at in enumerate(views):
        half_hbm = (first_hbm, second_hbm)[2 * n // blocks]
        coming.append(pltpu.make_async_copy(half_hbm.at[views[n % (blocks // 2)]], owned.at[at], sems.at[n]))
    for copy in coming:
        copy.start()

    shape = (128, index_ref.shape[1])
    high, low = digits(jnp.broadcast_to(index_ref[...], shape))
    row = lax.broadcasted_iota(jnp.int32, shape, 0).astype(F32).astype(BF16)
    hit = jnp.where(low == row, jnp.ones(shape, BF16), jnp.zeros(shape, BF16))

    def pick(n):
        tiles = [jnp.where(high == n * (BIG // 128) + t, hit, jnp.zeros(shape, BF16)) for t in range(BIG // 128)]
        return jnp.concatenate(tiles, axis=0)

    sending = []
    for n, at in enumerate(views):
        added = dot(pick(n), got_ref[...])
        coming[n].wait()
        out[at, :] = (owned[at, :] + added).astype(BF16)
        sending.append(pltpu.make_async_copy(out.at[at], out_hbm.at[at], sent.at[n]))
        sending[n].start()
    for copy in sending:
        copy.wait()


def give_back(keep, index, first, second, got):
    rows, width = 2 * first.shape[0], first.shape[1]
    (got,) = held(keep, got)
    return pl.pallas_call(
        return_kernel,
        in_specs=[VMEM, HBM, HBM, VMEM],
        out_specs=HBM,
        out_shape=far_made((rows, width), BF16),
        scratch_shapes=[
            pltpu.VMEM((rows, width), F32),
            pltpu.VMEM((rows, width), BF16),
            pltpu.SemaphoreType.DMA((rows // BIG,)),
            pltpu.SemaphoreType.DMA((rows // BIG,)),
        ],
        compiler_params=params(28 if keep else 60),
        name="give_back",
    )(index, *stored(first, second), got)


def exchange(x, axes):
    return lax.all_to_all(x, axes, split_axis=0, concat_axis=0, tiled=True)


def cut_kernel(me_ref, mine_ref, got_ref, *out_refs):
    height = mine_ref.shape[0] // len(out_refs)
    for k, out_ref in enumerate(out_refs):
        at = pl.ds(pl.multiple_of(((me_ref[0] // 2) ^ k) * height, height), height)
        out_ref[...] = (mine_ref[at, :] + got_ref[at, :].astype(F32)).astype(out_ref.dtype)


def cut(me, mine, got, chips):
    height, width = got.shape[0] // chips, got.shape[1]
    return pl.pallas_call(
        cut_kernel,
        in_specs=[SMEM, VMEM, VMEM],
        out_shape=[jax.ShapeDtypeStruct((height, width), F32 if k == 0 else BF16) for k in range(chips)],
        compiler_params=params(8),
        name="cut",
    )(me, mine, got)


def relay_kernel(after_ref, *refs):
    height = refs[0].shape[0]
    for k, ref in enumerate(refs[:-1]):
        refs[-1][k * height : (k + 1) * height, :] = ref[...]


def relay(after, pieces):
    height, width = pieces[0].shape
    return pl.pallas_call(
        relay_kernel,
        in_specs=[HBM] + [VMEM] * len(pieces),
        out_shape=jax.ShapeDtypeStruct((height * len(pieces), width), BF16),
        compiler_params=params(8),
        name="relay",
    )(*stored(after), *pieces)


def place_kernel(chips, other, me_ref, half_ref, *refs):
    out_hbm, placed, sem = refs[-3:]
    half = half_ref.shape[0]
    height = half // chips
    for k in range(chips):
        at = pl.multiple_of(((me_ref[0] // 2) ^ k) * height, height)
        placed[pl.ds(at, height), :] = half_ref[k * height : (k + 1) * height, :].astype(F32)
    at = pl.multiple_of((me_ref[0] + other) % 2 * half, half)
    copy = pltpu.make_async_copy(placed, out_hbm.at[pl.ds(at, half)], sem)
    copy.start()
    copy.wait()


def place(me, half, chips, into=()):
    return pl.pallas_call(
        functools.partial(place_kernel, chips, len(into)),
        in_specs=[SMEM, VMEM] + [HBM] * len(into),
        out_specs=HBM,
        out_shape=far_made((2 * half.shape[0], half.shape[1]), F32),
        scratch_shapes=[pltpu.VMEM(half.shape, F32), pltpu.SemaphoreType.DMA],
        input_output_aliases={2: 0} if into else {},
        compiler_params=params(8),
        name="place",
    )(me, half, *stored(*into))


def add_kernel(after_ref, *refs):
    parts = [ref[...].astype(F32) for ref in refs[:-1]]
    while len(parts) > 1:
        parts = [parts[k] + parts[k + 1] for k in range(0, len(parts), 2)]
    refs[-1][...] = parts[0].astype(BF16)


def add(after, parts):
    return pl.pallas_call(
        add_kernel,
        in_specs=[HBM] + [VMEM] * len(parts),
        out_shape=jax.ShapeDtypeStruct(parts[0].shape, BF16),
        compiler_params=params(8),
        name="add",
    )(*stored(after), *parts)


def swap(x, axis, size, k):
    return lax.ppermute(x, axis, [(i, i ^ k) for i in range(size)])


def per_device(groups, locals_, features, weight, cotangent, tile_vals, tile_rows, tile_cols, send_rows, counts):
    rows_own, width = features.shape
    lists = send_rows[0]
    peers, slots = lists.shape
    remote = peers * slots
    keep = remote <= rows_own
    me = lax.axis_index("local").astype(jnp.int32).reshape(1)
    outgoing = collect(counts, lists, features)
    arrived = exchange(outgoing.reshape(peers, slots, width), AXES).reshape(remote, width)
    adjacency, far, own = build(tile_rows, tile_cols, tile_vals, features, remote)
    activated, hidden, slope, grad, back = layer(keep, far, own, arrived, cotangent, weight)
    returned = exchange(back.reshape(peers, slots, width), AXES).reshape(remote, width)
    first = spread(adjacency, grad, 0, 2)
    second = spread(adjacency, grad, 1, 2)
    live = jnp.arange(slots)[None, :] < counts[0][:, None]
    feature_grad = give_back(keep, jnp.where(live, lists, -1).reshape(1, remote), first, second, returned)
    chips = locals_ // 2
    mine, other = partial_grad(keep, me, hidden, slope)
    pieces = cut(me, mine, swap(other, "local", locals_, 1), chips)
    piece = add(first, [pieces[0]] + [swap(pieces[k], "local", locals_, 2 * k) for k in range(1, chips)])
    step, after = 1, second
    while step < groups:
        piece = add(after, [piece, swap(piece, "group", groups, step)])
        step, after = 2 * step, second
    pieces = [piece] + [swap(piece, "local", locals_, 2 * k) for k in range(1, chips)]
    half = relay(feature_grad, pieces)
    weight_grad = place(me, swap(half, "local", locals_, 1), chips, [place(me, half, chips)])
    return activated, feature_grad, weight_grad


def solution(mesh):
    return jax.shard_map(
        functools.partial(per_device, mesh.shape["group"], mesh.shape["local"]),
        mesh=mesh,
        in_specs=(
            P(AXES, None),
            P(),
            P(AXES, None),
            P(AXES, None, None),
            P(AXES),
            P(AXES),
            P(AXES, None, None),
            P(AXES, None),
        ),
        out_specs=(P(AXES, None), P(AXES, None), P()),
        check_vma=False,
    )
```

```python
import functools

import jax
import jax.numpy as jnp
from jax import lax
from jax.experimental import pallas as pl
from jax.experimental.pallas import tpu as pltpu
from jax.sharding import PartitionSpec as P

AXES = ("group", "local")
BF16 = jnp.bfloat16
F32 = jnp.float32
ROWS = 256
BIG = 512
MIB = 1024 * 1024


def params(mib):
    return pltpu.CompilerParams(vmem_limit_bytes=mib * MIB)


VMEM = pl.BlockSpec(memory_space=pltpu.VMEM)
SMEM = pl.BlockSpec(memory_space=pltpu.SMEM)
HBM = pl.BlockSpec(memory_space=pltpu.MemorySpace.HBM)


def made(keep, shape, dtype):
    return pltpu.VMEM(shape, dtype) if keep else jax.ShapeDtypeStruct(shape, dtype)


def held(keep, *arrays):
    if not keep:
        return arrays
    return [pltpu.with_memory_space_constraint(x, pltpu.VMEM) for x in arrays]


def stored(*arrays):
    return [pltpu.with_memory_space_constraint(x, pltpu.MemorySpace.HBM) for x in arrays]


def far_made(shape, dtype):
    return pltpu.MemorySpace.HBM(shape, dtype)


def dot(a, b, contract=((1,), (0,))):
    return lax.dot_general(a, b, (contract, ((), ())), preferred_element_type=F32)


def whole(shape):
    return pl.BlockSpec(shape, lambda i, *unused: (0,) * len(shape))


def collect_kernel(counts_ref, lists_ref, x_ref, out_ref):
    dests, slots = lists_ref.shape
    step = BIG // slots
    lane = lax.broadcasted_iota(jnp.int32, (slots, x_ref.shape[0]), 1)
    slot = lax.broadcasted_iota(jnp.int32, (slots, 1), 0)
    turned = lists_ref[...].T
    for first in range(0, dests, step):
        parts = []
        for d in range(first, first + step):
            named = jnp.where(slot < counts_ref[0, d], turned[:, d : d + 1], -1)
            parts.append(jnp.where(named == lane, 1.0, 0.0).astype(BF16))
        pick = jnp.concatenate(parts, axis=0)
        out_ref[first * slots : (first + step) * slots, :] = dot(pick, x_ref[...]).astype(BF16)


def collect(counts, lists, x):
    dests, slots = lists.shape
    return pl.pallas_call(
        collect_kernel,
        in_specs=[SMEM, VMEM, VMEM],
        out_shape=jax.ShapeDtypeStruct((dests * slots, x.shape[1]), BF16),
        compiler_params=params(60),
        name="collect",
    )(counts, lists, x)


def build_kernel(rows_ref, cols_ref, tiles_ref, x_ref, adj_ref, far_ref, own_ref, total, order, starts, cursor):
    num_tiles, edge = tiles_ref.shape[0], tiles_ref.shape[1]
    per = ROWS // edge
    blocks = pl.num_programs(0)
    i = pl.program_id(0)

    @pl.when(i == 0)
    def _():
        def clear(b, unused):
            starts[b] = 0
            return unused

        lax.fori_loop(0, blocks + 1, clear, 0)

        def count(t, unused):
            k = rows_ref[t] // per + 1
            starts[k] = starts[k] + 1
            return unused

        lax.fori_loop(0, num_tiles, count, 0, unroll=4)

        def add(b, running):
            running = running + starts[b]
            starts[b] = running
            cursor[b] = running
            return running

        lax.fori_loop(0, blocks + 1, add, 0)

        def place(t, unused):
            k = rows_ref[t] // per
            at = cursor[k]
            cursor[k] = at + 1
            order[at] = t
            return unused

        lax.fori_loop(0, num_tiles, place, 0, unroll=4)

    total[...] = jnp.zeros_like(total)

    def one(j, unused):
        t = order[j]
        r = pl.multiple_of((rows_ref[t] % per) * edge, edge)
        c = pl.multiple_of(cols_ref[t] * edge, edge)
        at = (pl.ds(r, edge), pl.ds(c, edge))
        total[at] = total[at] + tiles_ref[t].astype(F32)
        return unused

    lax.fori_loop(starts[i], starts[i + 1], one, 0)
    owned = x_ref.shape[0]
    adj_ref[...] = total[:, :owned].astype(BF16)
    own_ref[...] = dot(adj_ref[...], x_ref[...])
    far_ref[...] = total[:, owned:].astype(BF16)


def build(tile_rows, tile_cols, tile_vals, x, remote):
    owned, width = x.shape
    num_tiles = tile_vals.shape[0]
    blocks = owned // ROWS
    return pl.pallas_call(
        build_kernel,
        grid_spec=pltpu.PrefetchScalarGridSpec(
            num_scalar_prefetch=2,
            grid=(blocks,),
            in_specs=[whole(tile_vals.shape), whole(x.shape)],
            out_specs=[
                pl.BlockSpec((ROWS, owned), lambda i, *unused: (i, 0)),
                pl.BlockSpec((ROWS, remote), lambda i, *unused: (i, 0)),
                pl.BlockSpec((ROWS, width), lambda i, *unused: (i, 0)),
            ],
            scratch_shapes=[
                pltpu.VMEM((ROWS, owned + remote), F32),
                pltpu.SMEM((num_tiles,), jnp.int32),
                pltpu.SMEM((blocks + 1,), jnp.int32),
                pltpu.SMEM((blocks + 1,), jnp.int32),
            ],
        ),
        out_shape=[
            far_made((owned, owned), BF16),
            far_made((owned, remote), BF16),
            far_made((owned, width), F32),
        ],
        compiler_params=params(48),
        cost_estimate=pl.CostEstimate(
            flops=2 * owned * owned * width, bytes_accessed=40 * 1024 * 1024, transcendentals=0
        ),
        name="build",
    )(tile_rows, tile_cols, tile_vals, x)


def layer_kernel(
    far_hbm, own_hbm, cot_hbm, w_hbm, got_ref,
    act_hbm, hid_hbm, slope_hbm, grad_hbm, back_hbm,
    far, own, cot, act, hid, slope, grad, w, back, sems, sent, w_sem,
):
    blocks = sems.shape[1]
    views = [pl.ds(n * BIG, BIG) for n in range(blocks)]

    def fetch(n):
        pairs = ((far_hbm, far), (own_hbm, own), (cot_hbm, cot))
        copies = [pltpu.make_async_copy(a.at[views[n]], b.at[views[n]], sems.at[k, n]) for k, (a, b) in enumerate(pairs)]
        for copy in copies:
            copy.start()
        return copies

    sending = []

    def send(k, n, a, b, at):
        sending.append(pltpu.make_async_copy(a.at[at], b.at[at], sent.at[k, n]))
        sending[-1].start()

    coming = fetch(0)
    weight = pltpu.make_async_copy(w_hbm, w, w_sem)
    weight.start()
    for n, at in enumerate(views):
        copies = coming
        for copy in copies[:2]:
            copy.wait()
        if n + 1 < blocks:
            coming = fetch(n + 1)
        hid[at, :] = (own[at, :] + dot(far[at, :], got_ref[...])).astype(BF16)
        send(0, n, hid, hid_hbm, at)
        copies[2].wait()
        if n == 0:
            weight.wait()
        preact = dot(hid[at, :], w[...])
        gate = 0.5 + 0.5 * jnp.tanh(0.5 * preact)
        act[at, :] = (preact * gate).astype(BF16)
        send(1, n, act, act_hbm, at)
        slope[at, :] = (cot[at, :].astype(F32) * gate * (1.0 + preact * (1.0 - gate))).astype(BF16)
        send(2, n, slope, slope_hbm, at)
        grad[at, :] = dot(slope[at, :], w[...], ((1,), (1,))).astype(BF16)
        send(3, n, grad, grad_hbm, at)
    for n in range(back.shape[0] // BIG):
        at = pl.ds(n * BIG, BIG)
        back[at, :] = dot(far[:, at], grad[...], ((0,), (0,))).astype(BF16)
        send(4, n, back, back_hbm, at)
    for copy in sending:
        copy.wait()


def layer(keep, far, own, got, cotangent, weight):
    owned, width = own.shape
    remote = got.shape[0]
    blocks = owned // BIG
    (got,) = held(keep, got)
    rows = (owned, width)
    return pl.pallas_call(
        layer_kernel,
        in_specs=[HBM] * 4 + [VMEM],
        out_specs=[HBM] * 5,
        out_shape=[far_made(rows, BF16)] * 4 + [far_made(got.shape, BF16)],
        scratch_shapes=[pltpu.VMEM(far.shape, BF16), pltpu.VMEM(rows, F32)]
        + [pltpu.VMEM(rows, BF16)] * 5
        + [
            pltpu.VMEM(weight.shape, BF16),
            pltpu.VMEM(got.shape, BF16),
            pltpu.SemaphoreType.DMA((3, blocks)),
            pltpu.SemaphoreType.DMA((5, max(blocks, remote // BIG))),
            pltpu.SemaphoreType.DMA,
        ],
        compiler_params=params(40 if keep else 60),
        name="layer",
    )(*stored(far, own, cotangent, weight), got)


def partial_kernel(me_ref, hid_hbm, slope_hbm, mine_ref, other_ref, hid, slope, total, sems):
    blocks = sems.shape[1]
    views = [pl.ds(n * BIG, BIG) for n in range(blocks)]
    coming = [
        [pltpu.make_async_copy(a.at[at], b.at[at], sems.at[k, n]) for k, (a, b) in enumerate(((hid_hbm, hid), (slope_hbm, slope)))]
        for n, at in enumerate(views)
    ]
    for copies in coming:
        for copy in copies:
            copy.start()
    for n, at in enumerate(views):
        for copy in coming[n]:
            copy.wait()
        part = dot(hid[at, :], slope[at, :], ((0,), (0,)))
        total[...] = part if n == 0 else total[...] + part
    half = mine_ref.shape[0]
    core = me_ref[0] % 2
    for out_ref, first in ((other_ref, (1 - core) * half), (mine_ref, core * half)):
        out_ref[...] = total[pl.ds(pl.multiple_of(first, half), half), :].astype(out_ref.dtype)


def partial_grad(keep, me, hidden, slope):
    owned, width = hidden.shape
    half = (width // 2, width)
    return pl.pallas_call(
        partial_kernel,
        in_specs=[SMEM, HBM, HBM],
        out_specs=[VMEM, VMEM],
        out_shape=[made(keep, half, F32), made(keep, half, BF16)],
        scratch_shapes=[
            pltpu.VMEM((owned, width), BF16),
            pltpu.VMEM((owned, width), BF16),
            pltpu.VMEM((width, width), F32),
            pltpu.SemaphoreType.DMA((2, owned // BIG)),
        ],
        compiler_params=params(20),
        name="partial_grad",
    )(me, *stored(hidden, slope))


def spread_kernel(adj_ref, grad_ref, out_ref):
    out_ref[...] = dot(adj_ref[...], grad_ref[...], ((0,), (0,)))


def spread(adjacency, grad, part, parts):
    owned, width = grad.shape
    blocks = owned // BIG // parts
    return pl.pallas_call(
        spread_kernel,
        grid=(blocks,),
        in_specs=[pl.BlockSpec((owned, BIG), lambda i: (0, i + part * blocks)), whole(grad.shape)],
        out_specs=pl.BlockSpec((BIG, width), lambda i: (i, 0)),
        out_shape=far_made((owned // parts, width), F32),
        compiler_params=params(60),
        cost_estimate=pl.CostEstimate(
            flops=2 * owned * owned * width, bytes_accessed=16 * 1024 * 1024, transcendentals=0
        ),
        name="spread",
    )(*stored(adjacency, grad))


def return_kernel(part, index_ref, owned_hbm, got_ref, *refs):
    out_hbm, owned, out, sems, sent = refs[-5:]
    views = [pl.ds(n * BIG, BIG) for n in range(sems.shape[0])]
    coming = [pltpu.make_async_copy(owned_hbm.at[at], owned.at[at], sems.at[n]) for n, at in enumerate(views)]
    for copy in coming:
        copy.start()
    base = part * owned.shape[0]

    def pick(n):
        row = lax.broadcasted_iota(jnp.int32, (BIG, index_ref.shape[1]), 0) + (base + n * BIG)
        return jnp.where(row == index_ref[...], 1.0, 0.0).astype(BF16)

    sending = []
    for n, at in enumerate(views):
        added = dot(pick(n), got_ref[...])
        coming[n].wait()
        out[at, :] = (owned[at, :] + added).astype(BF16)
        sending.append(pltpu.make_async_copy(out.at[at], out_hbm.at[pl.ds(base + n * BIG, BIG)], sent.at[n]))
        sending[n].start()
    for copy in sending:
        copy.wait()


def give_back(keep, index, owned, got, part, parts, into=()):
    rows, width = owned.shape
    (got,) = held(keep, got)
    return pl.pallas_call(
        functools.partial(return_kernel, part),
        in_specs=[VMEM, HBM, VMEM] + [HBM] * len(into[:1]) + [VMEM] * len(into[1:]),
        out_specs=HBM,
        out_shape=far_made((parts * rows, width), BF16),
        scratch_shapes=[
            pltpu.VMEM((rows, width), F32),
            pltpu.VMEM((rows, width), BF16),
            pltpu.SemaphoreType.DMA((rows // BIG,)),
            pltpu.SemaphoreType.DMA((rows // BIG,)),
        ],
        input_output_aliases={3: 0} if into else {},
        compiler_params=params(28 if keep else 60),
        name="give_back",
    )(index, *stored(owned), got, *stored(*into[:1]), *into[1:])


def exchange(x, axes):
    return lax.all_to_all(x, axes, split_axis=0, concat_axis=0, tiled=True)


def cut_kernel(me_ref, mine_ref, got_ref, *out_refs):
    height = mine_ref.shape[0] // len(out_refs)
    for k, out_ref in enumerate(out_refs):
        at = pl.ds(pl.multiple_of(((me_ref[0] // 2) ^ k) * height, height), height)
        out_ref[...] = (mine_ref[at, :] + got_ref[at, :].astype(F32)).astype(out_ref.dtype)


def cut(me, mine, got, chips):
    height, width = got.shape[0] // chips, got.shape[1]
    return pl.pallas_call(
        cut_kernel,
        in_specs=[SMEM, VMEM, VMEM],
        out_shape=[jax.ShapeDtypeStruct((height, width), F32 if k == 0 else BF16) for k in range(chips)],
        compiler_params=params(8),
        name="cut",
    )(me, mine, got)


def relay_kernel(after_ref, *refs):
    height = refs[0].shape[0]
    for k, ref in enumerate(refs[:-1]):
        refs[-1][k * height : (k + 1) * height, :] = ref[...]


def relay(after, pieces):
    height, width = pieces[0].shape
    return pl.pallas_call(
        relay_kernel,
        in_specs=[HBM] + [VMEM] * len(pieces),
        out_shape=jax.ShapeDtypeStruct((height * len(pieces), width), BF16),
        compiler_params=params(8),
        name="relay",
    )(*stored(after), *pieces)


def place_kernel(chips, other, me_ref, half_ref, *refs):
    out_hbm, placed, sem = refs[-3:]
    half = half_ref.shape[0]
    height = half // chips
    for k in range(chips):
        at = pl.multiple_of(((me_ref[0] // 2) ^ k) * height, height)
        placed[pl.ds(at, height), :] = half_ref[k * height : (k + 1) * height, :].astype(F32)
    at = pl.multiple_of((me_ref[0] + other) % 2 * half, half)
    copy = pltpu.make_async_copy(placed, out_hbm.at[pl.ds(at, half)], sem)
    copy.start()
    copy.wait()


def place(me, half, chips, into=()):
    return pl.pallas_call(
        functools.partial(place_kernel, chips, len(into)),
        in_specs=[SMEM, VMEM] + [HBM] * len(into),
        out_specs=HBM,
        out_shape=far_made((2 * half.shape[0], half.shape[1]), F32),
        scratch_shapes=[pltpu.VMEM(half.shape, F32), pltpu.SemaphoreType.DMA],
        input_output_aliases={2: 0} if into else {},
        compiler_params=params(8),
        name="place",
    )(me, half, *stored(*into))


def add_kernel(after_ref, *refs):
    parts = [ref[...].astype(F32) for ref in refs[:-1]]
    while len(parts) > 1:
        parts = [parts[k] + parts[k + 1] for k in range(0, len(parts), 2)]
    refs[-1][...] = parts[0].astype(BF16)


def add(after, parts):
    return pl.pallas_call(
        add_kernel,
        in_specs=[HBM] + [VMEM] * len(parts),
        out_shape=jax.ShapeDtypeStruct(parts[0].shape, BF16),
        compiler_params=params(8),
        name="add",
    )(*stored(after), *parts)


def swap(x, axis, size, k):
    return lax.ppermute(x, axis, [(i, i ^ k) for i in range(size)])


def per_device(groups, locals_, features, weight, cotangent, tile_vals, tile_rows, tile_cols, send_rows, counts):
    rows_own, width = features.shape
    lists = send_rows[0]
    peers, slots = lists.shape
    remote = peers * slots
    keep = remote <= rows_own
    me = lax.axis_index("local").astype(jnp.int32).reshape(1)
    outgoing = collect(counts, lists, features)
    arrived = exchange(outgoing.reshape(peers, slots, width), AXES).reshape(remote, width)
    adjacency, far, own = build(tile_rows, tile_cols, tile_vals, features, remote)
    activated, hidden, slope, grad, back = layer(keep, far, own, arrived, cotangent, weight)
    returned = exchange(back.reshape(peers, slots, width), AXES).reshape(remote, width)
    first = spread(adjacency, grad, 0, 2)
    second = spread(adjacency, grad, 1, 2)
    live = jnp.arange(slots)[None, :] < counts[0][:, None]
    index = jnp.where(live, lists, -1).reshape(1, remote)
    feature_grad = give_back(keep, index, first, returned, 0, 2)
    chips = locals_ // 2
    mine, other = partial_grad(keep, me, hidden, slope)
    pieces = cut(me, mine, swap(other, "local", locals_, 1), chips)
    piece = add(first, [pieces[0]] + [swap(pieces[k], "local", locals_, 2 * k) for k in range(1, chips)])
    step, after = 1, second
    while step < groups:
        piece = add(after, [piece, swap(piece, "group", groups, step)])
        step, after = 2 * step, feature_grad
    pieces = [piece] + [swap(piece, "local", locals_, 2 * k) for k in range(1, chips)]
    feature_grad = give_back(keep, index, second, returned, 1, 2, [feature_grad, piece])
    half = relay(feature_grad, pieces)
    weight_grad = place(me, swap(half, "local", locals_, 1), chips, [place(me, half, chips)])
    return activated, feature_grad, weight_grad


def solution(mesh):
    return jax.shard_map(
        functools.partial(per_device, mesh.shape["group"], mesh.shape["local"]),
        mesh=mesh,
        in_specs=(
            P(AXES, None),
            P(),
            P(AXES, None),
            P(AXES, None, None),
            P(AXES),
            P(AXES),
            P(AXES, None, None),
            P(AXES, None),
        ),
        out_specs=(P(AXES, None), P(AXES, None), P()),
        check_vma=False,
    )
```

```python
import functools

import jax
import jax.numpy as jnp
from jax import lax
from jax.experimental import pallas as pl
from jax.experimental.pallas import tpu as pltpu
from jax.sharding import PartitionSpec as P

AXES = ("group", "local")
BF16 = jnp.bfloat16
F32 = jnp.float32
ROWS = 256
BIG = 512
MIB = 1024 * 1024


def params(mib):
    return pltpu.CompilerParams(vmem_limit_bytes=mib * MIB)


VMEM = pl.BlockSpec(memory_space=pltpu.VMEM)
SMEM = pl.BlockSpec(memory_space=pltpu.SMEM)
HBM = pl.BlockSpec(memory_space=pltpu.MemorySpace.HBM)


def made(keep, shape, dtype):
    return pltpu.VMEM(shape, dtype) if keep else jax.ShapeDtypeStruct(shape, dtype)


def held(keep, *arrays):
    if not keep:
        return arrays
    return [pltpu.with_memory_space_constraint(x, pltpu.VMEM) for x in arrays]


def stored(*arrays):
    return [pltpu.with_memory_space_constraint(x, pltpu.MemorySpace.HBM) for x in arrays]


def far_made(shape, dtype):
    return pltpu.MemorySpace.HBM(shape, dtype)


def dot(a, b, contract=((1,), (0,))):
    return lax.dot_general(a, b, (contract, ((), ())), preferred_element_type=F32)


def whole(shape):
    return pl.BlockSpec(shape, lambda i, *unused: (0,) * len(shape))


def collect_kernel(counts_ref, lists_ref, x_ref, out_ref):
    dests, slots = lists_ref.shape
    step = BIG // slots
    lane = lax.broadcasted_iota(jnp.int32, (slots, x_ref.shape[0]), 1)
    slot = lax.broadcasted_iota(jnp.int32, (slots, 1), 0)
    turned = lists_ref[...].T
    for first in range(0, dests, step):
        parts = []
        for d in range(first, first + step):
            named = jnp.where(slot < counts_ref[0, d], turned[:, d : d + 1], -1)
            parts.append(jnp.where(named == lane, 1.0, 0.0).astype(BF16))
        pick = jnp.concatenate(parts, axis=0)
        out_ref[first * slots : (first + step) * slots, :] = dot(pick, x_ref[...]).astype(BF16)


def collect(counts, lists, x):
    dests, slots = lists.shape
    return pl.pallas_call(
        collect_kernel,
        in_specs=[SMEM, VMEM, VMEM],
        out_shape=jax.ShapeDtypeStruct((dests * slots, x.shape[1]), BF16),
        compiler_params=params(60),
        name="collect",
    )(counts, lists, x)


def build_kernel(rows_ref, cols_ref, tiles_ref, x_ref, adj_ref, far_ref, own_ref, head_ref, total, order, starts, cursor):
    num_tiles, edge = tiles_ref.shape[0], tiles_ref.shape[1]
    per = ROWS // edge
    blocks = pl.num_programs(0)
    i = pl.program_id(0)

    @pl.when(i == 0)
    def _():
        def clear(b, unused):
            starts[b] = 0
            return unused

        lax.fori_loop(0, blocks + 1, clear, 0)

        def count(t, unused):
            k = rows_ref[t] // per + 1
            starts[k] = starts[k] + 1
            return unused

        lax.fori_loop(0, num_tiles, count, 0, unroll=4)

        def add(b, running):
            running = running + starts[b]
            starts[b] = running
            cursor[b] = running
            return running

        lax.fori_loop(0, blocks + 1, add, 0)

        def place(t, unused):
            k = rows_ref[t] // per
            at = cursor[k]
            cursor[k] = at + 1
            order[at] = t
            return unused

        lax.fori_loop(0, num_tiles, place, 0, unroll=4)

    total[...] = jnp.zeros_like(total)

    def one(j, unused):
        t = order[j]
        r = pl.multiple_of((rows_ref[t] % per) * edge, edge)
        c = pl.multiple_of(cols_ref[t] * edge, edge)
        at = (pl.ds(r, edge), pl.ds(c, edge))
        total[at] = total[at] + tiles_ref[t].astype(F32)
        return unused

    lax.fori_loop(starts[i], starts[i + 1], one, 0)
    owned = x_ref.shape[0]
    adj_ref[...] = total[:, :owned].astype(BF16)
    own_ref[...] = dot(adj_ref[...], x_ref[...])
    far_ref[...] = total[:, owned:].astype(BF16)

    @pl.when(i < head_ref.shape[0] // ROWS)
    def _():
        head_ref[pl.ds(pl.multiple_of(i * ROWS, ROWS), ROWS), :] = far_ref[...]


def build(tile_rows, tile_cols, tile_vals, x, remote):
    owned, width = x.shape
    num_tiles = tile_vals.shape[0]
    blocks = owned // ROWS
    return pl.pallas_call(
        build_kernel,
        grid_spec=pltpu.PrefetchScalarGridSpec(
            num_scalar_prefetch=2,
            grid=(blocks,),
            in_specs=[whole(tile_vals.shape), whole(x.shape)],
            out_specs=[
                pl.BlockSpec((ROWS, owned), lambda i, *unused: (i, 0)),
                pl.BlockSpec((ROWS, remote), lambda i, *unused: (i, 0)),
                pl.BlockSpec((ROWS, width), lambda i, *unused: (i, 0)),
                whole((BIG, remote)),
            ],
            scratch_shapes=[
                pltpu.VMEM((ROWS, owned + remote), F32),
                pltpu.SMEM((num_tiles,), jnp.int32),
                pltpu.SMEM((blocks + 1,), jnp.int32),
                pltpu.SMEM((blocks + 1,), jnp.int32),
            ],
        ),
        out_shape=[
            far_made((owned, owned), BF16),
            far_made((owned, remote), BF16),
            far_made((owned, width), F32),
            far_made((BIG, remote), BF16),
        ],
        compiler_params=params(48),
        cost_estimate=pl.CostEstimate(
            flops=2 * owned * owned * width, bytes_accessed=40 * 1024 * 1024, transcendentals=0
        ),
        name="build",
    )(tile_rows, tile_cols, tile_vals, x)


def layer_kernel(
    far_hbm, own_hbm, cot_hbm, w_hbm, head_ref, got_ref,
    act_hbm, hid_hbm, slope_hbm, grad_hbm, back_hbm,
    far, own, cot, act, hid, slope, grad, w, back, sems, sent, w_sem,
):
    blocks = sems.shape[1]
    views = [pl.ds(n * BIG, BIG) for n in range(blocks)]

    def fetch(n):
        pairs = ((far_hbm, far), (own_hbm, own), (cot_hbm, cot))
        copies = [pltpu.make_async_copy(a.at[views[n]], b.at[views[n]], sems.at[k, n]) for k, (a, b) in enumerate(pairs)]
        for copy in copies:
            copy.start()
        return copies

    sending = []

    def send(k, n, a, b, at):
        sending.append(pltpu.make_async_copy(a.at[at], b.at[at], sent.at[k, n]))
        sending[-1].start()

    coming = fetch(0)
    weight = pltpu.make_async_copy(w_hbm, w, w_sem)
    weight.start()
    for n, at in enumerate(views):
        copies = coming
        if n == 0:
            summed = dot(head_ref[...], got_ref[...])
        else:
            copies[0].wait()
            summed = dot(far[at, :], got_ref[...])
        copies[1].wait()
        if n + 1 < blocks:
            coming = fetch(n + 1)
        hid[at, :] = (own[at, :] + summed).astype(BF16)
        send(0, n, hid, hid_hbm, at)
        copies[2].wait()
        if n == 0:
            weight.wait()
            copies[0].wait()
        preact = dot(hid[at, :], w[...])
        gate = 0.5 + 0.5 * jnp.tanh(0.5 * preact)
        act[at, :] = (preact * gate).astype(BF16)
        send(1, n, act, act_hbm, at)
        slope[at, :] = (cot[at, :].astype(F32) * gate * (1.0 + preact * (1.0 - gate))).astype(BF16)
        send(2, n, slope, slope_hbm, at)
        grad[at, :] = dot(slope[at, :], w[...], ((1,), (1,))).astype(BF16)
        send(3, n, grad, grad_hbm, at)
    for n in range(back.shape[0] // BIG):
        at = pl.ds(n * BIG, BIG)
        back[at, :] = dot(far[:, at], grad[...], ((0,), (0,))).astype(BF16)
        send(4, n, back, back_hbm, at)
    for copy in sending:
        copy.wait()


def layer(keep, far, own, head, got, cotangent, weight):
    owned, width = own.shape
    remote = got.shape[0]
    blocks = owned // BIG
    head, got = held(keep, head, got)
    rows = (owned, width)
    return pl.pallas_call(
        layer_kernel,
        in_specs=[HBM] * 4 + [VMEM] * 2,
        out_specs=[HBM] * 5,
        out_shape=[far_made(rows, BF16)] * 4 + [far_made(got.shape, BF16)],
        scratch_shapes=[pltpu.VMEM(far.shape, BF16), pltpu.VMEM(rows, F32)]
        + [pltpu.VMEM(rows, BF16)] * 5
        + [
            pltpu.VMEM(weight.shape, BF16),
            pltpu.VMEM(got.shape, BF16),
            pltpu.SemaphoreType.DMA((3, blocks)),
            pltpu.SemaphoreType.DMA((5, max(blocks, remote // BIG))),
            pltpu.SemaphoreType.DMA,
        ],
        compiler_params=params(40 if keep else 60),
        name="layer",
    )(*stored(far, own, cotangent, weight), head, got)


def partial_kernel(me_ref, hid_hbm, slope_hbm, mine_ref, other_ref, hid, slope, total, sems):
    blocks = sems.shape[1]
    views = [pl.ds(n * BIG, BIG) for n in range(blocks)]
    coming = [
        [pltpu.make_async_copy(a.at[at], b.at[at], sems.at[k, n]) for k, (a, b) in enumerate(((hid_hbm, hid), (slope_hbm, slope)))]
        for n, at in enumerate(views)
    ]
    for copies in coming:
        for copy in copies:
            copy.start()
    for n, at in enumerate(views):
        for copy in coming[n]:
            copy.wait()
        part = dot(hid[at, :], slope[at, :], ((0,), (0,)))
        total[...] = part if n == 0 else total[...] + part
    half = mine_ref.shape[0]
    core = me_ref[0] % 2
    for out_ref, first in ((other_ref, (1 - core) * half), (mine_ref, core * half)):
        out_ref[...] = total[pl.ds(pl.multiple_of(first, half), half), :].astype(out_ref.dtype)


def partial_grad(keep, me, hidden, slope):
    owned, width = hidden.shape
    half = (width // 2, width)
    return pl.pallas_call(
        partial_kernel,
        in_specs=[SMEM, HBM, HBM],
        out_specs=[VMEM, VMEM],
        out_shape=[made(keep, half, F32), made(keep, half, BF16)],
        scratch_shapes=[
            pltpu.VMEM((owned, width), BF16),
            pltpu.VMEM((owned, width), BF16),
            pltpu.VMEM((width, width), F32),
            pltpu.SemaphoreType.DMA((2, owned // BIG)),
        ],
        compiler_params=params(20),
        name="partial_grad",
    )(me, *stored(hidden, slope))


def spread_kernel(adj_ref, grad_ref, out_ref):
    out_ref[...] = dot(adj_ref[...], grad_ref[...], ((0,), (0,)))


def spread(adjacency, grad, part, parts):
    owned, width = grad.shape
    blocks = owned // BIG // parts
    return pl.pallas_call(
        spread_kernel,
        grid=(blocks,),
        in_specs=[pl.BlockSpec((owned, BIG), lambda i: (0, i + part * blocks)), whole(grad.shape)],
        out_specs=pl.BlockSpec((BIG, width), lambda i: (i, 0)),
        out_shape=far_made((owned // parts, width), F32),
        compiler_params=params(60),
        cost_estimate=pl.CostEstimate(
            flops=2 * owned * owned * width, bytes_accessed=16 * 1024 * 1024, transcendentals=0
        ),
        name="spread",
    )(*stored(adjacency, grad))


def return_kernel(index_ref, first_hbm, second_hbm, got_ref, out_hbm, owned, out, sems, sent):
    blocks = sems.shape[0]
    views = [pl.ds(n * BIG, BIG) for n in range(blocks)]
    coming = []
    for n, at in enumerate(views):
        half_hbm = (first_hbm, second_hbm)[2 * n // blocks]
        coming.append(pltpu.make_async_copy(half_hbm.at[views[n % (blocks // 2)]], owned.at[at], sems.at[n]))
    coming[0].start()
    coming[1].start()

    def pick(n):
        row = lax.broadcasted_iota(jnp.int32, (BIG, index_ref.shape[1]), 0) + n * BIG
        return jnp.where(row == index_ref[...], 1.0, 0.0).astype(BF16)

    sending = []
    for n, at in enumerate(views):
        added = dot(pick(n), got_ref[...])
        coming[n].wait()
        if n + 2 < blocks:
            coming[n + 2].start()
        out[at, :] = (owned[at, :] + added).astype(BF16)
        sending.append(pltpu.make_async_copy(out.at[at], out_hbm.at[at], sent.at[n]))
        sending[n].start()
    for copy in sending:
        copy.wait()


def give_back(keep, index, first, second, got):
    rows, width = 2 * first.shape[0], first.shape[1]
    (got,) = held(keep, got)
    return pl.pallas_call(
        return_kernel,
        in_specs=[VMEM, HBM, HBM, VMEM],
        out_specs=HBM,
        out_shape=far_made((rows, width), BF16),
        scratch_shapes=[
            pltpu.VMEM((rows, width), F32),
            pltpu.VMEM((rows, width), BF16),
            pltpu.SemaphoreType.DMA((rows // BIG,)),
            pltpu.SemaphoreType.DMA((rows // BIG,)),
        ],
        compiler_params=params(28 if keep else 60),
        name="give_back",
    )(index, *stored(first, second), got)


def exchange(x, axes):
    return lax.all_to_all(x, axes, split_axis=0, concat_axis=0, tiled=True)


def cut_kernel(me_ref, mine_ref, got_ref, *out_refs):
    height = mine_ref.shape[0] // len(out_refs)
    for k, out_ref in enumerate(out_refs):
        at = pl.ds(pl.multiple_of(((me_ref[0] // 2) ^ k) * height, height), height)
        out_ref[...] = (mine_ref[at, :] + got_ref[at, :].astype(F32)).astype(out_ref.dtype)


def cut(me, mine, got, chips):
    height, width = got.shape[0] // chips, got.shape[1]
    return pl.pallas_call(
        cut_kernel,
        in_specs=[SMEM, VMEM, VMEM],
        out_shape=[jax.ShapeDtypeStruct((height, width), F32 if k == 0 else BF16) for k in range(chips)],
        compiler_params=params(8),
        name="cut",
    )(me, mine, got)


def relay_kernel(after_ref, *refs):
    height = refs[0].shape[0]
    for k, ref in enumerate(refs[:-1]):
        refs[-1][k * height : (k + 1) * height, :] = ref[...]


def relay(after, pieces):
    height, width = pieces[0].shape
    return pl.pallas_call(
        relay_kernel,
        in_specs=[HBM] + [VMEM] * len(pieces),
        out_shape=jax.ShapeDtypeStruct((height * len(pieces), width), BF16),
        compiler_params=params(8),
        name="relay",
    )(*stored(after), *pieces)


def place_kernel(chips, other, me_ref, half_ref, *refs):
    out_hbm, placed, sem = refs[-3:]
    half = half_ref.shape[0]
    height = half // chips
    for k in range(chips):
        at = pl.multiple_of(((me_ref[0] // 2) ^ k) * height, height)
        placed[pl.ds(at, height), :] = half_ref[k * height : (k + 1) * height, :].astype(F32)
    at = pl.multiple_of((me_ref[0] + other) % 2 * half, half)
    copy = pltpu.make_async_copy(placed, out_hbm.at[pl.ds(at, half)], sem)
    copy.start()
    copy.wait()


def place(me, half, chips, into=()):
    return pl.pallas_call(
        functools.partial(place_kernel, chips, len(into)),
        in_specs=[SMEM, VMEM] + [HBM] * len(into),
        out_specs=HBM,
        out_shape=far_made((2 * half.shape[0], half.shape[1]), F32),
        scratch_shapes=[pltpu.VMEM(half.shape, F32), pltpu.SemaphoreType.DMA],
        input_output_aliases={2: 0} if into else {},
        compiler_params=params(8),
        name="place",
    )(me, half, *stored(*into))


def add_kernel(after_ref, *refs):
    parts = [ref[...].astype(F32) for ref in refs[:-1]]
    while len(parts) > 1:
        parts = [parts[k] + parts[k + 1] for k in range(0, len(parts), 2)]
    refs[-1][...] = parts[0].astype(BF16)


def add(after, parts):
    return pl.pallas_call(
        add_kernel,
        in_specs=[HBM] + [VMEM] * len(parts),
        out_shape=jax.ShapeDtypeStruct(parts[0].shape, BF16),
        compiler_params=params(8),
        name="add",
    )(*stored(after), *parts)


def swap(x, axis, size, k):
    return lax.ppermute(x, axis, [(i, i ^ k) for i in range(size)])


def per_device(groups, locals_, features, weight, cotangent, tile_vals, tile_rows, tile_cols, send_rows, counts):
    rows_own, width = features.shape
    lists = send_rows[0]
    peers, slots = lists.shape
    remote = peers * slots
    keep = remote <= rows_own
    me = lax.axis_index("local").astype(jnp.int32).reshape(1)
    outgoing = collect(counts, lists, features)
    arrived = exchange(outgoing.reshape(peers, slots, width), AXES).reshape(remote, width)
    adjacency, far, own, head = build(tile_rows, tile_cols, tile_vals, features, remote)
    activated, hidden, slope, grad, back = layer(keep, far, own, head, arrived, cotangent, weight)
    returned = exchange(back.reshape(peers, slots, width), AXES).reshape(remote, width)
    first = spread(adjacency, grad, 0, 2)
    second = spread(adjacency, grad, 1, 2)
    live = jnp.arange(slots)[None, :] < counts[0][:, None]
    feature_grad = give_back(keep, jnp.where(live, lists, -1).reshape(1, remote), first, second, returned)
    chips = locals_ // 2
    mine, other = partial_grad(keep, me, hidden, slope)
    pieces = cut(me, mine, swap(other, "local", locals_, 1), chips)
    piece = add(first, [pieces[0]] + [swap(pieces[k], "local", locals_, 2 * k) for k in range(1, chips)])
    step, after = 1, second
    while step < groups:
        piece = add(after, [piece, swap(piece, "group", groups, step)])
        step, after = 2 * step, second
    pieces = [piece] + [swap(piece, "local", locals_, 2 * k) for k in range(1, chips)]
    half = relay(feature_grad, pieces)
    weight_grad = place(me, swap(half, "local", locals_, 1), chips, [place(me, half, chips)])
    return activated, feature_grad, weight_grad


def solution(mesh):
    return jax.shard_map(
        functools.partial(per_device, mesh.shape["group"], mesh.shape["local"]),
        mesh=mesh,
        in_specs=(
            P(AXES, None),
            P(),
            P(AXES, None),
            P(AXES, None, None),
            P(AXES),
            P(AXES),
            P(AXES, None, None),
            P(AXES, None),
        ),
        out_specs=(P(AXES, None), P(AXES, None), P()),
        check_vma=False,
    )
```

```python
import functools

import jax
import jax.numpy as jnp
from jax import lax
from jax.experimental import pallas as pl
from jax.experimental.pallas import tpu as pltpu
from jax.sharding import PartitionSpec as P

AXES = ("group", "local")
BF16 = jnp.bfloat16
F32 = jnp.float32
ROWS = 256
BIG = 512
MIB = 1024 * 1024


def params(mib):
    return pltpu.CompilerParams(vmem_limit_bytes=mib * MIB)


VMEM = pl.BlockSpec(memory_space=pltpu.VMEM)
SMEM = pl.BlockSpec(memory_space=pltpu.SMEM)
HBM = pl.BlockSpec(memory_space=pltpu.MemorySpace.HBM)


def made(keep, shape, dtype):
    return pltpu.VMEM(shape, dtype) if keep else jax.ShapeDtypeStruct(shape, dtype)


def held(keep, *arrays):
    if not keep:
        return arrays
    return [pltpu.with_memory_space_constraint(x, pltpu.VMEM) for x in arrays]


def stored(*arrays):
    return [pltpu.with_memory_space_constraint(x, pltpu.MemorySpace.HBM) for x in arrays]


def far_made(shape, dtype):
    return pltpu.MemorySpace.HBM(shape, dtype)


def dot(a, b, contract=((1,), (0,))):
    return lax.dot_general(a, b, (contract, ((), ())), preferred_element_type=F32)


def whole(shape):
    return pl.BlockSpec(shape, lambda i, *unused: (0,) * len(shape))


def collect_kernel(counts_ref, lists_ref, x_ref, out_ref):
    dests, slots = lists_ref.shape
    step = BIG // slots
    lane = lax.broadcasted_iota(jnp.int32, (slots, x_ref.shape[0]), 1)
    slot = lax.broadcasted_iota(jnp.int32, (slots, 1), 0)
    turned = lists_ref[...].T
    for first in range(0, dests, step):
        parts = []
        for d in range(first, first + step):
            named = jnp.where(slot < counts_ref[0, d], turned[:, d : d + 1], -1)
            parts.append(jnp.where(named == lane, 1.0, 0.0).astype(BF16))
        pick = jnp.concatenate(parts, axis=0)
        out_ref[first * slots : (first + step) * slots, :] = dot(pick, x_ref[...]).astype(BF16)


def collect(counts, lists, x):
    dests, slots = lists.shape
    return pl.pallas_call(
        collect_kernel,
        in_specs=[SMEM, VMEM, VMEM],
        out_shape=jax.ShapeDtypeStruct((dests * slots, x.shape[1]), BF16),
        compiler_params=params(60),
        name="collect",
    )(counts, lists, x)


def build_kernel(rows_ref, cols_ref, tiles_ref, x_ref, adj_ref, far_ref, own_ref, total, order, starts, cursor):
    num_tiles, edge = tiles_ref.shape[0], tiles_ref.shape[1]
    per = ROWS // edge
    blocks = pl.num_programs(0)
    i = pl.program_id(0)

    @pl.when(i == 0)
    def _():
        def clear(b, unused):
            starts[b] = 0
            return unused

        lax.fori_loop(0, blocks + 1, clear, 0)

        def count(t, unused):
            k = rows_ref[t] // per + 1
            starts[k] = starts[k] + 1
            return unused

        lax.fori_loop(0, num_tiles, count, 0, unroll=4)

        def add(b, running):
            running = running + starts[b]
            starts[b] = running
            cursor[b] = running
            return running

        lax.fori_loop(0, blocks + 1, add, 0)

        def place(t, unused):
            k = rows_ref[t] // per
            at = cursor[k]
            cursor[k] = at + 1
            order[at] = t
            return unused

        lax.fori_loop(0, num_tiles, place, 0, unroll=4)

    total[...] = jnp.zeros_like(total)

    def one(j, unused):
        t = order[j]
        r = pl.multiple_of((rows_ref[t] % per) * edge, edge)
        c = pl.multiple_of(cols_ref[t] * edge, edge)
        at = (pl.ds(r, edge), pl.ds(c, edge))
        total[at] = total[at] + tiles_ref[t].astype(F32)
        return unused

    lax.fori_loop(starts[i], starts[i + 1], one, 0)
    owned = x_ref.shape[0]
    adj_ref[...] = total[:, :owned].astype(BF16)
    own_ref[...] = dot(adj_ref[...], x_ref[...])
    far_ref[...] = total[:, owned:].astype(BF16)


def build(tile_rows, tile_cols, tile_vals, x, remote):
    owned, width = x.shape
    num_tiles = tile_vals.shape[0]
    blocks = owned // ROWS
    return pl.pallas_call(
        build_kernel,
        grid_spec=pltpu.PrefetchScalarGridSpec(
            num_scalar_prefetch=2,
            grid=(blocks,),
            in_specs=[whole(tile_vals.shape), whole(x.shape)],
            out_specs=[
                pl.BlockSpec((ROWS, owned), lambda i, *unused: (i, 0)),
                pl.BlockSpec((ROWS, remote), lambda i, *unused: (i, 0)),
                pl.BlockSpec((ROWS, width), lambda i, *unused: (i, 0)),
            ],
            scratch_shapes=[
                pltpu.VMEM((ROWS, owned + remote), F32),
                pltpu.SMEM((num_tiles,), jnp.int32),
                pltpu.SMEM((blocks + 1,), jnp.int32),
                pltpu.SMEM((blocks + 1,), jnp.int32),
            ],
        ),
        out_shape=[
            far_made((owned, owned), BF16),
            far_made((owned, remote), BF16),
            far_made((owned, width), F32),
        ],
        compiler_params=params(48),
        cost_estimate=pl.CostEstimate(
            flops=2 * owned * owned * width, bytes_accessed=40 * 1024 * 1024, transcendentals=0
        ),
        name="build",
    )(tile_rows, tile_cols, tile_vals, x)


def layer_kernel(
    far_hbm, own_hbm, cot_hbm, w_hbm, got_ref,
    act_hbm, hid_hbm, slope_hbm, grad_hbm, back_hbm,
    far, own, cot, act, hid, slope, grad, w, back, sems, sent, w_sem,
):
    blocks = sems.shape[1]
    views = [pl.ds(n * BIG, BIG) for n in range(blocks)]

    def fetch(n):
        pairs = ((far_hbm, far), (own_hbm, own), (cot_hbm, cot))
        copies = [pltpu.make_async_copy(a.at[views[n]], b.at[views[n]], sems.at[k, n]) for k, (a, b) in enumerate(pairs)]
        for copy in copies:
            copy.start()
        return copies

    sending = []

    def send(k, n, a, b, at):
        sending.append(pltpu.make_async_copy(a.at[at], b.at[at], sent.at[k, n]))
        sending[-1].start()

    coming = [fetch(0)]
    weight = pltpu.make_async_copy(w_hbm, w, w_sem)
    weight.start()
    for n, at in enumerate(views):
        copies = coming[n]
        for copy in copies[:2]:
            copy.wait()
        while len(coming) < min(n + 3, blocks):
            coming.append(fetch(len(coming)))
        hid[at, :] = (own[at, :] + dot(far[at, :], got_ref[...])).astype(BF16)
        send(0, n, hid, hid_hbm, at)
        copies[2].wait()
        if n == 0:
            weight.wait()
        preact = dot(hid[at, :], w[...])
        gate = 0.5 + 0.5 * jnp.tanh(0.5 * preact)
        act[at, :] = (preact * gate).astype(BF16)
        send(1, n, act, act_hbm, at)
        slope[at, :] = (cot[at, :].astype(F32) * gate * (1.0 + preact * (1.0 - gate))).astype(BF16)
        send(2, n, slope, slope_hbm, at)
        grad[at, :] = dot(slope[at, :], w[...], ((1,), (1,))).astype(BF16)
        send(3, n, grad, grad_hbm, at)
    for n in range(back.shape[0] // BIG):
        at = pl.ds(n * BIG, BIG)
        back[at, :] = dot(far[:, at], grad[...], ((0,), (0,))).astype(BF16)
        send(4, n, back, back_hbm, at)
    for copy in sending:
        copy.wait()


def layer(keep, far, own, got, cotangent, weight):
    owned, width = own.shape
    remote = got.shape[0]
    blocks = owned // BIG
    (got,) = held(keep, got)
    rows = (owned, width)
    return pl.pallas_call(
        layer_kernel,
        in_specs=[HBM] * 4 + [VMEM],
        out_specs=[HBM] * 5,
        out_shape=[far_made(rows, BF16)] * 4 + [far_made(got.shape, BF16)],
        scratch_shapes=[pltpu.VMEM(far.shape, BF16), pltpu.VMEM(rows, F32)]
        + [pltpu.VMEM(rows, BF16)] * 5
        + [
            pltpu.VMEM(weight.shape, BF16),
            pltpu.VMEM(got.shape, BF16),
            pltpu.SemaphoreType.DMA((3, blocks)),
            pltpu.SemaphoreType.DMA((5, max(blocks, remote // BIG))),
            pltpu.SemaphoreType.DMA,
        ],
        compiler_params=params(40 if keep else 60),
        name="layer",
    )(*stored(far, own, cotangent, weight), got)


def partial_kernel(me_ref, hid_hbm, slope_hbm, mine_ref, other_ref, hid, slope, total, sems):
    blocks = sems.shape[1]
    views = [pl.ds(n * BIG, BIG) for n in range(blocks)]
    coming = [
        [pltpu.make_async_copy(a.at[at], b.at[at], sems.at[k, n]) for k, (a, b) in enumerate(((hid_hbm, hid), (slope_hbm, slope)))]
        for n, at in enumerate(views)
    ]
    for copies in coming:
        for copy in copies:
            copy.start()
    for n, at in enumerate(views):
        for copy in coming[n]:
            copy.wait()
        part = dot(hid[at, :], slope[at, :], ((0,), (0,)))
        total[...] = part if n == 0 else total[...] + part
    half = mine_ref.shape[0]
    core = me_ref[0] % 2
    for out_ref, first in ((other_ref, (1 - core) * half), (mine_ref, core * half)):
        out_ref[...] = total[pl.ds(pl.multiple_of(first, half), half), :].astype(out_ref.dtype)


def partial_grad(keep, me, hidden, slope):
    owned, width = hidden.shape
    half = (width // 2, width)
    return pl.pallas_call(
        partial_kernel,
        in_specs=[SMEM, HBM, HBM],
        out_specs=[VMEM, VMEM],
        out_shape=[made(keep, half, F32), made(keep, half, BF16)],
        scratch_shapes=[
            pltpu.VMEM((owned, width), BF16),
            pltpu.VMEM((owned, width), BF16),
            pltpu.VMEM((width, width), F32),
            pltpu.SemaphoreType.DMA((2, owned // BIG)),
        ],
        compiler_params=params(20),
        name="partial_grad",
    )(me, *stored(hidden, slope))


def spread_kernel(adj_ref, grad_ref, out_ref):
    out_ref[...] = dot(adj_ref[...], grad_ref[...], ((0,), (0,)))


def spread(adjacency, grad, part, parts):
    owned, width = grad.shape
    blocks = owned // BIG // parts
    return pl.pallas_call(
        spread_kernel,
        grid=(blocks,),
        in_specs=[pl.BlockSpec((owned, BIG), lambda i: (0, i + part * blocks)), whole(grad.shape)],
        out_specs=pl.BlockSpec((BIG, width), lambda i: (i, 0)),
        out_shape=far_made((owned // parts, width), F32),
        compiler_params=params(60),
        cost_estimate=pl.CostEstimate(
            flops=2 * owned * owned * width, bytes_accessed=16 * 1024 * 1024, transcendentals=0
        ),
        name="spread",
    )(*stored(adjacency, grad))


def return_kernel(index_ref, first_hbm, second_hbm, got_ref, out_hbm, owned, out, sems, sent):
    blocks = sems.shape[0]
    views = [pl.ds(n * BIG, BIG) for n in range(blocks)]
    coming = []
    for n, at in enumerate(views):
        half_hbm = (first_hbm, second_hbm)[2 * n // blocks]
        coming.append(pltpu.make_async_copy(half_hbm.at[views[n % (blocks // 2)]], owned.at[at], sems.at[n]))
    for copy in coming:
        copy.start()

    def pick(n):
        row = lax.broadcasted_iota(jnp.int32, (BIG, index_ref.shape[1]), 0) + n * BIG
        return jnp.where(row == index_ref[...], 1.0, 0.0).astype(BF16)

    sending = []
    for n, at in enumerate(views):
        added = dot(pick(n), got_ref[...])
        coming[n].wait()
        out[at, :] = (owned[at, :] + added).astype(BF16)
        sending.append(pltpu.make_async_copy(out.at[at], out_hbm.at[at], sent.at[n]))
        sending[n].start()
    for copy in sending:
        copy.wait()


def give_back(keep, index, first, second, got):
    rows, width = 2 * first.shape[0], first.shape[1]
    (got,) = held(keep, got)
    return pl.pallas_call(
        return_kernel,
        in_specs=[VMEM, HBM, HBM, VMEM],
        out_specs=HBM,
        out_shape=far_made((rows, width), BF16),
        scratch_shapes=[
            pltpu.VMEM((rows, width), F32),
            pltpu.VMEM((rows, width), BF16),
            pltpu.SemaphoreType.DMA((rows // BIG,)),
            pltpu.SemaphoreType.DMA((rows // BIG,)),
        ],
        compiler_params=params(28 if keep else 60),
        name="give_back",
    )(index, *stored(first, second), got)


def exchange(x, axes):
    return lax.all_to_all(x, axes, split_axis=0, concat_axis=0, tiled=True)


def cut_kernel(me_ref, mine_ref, got_ref, *out_refs):
    height = mine_ref.shape[0] // len(out_refs)
    for k, out_ref in enumerate(out_refs):
        at = pl.ds(pl.multiple_of(((me_ref[0] // 2) ^ k) * height, height), height)
        out_ref[...] = (mine_ref[at, :] + got_ref[at, :].astype(F32)).astype(out_ref.dtype)


def cut(me, mine, got, chips):
    height, width = got.shape[0] // chips, got.shape[1]
    return pl.pallas_call(
        cut_kernel,
        in_specs=[SMEM, VMEM, VMEM],
        out_shape=[jax.ShapeDtypeStruct((height, width), F32 if k == 0 else BF16) for k in range(chips)],
        compiler_params=params(8),
        name="cut",
    )(me, mine, got)


def relay_kernel(after_ref, *refs):
    height = refs[0].shape[0]
    for k, ref in enumerate(refs[:-1]):
        refs[-1][k * height : (k + 1) * height, :] = ref[...]


def relay(after, pieces):
    height, width = pieces[0].shape
    return pl.pallas_call(
        relay_kernel,
        in_specs=[HBM] + [VMEM] * len(pieces),
        out_shape=jax.ShapeDtypeStruct((height * len(pieces), width), BF16),
        compiler_params=params(8),
        name="relay",
    )(*stored(after), *pieces)


def place_kernel(chips, other, me_ref, half_ref, *refs):
    out_hbm, placed, sem = refs[-3:]
    half = half_ref.shape[0]
    height = half // chips
    for k in range(chips):
        at = pl.multiple_of(((me_ref[0] // 2) ^ k) * height, height)
        placed[pl.ds(at, height), :] = half_ref[k * height : (k + 1) * height, :].astype(F32)
    at = pl.multiple_of((me_ref[0] + other) % 2 * half, half)
    copy = pltpu.make_async_copy(placed, out_hbm.at[pl.ds(at, half)], sem)
    copy.start()
    copy.wait()


def place(me, half, chips, into=()):
    return pl.pallas_call(
        functools.partial(place_kernel, chips, len(into)),
        in_specs=[SMEM, VMEM] + [HBM] * len(into),
        out_specs=HBM,
        out_shape=far_made((2 * half.shape[0], half.shape[1]), F32),
        scratch_shapes=[pltpu.VMEM(half.shape, F32), pltpu.SemaphoreType.DMA],
        input_output_aliases={2: 0} if into else {},
        compiler_params=params(8),
        name="place",
    )(me, half, *stored(*into))


def add_kernel(after_ref, *refs):
    parts = [ref[...].astype(F32) for ref in refs[:-1]]
    while len(parts) > 1:
        parts = [parts[k] + parts[k + 1] for k in range(0, len(parts), 2)]
    refs[-1][...] = parts[0].astype(BF16)


def add(after, parts):
    return pl.pallas_call(
        add_kernel,
        in_specs=[HBM] + [VMEM] * len(parts),
        out_shape=jax.ShapeDtypeStruct(parts[0].shape, BF16),
        compiler_params=params(8),
        name="add",
    )(*stored(after), *parts)


def swap(x, axis, size, k):
    return lax.ppermute(x, axis, [(i, i ^ k) for i in range(size)])


def per_device(groups, locals_, features, weight, cotangent, tile_vals, tile_rows, tile_cols, send_rows, counts):
    rows_own, width = features.shape
    lists = send_rows[0]
    peers, slots = lists.shape
    remote = peers * slots
    keep = remote <= rows_own
    me = lax.axis_index("local").astype(jnp.int32).reshape(1)
    outgoing = collect(counts, lists, features)
    arrived = exchange(outgoing.reshape(peers, slots, width), AXES).reshape(remote, width)
    adjacency, far, own = build(tile_rows, tile_cols, tile_vals, features, remote)
    activated, hidden, slope, grad, back = layer(keep, far, own, arrived, cotangent, weight)
    returned = exchange(back.reshape(peers, slots, width), AXES).reshape(remote, width)
    first = spread(adjacency, grad, 0, 2)
    second = spread(adjacency, grad, 1, 2)
    live = jnp.arange(slots)[None, :] < counts[0][:, None]
    feature_grad = give_back(keep, jnp.where(live, lists, -1).reshape(1, remote), first, second, returned)
    chips = locals_ // 2
    mine, other = partial_grad(keep, me, hidden, slope)
    pieces = cut(me, mine, swap(other, "local", locals_, 1), chips)
    piece = add(first, [pieces[0]] + [swap(pieces[k], "local", locals_, 2 * k) for k in range(1, chips)])
    step, after = 1, second
    while step < groups:
        piece = add(after, [piece, swap(piece, "group", groups, step)])
        step, after = 2 * step, second
    pieces = [piece] + [swap(piece, "local", locals_, 2 * k) for k in range(1, chips)]
    half = relay(feature_grad, pieces)
    weight_grad = place(me, swap(half, "local", locals_, 1), chips, [place(me, half, chips)])
    return activated, feature_grad, weight_grad


def solution(mesh):
    return jax.shard_map(
        functools.partial(per_device, mesh.shape["group"], mesh.shape["local"]),
        mesh=mesh,
        in_specs=(
            P(AXES, None),
            P(),
            P(AXES, None),
            P(AXES, None, None),
            P(AXES),
            P(AXES),
            P(AXES, None, None),
            P(AXES, None),
        ),
        out_specs=(P(AXES, None), P(AXES, None), P()),
        check_vma=False,
    )
```

```python
import functools

import jax
import jax.numpy as jnp
from jax import lax
from jax.experimental import pallas as pl
from jax.experimental.pallas import tpu as pltpu
from jax.sharding import PartitionSpec as P

AXES = ("group", "local")
RANKS = ("local", "group")
BF16 = jnp.bfloat16
F32 = jnp.float32
ROWS = 256
BIG = 512
MIB = 1024 * 1024


def params(mib):
    return pltpu.CompilerParams(vmem_limit_bytes=mib * MIB)


VMEM = pl.BlockSpec(memory_space=pltpu.VMEM)
SMEM = pl.BlockSpec(memory_space=pltpu.SMEM)
HBM = pl.BlockSpec(memory_space=pltpu.MemorySpace.HBM)


def made(keep, shape, dtype):
    return pltpu.VMEM(shape, dtype) if keep else jax.ShapeDtypeStruct(shape, dtype)


def held(keep, *arrays):
    if not keep:
        return arrays
    return [pltpu.with_memory_space_constraint(x, pltpu.VMEM) for x in arrays]


def stored(*arrays):
    return [pltpu.with_memory_space_constraint(x, pltpu.MemorySpace.HBM) for x in arrays]


def far_made(shape, dtype):
    return pltpu.MemorySpace.HBM(shape, dtype)


def dot(a, b, contract=((1,), (0,))):
    return lax.dot_general(a, b, (contract, ((), ())), preferred_element_type=F32)


def whole(shape):
    return pl.BlockSpec(shape, lambda i, *unused: (0,) * len(shape))


def collect_kernel(order, counts_ref, lists_ref, x_ref, out_ref):
    dests, slots = lists_ref.shape
    step = BIG // slots
    lane = lax.broadcasted_iota(jnp.int32, (slots, x_ref.shape[0]), 1)
    slot = lax.broadcasted_iota(jnp.int32, (slots, 1), 0)
    turned = lists_ref[...].T
    for first in range(0, dests, step):
        parts = []
        for d in order[first : first + step]:
            named = jnp.where(slot < counts_ref[0, d], turned[:, d : d + 1], -1)
            parts.append(jnp.where(named == lane, 1.0, 0.0).astype(BF16))
        pick = jnp.concatenate(parts, axis=0)
        out_ref[first * slots : (first + step) * slots, :] = dot(pick, x_ref[...]).astype(BF16)


def collect(order, counts, lists, x):
    dests, slots = lists.shape
    return pl.pallas_call(
        functools.partial(collect_kernel, order),
        in_specs=[SMEM, VMEM, VMEM],
        out_shape=jax.ShapeDtypeStruct((dests * slots, x.shape[1]), BF16),
        compiler_params=params(60),
        name="collect",
    )(counts, lists, x)


def build_kernel(rows_ref, cols_ref, tiles_ref, x_ref, adj_ref, far_ref, own_ref, total, order, starts, cursor):
    num_tiles, edge = tiles_ref.shape[0], tiles_ref.shape[1]
    per = ROWS // edge
    blocks = pl.num_programs(0)
    i = pl.program_id(0)

    @pl.when(i == 0)
    def _():
        def clear(b, unused):
            starts[b] = 0
            return unused

        lax.fori_loop(0, blocks + 1, clear, 0)

        def count(t, unused):
            k = rows_ref[t] // per + 1
            starts[k] = starts[k] + 1
            return unused

        lax.fori_loop(0, num_tiles, count, 0, unroll=4)

        def add(b, running):
            running = running + starts[b]
            starts[b] = running
            cursor[b] = running
            return running

        lax.fori_loop(0, blocks + 1, add, 0)

        def place(t, unused):
            k = rows_ref[t] // per
            at = cursor[k]
            cursor[k] = at + 1
            order[at] = t
            return unused

        lax.fori_loop(0, num_tiles, place, 0, unroll=4)

    total[...] = jnp.zeros_like(total)

    def one(j, unused):
        t = order[j]
        r = pl.multiple_of((rows_ref[t] % per) * edge, edge)
        c = pl.multiple_of(cols_ref[t] * edge, edge)
        at = (pl.ds(r, edge), pl.ds(c, edge))
        total[at] = total[at] + tiles_ref[t].astype(F32)
        return unused

    lax.fori_loop(starts[i], starts[i + 1], one, 0)
    owned = x_ref.shape[0]
    adj_ref[...] = total[:, :owned].astype(BF16)
    own_ref[...] = dot(adj_ref[...], x_ref[...])
    far_ref[...] = total[:, owned:].astype(BF16)


def build(tile_rows, tile_cols, tile_vals, x, remote):
    owned, width = x.shape
    num_tiles = tile_vals.shape[0]
    blocks = owned // ROWS
    return pl.pallas_call(
        build_kernel,
        grid_spec=pltpu.PrefetchScalarGridSpec(
            num_scalar_prefetch=2,
            grid=(blocks,),
            in_specs=[whole(tile_vals.shape), whole(x.shape)],
            out_specs=[
                pl.BlockSpec((ROWS, owned), lambda i, *unused: (i, 0)),
                pl.BlockSpec((ROWS, remote), lambda i, *unused: (i, 0)),
                pl.BlockSpec((ROWS, width), lambda i, *unused: (i, 0)),
            ],
            scratch_shapes=[
                pltpu.VMEM((ROWS, owned + remote), F32),
                pltpu.SMEM((num_tiles,), jnp.int32),
                pltpu.SMEM((blocks + 1,), jnp.int32),
                pltpu.SMEM((blocks + 1,), jnp.int32),
            ],
        ),
        out_shape=[
            far_made((owned, owned), BF16),
            far_made((owned, remote), BF16),
            far_made((owned, width), F32),
        ],
        compiler_params=params(48),
        cost_estimate=pl.CostEstimate(
            flops=2 * owned * owned * width, bytes_accessed=40 * 1024 * 1024, transcendentals=0
        ),
        name="build",
    )(tile_rows, tile_cols, tile_vals, x)


def layer_kernel(
    order, far_hbm, own_hbm, cot_hbm, w_hbm, got_ref,
    act_hbm, hid_hbm, slope_hbm, grad_hbm, back_hbm,
    far, own, cot, act, hid, slope, grad, w, near, back, sems, sent, w_sem, back_sems,
):
    blocks = sems.shape[1]
    views = [pl.ds(n * BIG, BIG) for n in range(blocks)]

    def fetch(n):
        pairs = ((far_hbm, far), (own_hbm, own), (cot_hbm, cot))
        copies = [pltpu.make_async_copy(a.at[views[n]], b.at[views[n]], sems.at[k, n]) for k, (a, b) in enumerate(pairs)]
        for copy in copies:
            copy.start()
        return copies

    sending = []

    def send(k, n, a, b, at):
        sending.append(pltpu.make_async_copy(a.at[at], b.at[at], sent.at[k, n]))
        sending[-1].start()

    coming = [fetch(0)]
    weight = pltpu.make_async_copy(w_hbm, w, w_sem)
    weight.start()
    slots = near.shape[0] // len(order)
    for p, s in enumerate(order):
        near[s * slots : (s + 1) * slots, :] = got_ref[p * slots : (p + 1) * slots, :]
    for n, at in enumerate(views):
        copies = coming[n]
        for copy in copies[:2]:
            copy.wait()
        while len(coming) < min(n + 3, blocks):
            coming.append(fetch(len(coming)))
        hid[at, :] = (own[at, :] + dot(far[at, :], near[...])).astype(BF16)
        send(0, n, hid, hid_hbm, at)
        copies[2].wait()
        if n == 0:
            weight.wait()
        preact = dot(hid[at, :], w[...])
        gate = 0.5 + 0.5 * jnp.tanh(0.5 * preact)
        act[at, :] = (preact * gate).astype(BF16)
        send(1, n, act, act_hbm, at)
        slope[at, :] = (cot[at, :].astype(F32) * gate * (1.0 + preact * (1.0 - gate))).astype(BF16)
        send(2, n, slope, slope_hbm, at)
        grad[at, :] = dot(slope[at, :], w[...], ((1,), (1,))).astype(BF16)
        send(3, n, grad, grad_hbm, at)
    place_of = {s: p for p, s in enumerate(order)}
    for n in range(back.shape[0] // BIG):
        at = pl.ds(n * BIG, BIG)
        back[at, :] = dot(far[:, at], grad[...], ((0,), (0,))).astype(BF16)
        for s in range(n * BIG // slots, (n + 1) * BIG // slots):
            rows = back.at[pl.ds(s * slots, slots)]
            sending.append(pltpu.make_async_copy(rows, back_hbm.at[pl.ds(place_of[s] * slots, slots)], back_sems.at[s]))
            sending[-1].start()
    for copy in sending:
        copy.wait()


def layer(keep, order, far, own, got, cotangent, weight):
    owned, width = own.shape
    blocks = owned // BIG
    (got,) = held(keep, got)
    rows = (owned, width)
    return pl.pallas_call(
        functools.partial(layer_kernel, order),
        in_specs=[HBM] * 4 + [VMEM],
        out_specs=[HBM] * 5,
        out_shape=[far_made(rows, BF16)] * 4 + [far_made(got.shape, BF16)],
        scratch_shapes=[pltpu.VMEM(far.shape, BF16), pltpu.VMEM(rows, F32)]
        + [pltpu.VMEM(rows, BF16)] * 5
        + [
            pltpu.VMEM(weight.shape, BF16),
            pltpu.VMEM(got.shape, BF16),
            pltpu.VMEM(got.shape, BF16),
            pltpu.SemaphoreType.DMA((3, blocks)),
            pltpu.SemaphoreType.DMA((4, blocks)),
            pltpu.SemaphoreType.DMA,
            pltpu.SemaphoreType.DMA((len(order),)),
        ],
        compiler_params=params(40 if keep else 60),
        name="layer",
    )(*stored(far, own, cotangent, weight), got)


def partial_kernel(me_ref, hid_hbm, slope_hbm, mine_ref, other_ref, hid, slope, total, sems):
    blocks = sems.shape[1]
    views = [pl.ds(n * BIG, BIG) for n in range(blocks)]
    coming = [
        [pltpu.make_async_copy(a.at[at], b.at[at], sems.at[k, n]) for k, (a, b) in enumerate(((hid_hbm, hid), (slope_hbm, slope)))]
        for n, at in enumerate(views)
    ]
    for copies in coming:
        for copy in copies:
            copy.start()
    for n, at in enumerate(views):
        for copy in coming[n]:
            copy.wait()
        part = dot(hid[at, :], slope[at, :], ((0,), (0,)))
        total[...] = part if n == 0 else total[...] + part
    half = mine_ref.shape[0]
    core = me_ref[0] % 2
    for out_ref, first in ((other_ref, (1 - core) * half), (mine_ref, core * half)):
        out_ref[...] = total[pl.ds(pl.multiple_of(first, half), half), :].astype(out_ref.dtype)


def partial_grad(keep, me, hidden, slope):
    owned, width = hidden.shape
    half = (width // 2, width)
    return pl.pallas_call(
        partial_kernel,
        in_specs=[SMEM, HBM, HBM],
        out_specs=[VMEM, VMEM],
        out_shape=[made(keep, half, F32), made(keep, half, BF16)],
        scratch_shapes=[
            pltpu.VMEM((owned, width), BF16),
            pltpu.VMEM((owned, width), BF16),
            pltpu.VMEM((width, width), F32),
            pltpu.SemaphoreType.DMA((2, owned // BIG)),
        ],
        compiler_params=params(20),
        name="partial_grad",
    )(me, *stored(hidden, slope))


def spread_kernel(adj_ref, grad_ref, out_ref):
    out_ref[...] = dot(adj_ref[...], grad_ref[...], ((0,), (0,)))


def spread(adjacency, grad, part, parts):
    owned, width = grad.shape
    blocks = owned // BIG // parts
    return pl.pallas_call(
        spread_kernel,
        grid=(blocks,),
        in_specs=[pl.BlockSpec((owned, BIG), lambda i: (0, i + part * blocks)), whole(grad.shape)],
        out_specs=pl.BlockSpec((BIG, width), lambda i: (i, 0)),
        out_shape=far_made((owned // parts, width), F32),
        compiler_params=params(60),
        cost_estimate=pl.CostEstimate(
            flops=2 * owned * owned * width, bytes_accessed=16 * 1024 * 1024, transcendentals=0
        ),
        name="spread",
    )(*stored(adjacency, grad))


def return_kernel(index_ref, first_hbm, second_hbm, got_ref, out_hbm, owned, out, sems, sent):
    blocks = sems.shape[0]
    views = [pl.ds(n * BIG, BIG) for n in range(blocks)]
    coming = []
    for n, at in enumerate(views):
        half_hbm = (first_hbm, second_hbm)[2 * n // blocks]
        coming.append(pltpu.make_async_copy(half_hbm.at[views[n % (blocks // 2)]], owned.at[at], sems.at[n]))
    for copy in coming:
        copy.start()

    def pick(n):
        row = lax.broadcasted_iota(jnp.int32, (BIG, index_ref.shape[1]), 0) + n * BIG
        return jnp.where(row == index_ref[...], 1.0, 0.0).astype(BF16)

    sending = []
    for n, at in enumerate(views):
        added = dot(pick(n), got_ref[...])
        coming[n].wait()
        out[at, :] = (owned[at, :] + added).astype(BF16)
        sending.append(pltpu.make_async_copy(out.at[at], out_hbm.at[at], sent.at[n]))
        sending[n].start()
    for copy in sending:
        copy.wait()


def give_back(keep, index, first, second, got):
    rows, width = 2 * first.shape[0], first.shape[1]
    (got,) = held(keep, got)
    return pl.pallas_call(
        return_kernel,
        in_specs=[VMEM, HBM, HBM, VMEM],
        out_specs=HBM,
        out_shape=far_made((rows, width), BF16),
        scratch_shapes=[
            pltpu.VMEM((rows, width), F32),
            pltpu.VMEM((rows, width), BF16),
            pltpu.SemaphoreType.DMA((rows // BIG,)),
            pltpu.SemaphoreType.DMA((rows // BIG,)),
        ],
        compiler_params=params(28 if keep else 60),
        name="give_back",
    )(index, *stored(first, second), got)


def exchange(x, axes):
    return lax.all_to_all(x, axes, split_axis=0, concat_axis=0, tiled=True)


def cut_kernel(me_ref, mine_ref, got_ref, *out_refs):
    height = mine_ref.shape[0] // len(out_refs)
    for k, out_ref in enumerate(out_refs):
        at = pl.ds(pl.multiple_of(((me_ref[0] // 2) ^ k) * height, height), height)
        out_ref[...] = (mine_ref[at, :] + got_ref[at, :].astype(F32)).astype(out_ref.dtype)


def cut(me, mine, got, chips):
    height, width = got.shape[0] // chips, got.shape[1]
    return pl.pallas_call(
        cut_kernel,
        in_specs=[SMEM, VMEM, VMEM],
        out_shape=[jax.ShapeDtypeStruct((height, width), F32 if k == 0 else BF16) for k in range(chips)],
        compiler_params=params(8),
        name="cut",
    )(me, mine, got)


def relay_kernel(after_ref, *refs):
    height = refs[0].shape[0]
    for k, ref in enumerate(refs[:-1]):
        refs[-1][k * height : (k + 1) * height, :] = ref[...]


def relay(after, pieces):
    height, width = pieces[0].shape
    return pl.pallas_call(
        relay_kernel,
        in_specs=[HBM] + [VMEM] * len(pieces),
        out_shape=jax.ShapeDtypeStruct((height * len(pieces), width), BF16),
        compiler_params=params(8),
        name="relay",
    )(*stored(after), *pieces)


def place_kernel(chips, other, me_ref, half_ref, *refs):
    out_hbm, placed, sem = refs[-3:]
    half = half_ref.shape[0]
    height = half // chips
    for k in range(chips):
        at = pl.multiple_of(((me_ref[0] // 2) ^ k) * height, height)
        placed[pl.ds(at, height), :] = half_ref[k * height : (k + 1) * height, :].astype(F32)
    at = pl.multiple_of((me_ref[0] + other) % 2 * half, half)
    copy = pltpu.make_async_copy(placed, out_hbm.at[pl.ds(at, half)], sem)
    copy.start()
    copy.wait()


def place(me, half, chips, into=()):
    return pl.pallas_call(
        functools.partial(place_kernel, chips, len(into)),
        in_specs=[SMEM, VMEM] + [HBM] * len(into),
        out_specs=HBM,
        out_shape=far_made((2 * half.shape[0], half.shape[1]), F32),
        scratch_shapes=[pltpu.VMEM(half.shape, F32), pltpu.SemaphoreType.DMA],
        input_output_aliases={2: 0} if into else {},
        compiler_params=params(8),
        name="place",
    )(me, half, *stored(*into))


def add_kernel(after_ref, *refs):
    parts = [ref[...].astype(F32) for ref in refs[:-1]]
    while len(parts) > 1:
        parts = [parts[k] + parts[k + 1] for k in range(0, len(parts), 2)]
    refs[-1][...] = parts[0].astype(BF16)


def add(after, parts):
    return pl.pallas_call(
        add_kernel,
        in_specs=[HBM] + [VMEM] * len(parts),
        out_shape=jax.ShapeDtypeStruct(parts[0].shape, BF16),
        compiler_params=params(8),
        name="add",
    )(*stored(after), *parts)


def swap(x, axis, size, k):
    return lax.ppermute(x, axis, [(i, i ^ k) for i in range(size)])


def per_device(groups, locals_, features, weight, cotangent, tile_vals, tile_rows, tile_cols, send_rows, counts):
    rows_own, width = features.shape
    lists = send_rows[0]
    peers, slots = lists.shape
    remote = peers * slots
    keep = remote <= rows_own
    me = lax.axis_index("local").astype(jnp.int32).reshape(1)
    order = [g * locals_ + l for l in range(locals_) for g in range(groups)]
    outgoing = collect(order, counts, lists, features)
    arrived = exchange(outgoing.reshape(peers, slots, width), RANKS).reshape(remote, width)
    adjacency, far, own = build(tile_rows, tile_cols, tile_vals, features, remote)
    activated, hidden, slope, grad, back = layer(keep, order, far, own, arrived, cotangent, weight)
    returned = exchange(back.reshape(peers, slots, width), RANKS).reshape(remote, width)
    first = spread(adjacency, grad, 0, 2)
    second = spread(adjacency, grad, 1, 2)
    live = jnp.arange(slots)[None, :] < counts[0][:, None]
    index = jnp.where(live, lists, -1).reshape(groups, locals_, slots).swapaxes(0, 1).reshape(1, remote)
    feature_grad = give_back(keep, index, first, second, returned)
    chips = locals_ // 2
    mine, other = partial_grad(keep, me, hidden, slope)
    pieces = cut(me, mine, swap(other, "local", locals_, 1), chips)
    piece = add(first, [pieces[0]] + [swap(pieces[k], "local", locals_, 2 * k) for k in range(1, chips)])
    step, after = 1, second
    while step < groups:
        piece = add(after, [piece, swap(piece, "group", groups, step)])
        step, after = 2 * step, second
    pieces = [piece] + [swap(piece, "local", locals_, 2 * k) for k in range(1, chips)]
    half = relay(feature_grad, pieces)
    weight_grad = place(me, swap(half, "local", locals_, 1), chips, [place(me, half, chips)])
    return activated, feature_grad, weight_grad


def solution(mesh):
    return jax.shard_map(
        functools.partial(per_device, mesh.shape["group"], mesh.shape["local"]),
        mesh=mesh,
        in_specs=(
            P(AXES, None),
            P(),
            P(AXES, None),
            P(AXES, None, None),
            P(AXES),
            P(AXES),
            P(AXES, None, None),
            P(AXES, None),
        ),
        out_specs=(P(AXES, None), P(AXES, None), P()),
        check_vma=False,
    )
```

```python
import functools

import jax
import jax.numpy as jnp
from jax import lax
from jax.experimental import pallas as pl
from jax.experimental.pallas import tpu as pltpu
from jax.sharding import PartitionSpec as P

AXES = ("group", "local")
RANKS = ("local", "group")
BF16 = jnp.bfloat16
F32 = jnp.float32
ROWS = 256
BIG = 512
MIB = 1024 * 1024


def params(mib):
    return pltpu.CompilerParams(vmem_limit_bytes=mib * MIB)


VMEM = pl.BlockSpec(memory_space=pltpu.VMEM)
SMEM = pl.BlockSpec(memory_space=pltpu.SMEM)
HBM = pl.BlockSpec(memory_space=pltpu.MemorySpace.HBM)


def made(keep, shape, dtype):
    return pltpu.VMEM(shape, dtype) if keep else jax.ShapeDtypeStruct(shape, dtype)


def held(keep, *arrays):
    if not keep:
        return arrays
    return [pltpu.with_memory_space_constraint(x, pltpu.VMEM) for x in arrays]


def stored(*arrays):
    return [pltpu.with_memory_space_constraint(x, pltpu.MemorySpace.HBM) for x in arrays]


def far_made(shape, dtype):
    return pltpu.MemorySpace.HBM(shape, dtype)


def dot(a, b, contract=((1,), (0,))):
    return lax.dot_general(a, b, (contract, ((), ())), preferred_element_type=F32)


def whole(shape):
    return pl.BlockSpec(shape, lambda i, *unused: (0,) * len(shape))


def collect_kernel(order, counts_ref, lists_ref, x_ref, out_ref):
    dests, slots = lists_ref.shape
    step = 2 * BIG // slots
    lane = lax.broadcasted_iota(jnp.int32, (slots, x_ref.shape[0]), 1)
    slot = lax.broadcasted_iota(jnp.int32, (slots, 1), 0)
    turned = lists_ref[...].T
    for first in range(0, dests, step):
        parts = []
        for d in order[first : first + step]:
            named = jnp.where(slot < counts_ref[0, d], turned[:, d : d + 1], -1)
            parts.append(jnp.where(named == lane, 1.0, 0.0).astype(BF16))
        pick = jnp.concatenate(parts, axis=0)
        out_ref[first * slots : (first + step) * slots, :] = dot(pick, x_ref[...]).astype(BF16)


def collect(order, counts, lists, x):
    dests, slots = lists.shape
    return pl.pallas_call(
        functools.partial(collect_kernel, order),
        in_specs=[SMEM, VMEM, VMEM],
        out_shape=jax.ShapeDtypeStruct((dests * slots, x.shape[1]), BF16),
        compiler_params=params(60),
        name="collect",
    )(counts, lists, x)


def build_kernel(rows_ref, cols_ref, tiles_ref, x_ref, adj_ref, far_ref, own_ref, total, order, starts, cursor):
    num_tiles, edge = tiles_ref.shape[0], tiles_ref.shape[1]
    per = ROWS // edge
    blocks = pl.num_programs(0)
    i = pl.program_id(0)

    @pl.when(i == 0)
    def _():
        def clear(b, unused):
            starts[b] = 0
            return unused

        lax.fori_loop(0, blocks + 1, clear, 0)

        def count(t, unused):
            k = rows_ref[t] // per + 1
            starts[k] = starts[k] + 1
            return unused

        lax.fori_loop(0, num_tiles, count, 0, unroll=4)

        def add(b, running):
            running = running + starts[b]
            starts[b] = running
            cursor[b] = running
            return running

        lax.fori_loop(0, blocks + 1, add, 0)

        def place(t, unused):
            k = rows_ref[t] // per
            at = cursor[k]
            cursor[k] = at + 1
            order[at] = t
            return unused

        lax.fori_loop(0, num_tiles, place, 0, unroll=4)

    total[...] = jnp.zeros_like(total)

    def one(j, unused):
        t = order[j]
        r = pl.multiple_of((rows_ref[t] % per) * edge, edge)
        c = pl.multiple_of(cols_ref[t] * edge, edge)
        at = (pl.ds(r, edge), pl.ds(c, edge))
        total[at] = total[at] + tiles_ref[t].astype(F32)
        return unused

    lax.fori_loop(starts[i], starts[i + 1], one, 0)
    owned = x_ref.shape[0]
    adj_ref[...] = total[:, :owned].astype(BF16)
    own_ref[...] = dot(adj_ref[...], x_ref[...])
    far_ref[...] = total[:, owned:].astype(BF16)


def build(tile_rows, tile_cols, tile_vals, x, remote):
    owned, width = x.shape
    num_tiles = tile_vals.shape[0]
    blocks = owned // ROWS
    return pl.pallas_call(
        build_kernel,
        grid_spec=pltpu.PrefetchScalarGridSpec(
            num_scalar_prefetch=2,
            grid=(blocks,),
            in_specs=[whole(tile_vals.shape), whole(x.shape)],
            out_specs=[
                pl.BlockSpec((ROWS, owned), lambda i, *unused: (i, 0)),
                pl.BlockSpec((ROWS, remote), lambda i, *unused: (i, 0)),
                pl.BlockSpec((ROWS, width), lambda i, *unused: (i, 0)),
            ],
            scratch_shapes=[
                pltpu.VMEM((ROWS, owned + remote), F32),
                pltpu.SMEM((num_tiles,), jnp.int32),
                pltpu.SMEM((blocks + 1,), jnp.int32),
                pltpu.SMEM((blocks + 1,), jnp.int32),
            ],
        ),
        out_shape=[
            far_made((owned, owned), BF16),
            far_made((owned, remote), BF16),
            far_made((owned, width), F32),
        ],
        compiler_params=params(48),
        cost_estimate=pl.CostEstimate(
            flops=2 * owned * owned * width, bytes_accessed=40 * 1024 * 1024, transcendentals=0
        ),
        name="build",
    )(tile_rows, tile_cols, tile_vals, x)


def layer_kernel(
    order, far_hbm, own_hbm, cot_hbm, w_hbm, got_ref,
    act_hbm, hid_hbm, slope_hbm, grad_hbm, back_hbm,
    far, own, cot, act, hid, slope, grad, w, near, back, sems, sent, w_sem, back_sems,
):
    blocks = sems.shape[1]
    views = [pl.ds(n * BIG, BIG) for n in range(blocks)]

    def fetch(n):
        pairs = ((far_hbm, far), (own_hbm, own), (cot_hbm, cot))
        copies = [pltpu.make_async_copy(a.at[views[n]], b.at[views[n]], sems.at[k, n]) for k, (a, b) in enumerate(pairs)]
        for copy in copies:
            copy.start()
        return copies

    sending = []

    def send(k, n, a, b, at):
        sending.append(pltpu.make_async_copy(a.at[at], b.at[at], sent.at[k, n]))
        sending[-1].start()

    coming = [fetch(0)]
    weight = pltpu.make_async_copy(w_hbm, w, w_sem)
    weight.start()
    slots = near.shape[0] // len(order)
    for p, s in enumerate(order):
        near[s * slots : (s + 1) * slots, :] = got_ref[p * slots : (p + 1) * slots, :]
    for n, at in enumerate(views):
        copies = coming[n]
        for copy in copies[:2]:
            copy.wait()
        while len(coming) < min(n + 3, blocks):
            coming.append(fetch(len(coming)))
        hid[at, :] = (own[at, :] + dot(far[at, :], near[...])).astype(BF16)
        send(0, n, hid, hid_hbm, at)
        copies[2].wait()
        if n == 0:
            weight.wait()
        preact = dot(hid[at, :], w[...])
        gate = 0.5 + 0.5 * jnp.tanh(0.5 * preact)
        act[at, :] = (preact * gate).astype(BF16)
        send(1, n, act, act_hbm, at)
        slope[at, :] = (cot[at, :].astype(F32) * gate * (1.0 + preact * (1.0 - gate))).astype(BF16)
        send(2, n, slope, slope_hbm, at)
        grad[at, :] = dot(slope[at, :], w[...], ((1,), (1,))).astype(BF16)
        send(3, n, grad, grad_hbm, at)
    place_of = {s: p for p, s in enumerate(order)}
    for n in range(back.shape[0] // BIG):
        at = pl.ds(n * BIG, BIG)
        back[at, :] = dot(far[:, at], grad[...], ((0,), (0,))).astype(BF16)
        for s in range(n * BIG // slots, (n + 1) * BIG // slots):
            rows = back.at[pl.ds(s * slots, slots)]
            sending.append(pltpu.make_async_copy(rows, back_hbm.at[pl.ds(place_of[s] * slots, slots)], back_sems.at[s]))
            sending[-1].start()
    for copy in sending:
        copy.wait()


def layer(keep, order, far, own, got, cotangent, weight):
    owned, width = own.shape
    blocks = owned // BIG
    (got,) = held(keep, got)
    rows = (owned, width)
    return pl.pallas_call(
        functools.partial(layer_kernel, order),
        in_specs=[HBM] * 4 + [VMEM],
        out_specs=[HBM] * 5,
        out_shape=[far_made(rows, BF16)] * 4 + [far_made(got.shape, BF16)],
        scratch_shapes=[pltpu.VMEM(far.shape, BF16), pltpu.VMEM(rows, F32)]
        + [pltpu.VMEM(rows, BF16)] * 5
        + [
            pltpu.VMEM(weight.shape, BF16),
            pltpu.VMEM(got.shape, BF16),
            pltpu.VMEM(got.shape, BF16),
            pltpu.SemaphoreType.DMA((3, blocks)),
            pltpu.SemaphoreType.DMA((4, blocks)),
            pltpu.SemaphoreType.DMA,
            pltpu.SemaphoreType.DMA((len(order),)),
        ],
        compiler_params=params(40 if keep else 60),
        name="layer",
    )(*stored(far, own, cotangent, weight), got)


def partial_kernel(me_ref, hid_hbm, slope_hbm, mine_ref, other_ref, hid, slope, total, sems):
    blocks = sems.shape[1]
    views = [pl.ds(n * BIG, BIG) for n in range(blocks)]
    coming = [
        [pltpu.make_async_copy(a.at[at], b.at[at], sems.at[k, n]) for k, (a, b) in enumerate(((hid_hbm, hid), (slope_hbm, slope)))]
        for n, at in enumerate(views)
    ]
    for copies in coming:
        for copy in copies:
            copy.start()
    for n, at in enumerate(views):
        for copy in coming[n]:
            copy.wait()
        part = dot(hid[at, :], slope[at, :], ((0,), (0,)))
        total[...] = part if n == 0 else total[...] + part
    half = mine_ref.shape[0]
    core = me_ref[0] % 2
    for out_ref, first in ((other_ref, (1 - core) * half), (mine_ref, core * half)):
        out_ref[...] = total[pl.ds(pl.multiple_of(first, half), half), :].astype(out_ref.dtype)


def partial_grad(keep, me, hidden, slope):
    owned, width = hidden.shape
    half = (width // 2, width)
    return pl.pallas_call(
        partial_kernel,
        in_specs=[SMEM, HBM, HBM],
        out_specs=[VMEM, VMEM],
        out_shape=[made(keep, half, F32), made(keep, half, BF16)],
        scratch_shapes=[
            pltpu.VMEM((owned, width), BF16),
            pltpu.VMEM((owned, width), BF16),
            pltpu.VMEM((width, width), F32),
            pltpu.SemaphoreType.DMA((2, owned // BIG)),
        ],
        compiler_params=params(20),
        name="partial_grad",
    )(me, *stored(hidden, slope))


def spread_kernel(adj_ref, grad_ref, out_ref):
    out_ref[...] = dot(adj_ref[...], grad_ref[...], ((0,), (0,)))


def spread(adjacency, grad, part, parts):
    owned, width = grad.shape
    blocks = owned // BIG // parts
    return pl.pallas_call(
        spread_kernel,
        grid=(blocks,),
        in_specs=[pl.BlockSpec((owned, BIG), lambda i: (0, i + part * blocks)), whole(grad.shape)],
        out_specs=pl.BlockSpec((BIG, width), lambda i: (i, 0)),
        out_shape=far_made((owned // parts, width), F32),
        compiler_params=params(60),
        cost_estimate=pl.CostEstimate(
            flops=2 * owned * owned * width, bytes_accessed=16 * 1024 * 1024, transcendentals=0
        ),
        name="spread",
    )(*stored(adjacency, grad))


def return_kernel(index_ref, first_hbm, second_hbm, got_ref, out_hbm, owned, out, sems, sent):
    blocks = sems.shape[0]
    views = [pl.ds(n * BIG, BIG) for n in range(blocks)]
    coming = []
    for n, at in enumerate(views):
        half_hbm = (first_hbm, second_hbm)[2 * n // blocks]
        coming.append(pltpu.make_async_copy(half_hbm.at[views[n % (blocks // 2)]], owned.at[at], sems.at[n]))
    for copy in coming:
        copy.start()

    def pick(n):
        row = lax.broadcasted_iota(jnp.int32, (BIG, index_ref.shape[1]), 0) + n * BIG
        return jnp.where(row == index_ref[...], 1.0, 0.0).astype(BF16)

    sending = []
    for n, at in enumerate(views):
        added = dot(pick(n), got_ref[...])
        coming[n].wait()
        out[at, :] = (owned[at, :] + added).astype(BF16)
        sending.append(pltpu.make_async_copy(out.at[at], out_hbm.at[at], sent.at[n]))
        sending[n].start()
    for copy in sending:
        copy.wait()


def give_back(keep, index, first, second, got):
    rows, width = 2 * first.shape[0], first.shape[1]
    (got,) = held(keep, got)
    return pl.pallas_call(
        return_kernel,
        in_specs=[VMEM, HBM, HBM, VMEM],
        out_specs=HBM,
        out_shape=far_made((rows, width), BF16),
        scratch_shapes=[
            pltpu.VMEM((rows, width), F32),
            pltpu.VMEM((rows, width), BF16),
            pltpu.SemaphoreType.DMA((rows // BIG,)),
            pltpu.SemaphoreType.DMA((rows // BIG,)),
        ],
        compiler_params=params(28 if keep else 60),
        name="give_back",
    )(index, *stored(first, second), got)


def exchange(x, axes):
    return lax.all_to_all(x, axes, split_axis=0, concat_axis=0, tiled=True)


def cut_kernel(me_ref, mine_ref, got_ref, *out_refs):
    height = mine_ref.shape[0] // len(out_refs)
    for k, out_ref in enumerate(out_refs):
        at = pl.ds(pl.multiple_of(((me_ref[0] // 2) ^ k) * height, height), height)
        out_ref[...] = (mine_ref[at, :] + got_ref[at, :].astype(F32)).astype(out_ref.dtype)


def cut(me, mine, got, chips):
    height, width = got.shape[0] // chips, got.shape[1]
    return pl.pallas_call(
        cut_kernel,
        in_specs=[SMEM, VMEM, VMEM],
        out_shape=[jax.ShapeDtypeStruct((height, width), F32 if k == 0 else BF16) for k in range(chips)],
        compiler_params=params(8),
        name="cut",
    )(me, mine, got)


def relay_kernel(after_ref, *refs):
    height = refs[0].shape[0]
    for k, ref in enumerate(refs[:-1]):
        refs[-1][k * height : (k + 1) * height, :] = ref[...]


def relay(after, pieces):
    height, width = pieces[0].shape
    return pl.pallas_call(
        relay_kernel,
        in_specs=[HBM] + [VMEM] * len(pieces),
        out_shape=jax.ShapeDtypeStruct((height * len(pieces), width), BF16),
        compiler_params=params(8),
        name="relay",
    )(*stored(after), *pieces)


def place_kernel(chips, other, me_ref, half_ref, *refs):
    out_hbm, placed, sem = refs[-3:]
    half = half_ref.shape[0]
    height = half // chips
    for k in range(chips):
        at = pl.multiple_of(((me_ref[0] // 2) ^ k) * height, height)
        placed[pl.ds(at, height), :] = half_ref[k * height : (k + 1) * height, :].astype(F32)
    at = pl.multiple_of((me_ref[0] + other) % 2 * half, half)
    copy = pltpu.make_async_copy(placed, out_hbm.at[pl.ds(at, half)], sem)
    copy.start()
    copy.wait()


def place(me, half, chips, into=()):
    return pl.pallas_call(
        functools.partial(place_kernel, chips, len(into)),
        in_specs=[SMEM, VMEM] + [HBM] * len(into),
        out_specs=HBM,
        out_shape=far_made((2 * half.shape[0], half.shape[1]), F32),
        scratch_shapes=[pltpu.VMEM(half.shape, F32), pltpu.SemaphoreType.DMA],
        input_output_aliases={2: 0} if into else {},
        compiler_params=params(8),
        name="place",
    )(me, half, *stored(*into))


def add_kernel(after_ref, *refs):
    parts = [ref[...].astype(F32) for ref in refs[:-1]]
    while len(parts) > 1:
        parts = [parts[k] + parts[k + 1] for k in range(0, len(parts), 2)]
    refs[-1][...] = parts[0].astype(BF16)


def add(after, parts):
    return pl.pallas_call(
        add_kernel,
        in_specs=[HBM] + [VMEM] * len(parts),
        out_shape=jax.ShapeDtypeStruct(parts[0].shape, BF16),
        compiler_params=params(8),
        name="add",
    )(*stored(after), *parts)


def swap(x, axis, size, k):
    return lax.ppermute(x, axis, [(i, i ^ k) for i in range(size)])


def per_device(groups, locals_, features, weight, cotangent, tile_vals, tile_rows, tile_cols, send_rows, counts):
    rows_own, width = features.shape
    lists = send_rows[0]
    peers, slots = lists.shape
    remote = peers * slots
    keep = remote <= rows_own
    me = lax.axis_index("local").astype(jnp.int32).reshape(1)
    order = [g * locals_ + l for l in range(locals_) for g in range(groups)]
    outgoing = collect(order, counts, lists, features)
    arrived = exchange(outgoing.reshape(peers, slots, width), RANKS).reshape(remote, width)
    adjacency, far, own = build(tile_rows, tile_cols, tile_vals, features, remote)
    activated, hidden, slope, grad, back = layer(keep, order, far, own, arrived, cotangent, weight)
    returned = exchange(back.reshape(peers, slots, width), RANKS).reshape(remote, width)
    first = spread(adjacency, grad, 0, 2)
    second = spread(adjacency, grad, 1, 2)
    live = jnp.arange(slots)[None, :] < counts[0][:, None]
    index = jnp.where(live, lists, -1).reshape(groups, locals_, slots).swapaxes(0, 1).reshape(1, remote)
    feature_grad = give_back(keep, index, first, second, returned)
    chips = locals_ // 2
    mine, other = partial_grad(keep, me, hidden, slope)
    pieces = cut(me, mine, swap(other, "local", locals_, 1), chips)
    piece = add(first, [pieces[0]] + [swap(pieces[k], "local", locals_, 2 * k) for k in range(1, chips)])
    step, after = 1, second
    while step < groups:
        piece = add(after, [piece, swap(piece, "group", groups, step)])
        step, after = 2 * step, second
    pieces = [piece] + [swap(piece, "local", locals_, 2 * k) for k in range(1, chips)]
    half = relay(feature_grad, pieces)
    weight_grad = place(me, swap(half, "local", locals_, 1), chips, [place(me, half, chips)])
    return activated, feature_grad, weight_grad


def solution(mesh):
    return jax.shard_map(
        functools.partial(per_device, mesh.shape["group"], mesh.shape["local"]),
        mesh=mesh,
        in_specs=(
            P(AXES, None),
            P(),
            P(AXES, None),
            P(AXES, None, None),
            P(AXES),
            P(AXES),
            P(AXES, None, None),
            P(AXES, None),
        ),
        out_specs=(P(AXES, None), P(AXES, None), P()),
        check_vma=False,
    )
```

```python
import functools

import jax
import jax.numpy as jnp
from jax import lax
from jax.experimental import pallas as pl
from jax.experimental.pallas import tpu as pltpu
from jax.sharding import PartitionSpec as P

AXES = ("group", "local")
RANKS = ("local", "group")
BF16 = jnp.bfloat16
F32 = jnp.float32
ROWS = 256
BIG = 512
MIB = 1024 * 1024


def params(mib):
    return pltpu.CompilerParams(vmem_limit_bytes=mib * MIB)


VMEM = pl.BlockSpec(memory_space=pltpu.VMEM)
SMEM = pl.BlockSpec(memory_space=pltpu.SMEM)
HBM = pl.BlockSpec(memory_space=pltpu.MemorySpace.HBM)


def made(keep, shape, dtype):
    return pltpu.VMEM(shape, dtype) if keep else jax.ShapeDtypeStruct(shape, dtype)


def held(keep, *arrays):
    if not keep:
        return arrays
    return [pltpu.with_memory_space_constraint(x, pltpu.VMEM) for x in arrays]


def stored(*arrays):
    return [pltpu.with_memory_space_constraint(x, pltpu.MemorySpace.HBM) for x in arrays]


def far_made(shape, dtype):
    return pltpu.MemorySpace.HBM(shape, dtype)


def dot(a, b, contract=((1,), (0,))):
    return lax.dot_general(a, b, (contract, ((), ())), preferred_element_type=F32)


def whole(shape):
    return pl.BlockSpec(shape, lambda i, *unused: (0,) * len(shape))


def collect_kernel(order, counts_ref, lists_ref, x_ref, out_ref):
    dests, slots = lists_ref.shape
    step = BIG // slots
    lane = lax.broadcasted_iota(jnp.int32, (slots, x_ref.shape[0]), 1)
    slot = lax.broadcasted_iota(jnp.int32, (slots, 1), 0)
    turned = lists_ref[...].T
    for first in range(0, dests, step):
        parts = []
        for d in order[first : first + step]:
            named = jnp.where(slot < counts_ref[0, d], turned[:, d : d + 1], -1)
            parts.append(jnp.where(named == lane, 1.0, 0.0).astype(BF16))
        pick = jnp.concatenate(parts, axis=0)
        out_ref[first * slots : (first + step) * slots, :] = dot(pick, x_ref[...]).astype(BF16)


def collect(order, counts, lists, x):
    dests, slots = lists.shape
    return pl.pallas_call(
        functools.partial(collect_kernel, order),
        in_specs=[SMEM, VMEM, VMEM],
        out_shape=jax.ShapeDtypeStruct((dests * slots, x.shape[1]), BF16),
        compiler_params=params(60),
        name="collect",
    )(counts, lists, x)


def build_kernel(rows_ref, cols_ref, tiles_ref, x_ref, adj_ref, far_ref, own_ref, total, order, starts, cursor):
    num_tiles, edge = tiles_ref.shape[0], tiles_ref.shape[1]
    per = ROWS // edge
    blocks = pl.num_programs(0)
    i = pl.program_id(0)

    @pl.when(i == 0)
    def _():
        def clear(b, unused):
            starts[b] = 0
            return unused

        lax.fori_loop(0, blocks + 1, clear, 0)

        def count(t, unused):
            k = rows_ref[t] // per + 1
            starts[k] = starts[k] + 1
            return unused

        lax.fori_loop(0, num_tiles, count, 0, unroll=4)

        def add(b, running):
            running = running + starts[b]
            starts[b] = running
            cursor[b] = running
            return running

        lax.fori_loop(0, blocks + 1, add, 0)

        def place(t, unused):
            k = rows_ref[t] // per
            at = cursor[k]
            cursor[k] = at + 1
            order[at] = t
            return unused

        lax.fori_loop(0, num_tiles, place, 0, unroll=4)

    total[...] = jnp.zeros_like(total)

    def one(j, unused):
        t = order[j]
        r = pl.multiple_of((rows_ref[t] % per) * edge, edge)
        c = pl.multiple_of(cols_ref[t] * edge, edge)
        at = (pl.ds(r, edge), pl.ds(c, edge))
        total[at] = total[at] + tiles_ref[t].astype(F32)
        return unused

    lax.fori_loop(starts[i], starts[i + 1], one, 0)
    owned = x_ref.shape[0]
    adj_ref[...] = total[:, :owned].astype(BF16)
    own_ref[...] = dot(adj_ref[...], x_ref[...])
    far_ref[...] = total[:, owned:].astype(BF16)


def build(tile_rows, tile_cols, tile_vals, x, remote):
    owned, width = x.shape
    num_tiles = tile_vals.shape[0]
    blocks = owned // ROWS
    return pl.pallas_call(
        build_kernel,
        grid_spec=pltpu.PrefetchScalarGridSpec(
            num_scalar_prefetch=2,
            grid=(blocks,),
            in_specs=[whole(tile_vals.shape), whole(x.shape)],
            out_specs=[
                pl.BlockSpec((ROWS, owned), lambda i, *unused: (i, 0)),
                pl.BlockSpec((ROWS, remote), lambda i, *unused: (i, 0)),
                pl.BlockSpec((ROWS, width), lambda i, *unused: (i, 0)),
            ],
            scratch_shapes=[
                pltpu.VMEM((ROWS, owned + remote), F32),
                pltpu.SMEM((num_tiles,), jnp.int32),
                pltpu.SMEM((blocks + 1,), jnp.int32),
                pltpu.SMEM((blocks + 1,), jnp.int32),
            ],
        ),
        out_shape=[
            far_made((owned, owned), BF16),
            far_made((owned, remote), BF16),
            far_made((owned, width), F32),
        ],
        compiler_params=params(48),
        cost_estimate=pl.CostEstimate(
            flops=2 * owned * owned * width, bytes_accessed=40 * 1024 * 1024, transcendentals=0
        ),
        name="build",
    )(tile_rows, tile_cols, tile_vals, x)


def layer_kernel(
    order, far_hbm, own_hbm, cot_hbm, w_hbm, got_ref,
    act_hbm, hid_hbm, slope_hbm, grad_hbm, back_hbm,
    far, own, cot, act, hid, slope, grad, w, near, back, sems, sent, w_sem, back_sems,
):
    blocks = sems.shape[1]
    views = [pl.ds(n * BIG, BIG) for n in range(blocks)]

    def fetch(n):
        pairs = ((far_hbm, far), (own_hbm, own), (cot_hbm, cot))
        copies = [pltpu.make_async_copy(a.at[views[n]], b.at[views[n]], sems.at[k, n]) for k, (a, b) in enumerate(pairs)]
        for copy in copies:
            copy.start()
        return copies

    sending = []

    def send(k, n, a, b, at):
        sending.append(pltpu.make_async_copy(a.at[at], b.at[at], sent.at[k, n]))
        sending[-1].start()

    coming = [fetch(0)]
    weight = pltpu.make_async_copy(w_hbm, w, w_sem)
    weight.start()
    slots = near.shape[0] // len(order)
    for p, s in enumerate(order):
        near[s * slots : (s + 1) * slots, :] = got_ref[p * slots : (p + 1) * slots, :]
    for n, at in enumerate(views):
        copies = coming[n]
        for copy in copies[:2]:
            copy.wait()
        while len(coming) < min(n + 3, blocks):
            coming.append(fetch(len(coming)))
        hid[at, :] = (own[at, :] + dot(far[at, :], near[...])).astype(BF16)
        send(0, n, hid, hid_hbm, at)
        copies[2].wait()
        if n == 0:
            weight.wait()
        preact = dot(hid[at, :], w[...])
        gate = 0.5 + 0.5 * jnp.tanh(0.5 * preact)
        act[at, :] = (preact * gate).astype(BF16)
        send(1, n, act, act_hbm, at)
        slope[at, :] = (cot[at, :].astype(F32) * gate * (1.0 + preact * (1.0 - gate))).astype(BF16)
        send(2, n, slope, slope_hbm, at)
        grad[at, :] = dot(slope[at, :], w[...], ((1,), (1,))).astype(BF16)
        send(3, n, grad, grad_hbm, at)
    place_of = {s: p for p, s in enumerate(order)}
    for n in range(back.shape[0] // BIG):
        at = pl.ds(n * BIG, BIG)
        back[at, :] = dot(far[:, at], grad[...], ((0,), (0,))).astype(BF16)
        for s in range(n * BIG // slots, (n + 1) * BIG // slots):
            rows = back.at[pl.ds(s * slots, slots)]
            sending.append(pltpu.make_async_copy(rows, back_hbm.at[pl.ds(place_of[s] * slots, slots)], back_sems.at[s]))
            sending[-1].start()
    for copy in sending:
        copy.wait()


def layer(keep, order, far, own, got, cotangent, weight):
    owned, width = own.shape
    blocks = owned // BIG
    (got,) = held(keep, got)
    rows = (owned, width)
    return pl.pallas_call(
        functools.partial(layer_kernel, order),
        in_specs=[HBM] * 4 + [VMEM],
        out_specs=[HBM] * 5,
        out_shape=[far_made(rows, BF16)] * 4 + [far_made(got.shape, BF16)],
        scratch_shapes=[pltpu.VMEM(far.shape, BF16), pltpu.VMEM(rows, F32)]
        + [pltpu.VMEM(rows, BF16)] * 5
        + [
            pltpu.VMEM(weight.shape, BF16),
            pltpu.VMEM(got.shape, BF16),
            pltpu.VMEM(got.shape, BF16),
            pltpu.SemaphoreType.DMA((3, blocks)),
            pltpu.SemaphoreType.DMA((4, blocks)),
            pltpu.SemaphoreType.DMA,
            pltpu.SemaphoreType.DMA((len(order),)),
        ],
        compiler_params=params(40 if keep else 60),
        name="layer",
    )(*stored(far, own, cotangent, weight), got)


def partial_kernel(me_ref, hid_hbm, slope_hbm, mine_ref, other_ref, hid, slope, total, sems):
    blocks = sems.shape[1]
    views = [pl.ds(n * BIG, BIG) for n in range(blocks)]
    coming = [
        [pltpu.make_async_copy(a.at[at], b.at[at], sems.at[k, n]) for k, (a, b) in enumerate(((hid_hbm, hid), (slope_hbm, slope)))]
        for n, at in enumerate(views)
    ]
    for copies in coming:
        for copy in copies:
            copy.start()
    for n, at in enumerate(views):
        for copy in coming[n]:
            copy.wait()
        part = dot(hid[at, :], slope[at, :], ((0,), (0,)))
        total[...] = part if n == 0 else total[...] + part
    half = mine_ref.shape[0]
    core = me_ref[0] % 2
    for out_ref, first in ((other_ref, (1 - core) * half), (mine_ref, core * half)):
        out_ref[...] = total[pl.ds(pl.multiple_of(first, half), half), :].astype(out_ref.dtype)


def partial_grad(keep, me, hidden, slope):
    owned, width = hidden.shape
    half = (width // 2, width)
    return pl.pallas_call(
        partial_kernel,
        in_specs=[SMEM, HBM, HBM],
        out_specs=[VMEM, VMEM],
        out_shape=[made(keep, half, F32), made(keep, half, BF16)],
        scratch_shapes=[
            pltpu.VMEM((owned, width), BF16),
            pltpu.VMEM((owned, width), BF16),
            pltpu.VMEM((width, width), F32),
            pltpu.SemaphoreType.DMA((2, owned // BIG)),
        ],
        compiler_params=params(20),
        name="partial_grad",
    )(me, *stored(hidden, slope))


def spread_kernel(adj_ref, grad_ref, out_ref):
    out_ref[...] = dot(adj_ref[...], grad_ref[...], ((0,), (0,)))


def spread(adjacency, grad, part, parts):
    owned, width = grad.shape
    blocks = owned // BIG // parts
    return pl.pallas_call(
        spread_kernel,
        grid=(blocks,),
        in_specs=[pl.BlockSpec((owned, BIG), lambda i: (0, i + part * blocks)), whole(grad.shape)],
        out_specs=pl.BlockSpec((BIG, width), lambda i: (i, 0)),
        out_shape=far_made((owned // parts, width), F32),
        compiler_params=params(60),
        cost_estimate=pl.CostEstimate(
            flops=2 * owned * owned * width, bytes_accessed=16 * 1024 * 1024, transcendentals=0
        ),
        name="spread",
    )(*stored(adjacency, grad))


def return_kernel(index_ref, first_hbm, second_hbm, got_ref, out_hbm, owned, out, sems, sent):
    blocks = sems.shape[0]
    views = [pl.ds(n * BIG, BIG) for n in range(blocks)]
    coming = []
    for n, at in enumerate(views):
        half_hbm = (first_hbm, second_hbm)[2 * n // blocks]
        coming.append(pltpu.make_async_copy(half_hbm.at[views[n % (blocks // 2)]], owned.at[at], sems.at[n]))
    for copy in coming:
        copy.start()

    def pick(n):
        row = lax.broadcasted_iota(jnp.int32, (BIG, index_ref.shape[1]), 0) + n * BIG
        return jnp.where(row == index_ref[...], 1.0, 0.0).astype(BF16)

    sending = []
    for n, at in enumerate(views):
        added = dot(pick(n), got_ref[...])
        coming[n].wait()
        out[at, :] = (owned[at, :] + added).astype(BF16)
        sending.append(pltpu.make_async_copy(out.at[at], out_hbm.at[at], sent.at[n]))
        sending[n].start()
    for copy in sending:
        copy.wait()


def give_back(keep, index, first, second, got):
    rows, width = 2 * first.shape[0], first.shape[1]
    (got,) = held(keep, got)
    return pl.pallas_call(
        return_kernel,
        in_specs=[VMEM, HBM, HBM, VMEM],
        out_specs=HBM,
        out_shape=far_made((rows, width), BF16),
        scratch_shapes=[
            pltpu.VMEM((rows, width), F32),
            pltpu.VMEM((rows, width), BF16),
            pltpu.SemaphoreType.DMA((rows // BIG,)),
            pltpu.SemaphoreType.DMA((rows // BIG,)),
        ],
        compiler_params=params(28 if keep else 60),
        name="give_back",
    )(index, *stored(first, second), got)


def exchange(x, axes):
    return lax.all_to_all(x, axes, split_axis=0, concat_axis=0, tiled=True)


def cut_kernel(me_ref, mine_ref, got_ref, *out_refs):
    height = mine_ref.shape[0] // len(out_refs)
    for k, out_ref in enumerate(out_refs):
        at = pl.ds(pl.multiple_of(((me_ref[0] // 2) ^ k) * height, height), height)
        out_ref[...] = (mine_ref[at, :] + got_ref[at, :].astype(F32)).astype(out_ref.dtype)


def cut(me, mine, got, chips):
    height, width = got.shape[0] // chips, got.shape[1]
    return pl.pallas_call(
        cut_kernel,
        in_specs=[SMEM, VMEM, VMEM],
        out_shape=[jax.ShapeDtypeStruct((height, width), F32 if k == 0 else BF16) for k in range(chips)],
        compiler_params=params(8),
        name="cut",
    )(me, mine, got)


def relay_kernel(after_ref, *refs):
    height = refs[0].shape[0]
    for k, ref in enumerate(refs[:-1]):
        refs[-1][k * height : (k + 1) * height, :] = ref[...]


def relay(after, pieces):
    height, width = pieces[0].shape
    return pl.pallas_call(
        relay_kernel,
        in_specs=[HBM] + [VMEM] * len(pieces),
        out_shape=jax.ShapeDtypeStruct((height * len(pieces), width), BF16),
        compiler_params=params(8),
        name="relay",
    )(*stored(after), *pieces)


def place_kernel(chips, other, me_ref, half_ref, *refs):
    out_hbm, placed, sem = refs[-3:]
    half = half_ref.shape[0]
    height = half // chips
    for k in range(chips):
        at = pl.multiple_of(((me_ref[0] // 2) ^ k) * height, height)
        placed[pl.ds(at, height), :] = half_ref[k * height : (k + 1) * height, :].astype(F32)
    at = pl.multiple_of((me_ref[0] + other) % 2 * half, half)
    copy = pltpu.make_async_copy(placed, out_hbm.at[pl.ds(at, half)], sem)
    copy.start()
    copy.wait()


def place(me, half, chips, into=()):
    return pl.pallas_call(
        functools.partial(place_kernel, chips, len(into)),
        in_specs=[SMEM, VMEM] + [HBM] * len(into),
        out_specs=HBM,
        out_shape=far_made((2 * half.shape[0], half.shape[1]), F32),
        scratch_shapes=[pltpu.VMEM(half.shape, F32), pltpu.SemaphoreType.DMA],
        input_output_aliases={2: 0} if into else {},
        compiler_params=params(8),
        name="place",
    )(me, half, *stored(*into))


def add_kernel(after_ref, *refs):
    parts = [ref[...].astype(F32) for ref in refs[:-1]]
    while len(parts) > 1:
        parts = [parts[k] + parts[k + 1] for k in range(0, len(parts), 2)]
    refs[-1][...] = parts[0].astype(BF16)


def add(after, parts):
    return pl.pallas_call(
        add_kernel,
        in_specs=[HBM] + [VMEM] * len(parts),
        out_shape=jax.ShapeDtypeStruct(parts[0].shape, BF16),
        compiler_params=params(8),
        name="add",
    )(*stored(after), *parts)


def swap(x, axis, size, k):
    return lax.ppermute(x, axis, [(i, i ^ k) for i in range(size)])


def per_device(groups, locals_, features, weight, cotangent, tile_vals, tile_rows, tile_cols, send_rows, counts):
    rows_own, width = features.shape
    lists = send_rows[0]
    peers, slots = lists.shape
    remote = peers * slots
    keep = remote <= rows_own
    me = lax.axis_index("local").astype(jnp.int32).reshape(1)
    order = [g * locals_ + l for l in range(locals_) for g in range(groups)]
    outgoing = collect(order, counts, lists, features)
    arrived = exchange(outgoing.reshape(peers, slots, width), RANKS).reshape(remote, width)
    adjacency, far, own = build(tile_rows, tile_cols, tile_vals, features, remote)
    activated, hidden, slope, grad, back = layer(keep, order, far, own, arrived, cotangent, weight)
    returned = exchange(back.reshape(peers, slots, width), RANKS).reshape(remote, width)
    first = spread(adjacency, grad, 0, 2)
    second = spread(adjacency, grad, 1, 2)
    live = jnp.arange(slots)[None, :] < counts[0][:, None]
    index = jnp.where(live, lists, -1).reshape(groups, locals_, slots).swapaxes(0, 1).reshape(1, remote)
    feature_grad = give_back(keep, index, first, second, returned)
    chips = locals_ // 2
    mine, other = partial_grad(keep, me, hidden, slope)
    pieces = cut(me, mine, swap(other, "local", locals_, 1), chips)
    piece = add(first, [pieces[0]] + [swap(pieces[k], "local", locals_, 2 * k) for k in range(1, chips)])
    piece = add(second, [piece] + [swap(piece, "group", groups, k) for k in range(1, groups)])
    pieces = [piece] + [swap(piece, "local", locals_, 2 * k) for k in range(1, chips)]
    half = relay(feature_grad, pieces)
    weight_grad = place(me, swap(half, "local", locals_, 1), chips, [place(me, half, chips)])
    return activated, feature_grad, weight_grad


def solution(mesh):
    return jax.shard_map(
        functools.partial(per_device, mesh.shape["group"], mesh.shape["local"]),
        mesh=mesh,
        in_specs=(
            P(AXES, None),
            P(),
            P(AXES, None),
            P(AXES, None, None),
            P(AXES),
            P(AXES),
            P(AXES, None, None),
            P(AXES, None),
        ),
        out_specs=(P(AXES, None), P(AXES, None), P()),
        check_vma=False,
    )
```
